32 devices in a mesh: dp: 4 (over y, x), seq: 8 (over z, core).
Axes of the slice: x: 2, y: 2, z: 4, core: 2. Of those that a mesh axis runs over, the one named last changes fastest.
Arguments:
- tokens: bfloat16 [8, 1024, 2048], P('dp', 'seq'), may hold values from -6 to 6
- segment_ids: int32 [8, 1024], P('dp', 'seq'), may hold values from 0 to 4, as said below
- cotangent: bfloat16 [8, 1024, 2048], P('dp', 'seq'), may hold values from -6 to 6
- norm_one: bfloat16 [2048], P(('dp', 'seq')), may hold values from 0.5 to 1.5
- branch_weight: bfloat16 [2048, 2560], P(('dp', 'seq')), may hold values from -0.125 to 0.125
- input_proj: bfloat16 [2048, 2560], P(('dp', 'seq')), may hold values from -0.125 to 0.125
- conv_weight: bfloat16 [4, 2560], P(None, ('dp', 'seq')), may hold values from -3 to 3
- conv_bias: bfloat16 [2560], P(('dp', 'seq')), may hold values from -3 to 3
- rate_weight: bfloat16 [2560, 160], P(('dp', 'seq')), may hold values from -0.5 to 0.5
- igate_weight: bfloat16 [2560, 160], P(('dp', 'seq')), may hold values from -0.5 to 0.5
- rate_bias: bfloat16 [2560], P(('dp', 'seq')), may hold values from -4 to 4
- igate_bias: bfloat16 [2560], P(('dp', 'seq')), may hold values from -4 to 4
- decay_param: bfloat16 [2560], P(('dp', 'seq')), may hold values from 4.5 to 10.5
- out_proj: bfloat16 [2560, 2048], P(('dp', 'seq')), may hold values from -0.5 to 0.5
- norm_two: bfloat16 [2048], P(('dp', 'seq')), may hold values from 0.5 to 1.5
- mlp_gate: bfloat16 [2048, 6144], P(('dp', 'seq')), may hold values from -0.125 to 0.125
- mlp_up: bfloat16 [2048, 6144], P(('dp', 'seq')), may hold values from -0.125 to 0.125
- mlp_down: bfloat16 [6144, 2048], P(('dp', 'seq')), may hold values from -0.15625 to 0.15625
Outputs:
- block_out: bfloat16 [8, 1024, 2048], P('dp', 'seq')
- grad_tokens: float32 [8, 1024, 2048], P('dp', 'seq')
- grad_norm_one: float32 [2048], P(('dp', 'seq'))
- grad_branch_weight: float32 [2048, 2560], P(('dp', 'seq'))
- grad_input_proj: float32 [2048, 2560], P(('dp', 'seq'))
- grad_conv_weight: float32 [4, 2560], P(None, ('dp', 'seq'))
- grad_conv_bias: float32 [2560], P(('dp', 'seq'))
- grad_rate_weight: float32 [2560, 160], P(('dp', 'seq'))
- grad_igate_weight: float32 [2560, 160], P(('dp', 'seq'))
- grad_rate_bias: float32 [2560], P(('dp', 'seq'))
- grad_igate_bias: float32 [2560], P(('dp', 'seq'))
- grad_decay_param: float32 [2560], P(('dp', 'seq'))
- grad_out_proj: float32 [2560, 2048], P(('dp', 'seq'))
- grad_norm_two: float32 [2048], P(('dp', 'seq'))
- grad_mlp_gate: float32 [2048, 6144], P(('dp', 'seq'))
- grad_mlp_up: float32 [2048, 6144], P(('dp', 'seq'))
- grad_mlp_down: float32 [6144, 2048], P(('dp', 'seq'))
The draws below stay inside these ranges and needn't reach their ends.
Inputs may be any that keep to these rules, and one draw needn't show every extreme that they name: `segment_ids`: along each row the ids start at 0 and rise by one where a new item begins. Among the 2 rows of each index of dp, one row is a single item of 1024 tokens; every other row holds exactly 5 items.
All inputs are finite; a program needn't handle non-finite values.
Results may differ from the reference program's by a relative error of at most 0.012.
The reference program's roundings to bfloat16 on the way count: a program that leaves them out, or rounds other values in their place, can miss the bound.
Values may be sent and summed in bfloat16 or wider, within the bound.
No kernel may reach another device: no remote copies, remote signals or barrier semaphores. Data moves between devices by JAX's collectives and lax.ppermute only.
A program may use at most 448 MiB of HBM per device.

```python
import jax
import jax.numpy as jnp
from jax import lax

D = 2048
WIDTH = 2560
HEADS = 16
BS = 160
KW = 4
FF = 6144
ROW_DEV = 2
LENGTH = 1024
ROWS = 8


def draw_segment_ids(key, part):
    key = jax.random.fold_in(key, 7)
    start_key, pick_key = jax.random.split(key)
    row_keys = jax.random.split(start_key, ROWS)

    def pick_starts(row_key):
        order = jax.random.permutation(row_key, LENGTH - 1)
        return order[:4].astype(jnp.int32) + 1
    chosen_spots = jax.vmap(pick_starts)(row_keys)
    position = jnp.arange(LENGTH, dtype=jnp.int32)
    item_starts = jnp.sum((position[None, None, :] == chosen_spots[:, :, None]).astype(jnp.int32), axis=1)
    chosen = jax.random.randint(pick_key, (ROWS // ROW_DEV,), 0, ROW_DEV)
    row_order = jnp.arange(ROWS, dtype=jnp.int32)
    single_row = row_order % ROW_DEV == jnp.repeat(chosen, ROW_DEV)
    item_starts = jnp.where(single_row[:, None], 0, item_starts)
    return jnp.cumsum(item_starts, axis=1).astype(jnp.int32)


def draw_decay_param(key, part):
    key = jax.random.fold_in(key, 11)
    levels = jax.random.uniform(key, (WIDTH,), jnp.float32, 4.5, 10.5)
    return levels.astype(jnp.bfloat16)


def shard_levels(rng, shape, cuts, least, high):
    level, own = 1.0, jax.random.fold_in(rng, 6)
    for dim, shards_of in cuts:
        draws = jnp.exp(jax.random.uniform(jax.random.fold_in(own, dim), (shards_of,), jnp.float32, least / len(cuts), high / len(cuts)))
        level = level * jnp.repeat(draws, shape[dim] // shards_of).reshape([-1 if axis == dim else 1 for axis in range(len(shape))])
    return level


def centred(own_key, shape, scale, limit, cuts=(), held_as=jnp.bfloat16):
    values = scale * jax.random.normal(own_key, shape, jnp.float32)
    if cuts:
        values = values * shard_levels(own_key, shape, cuts, -0.22, 0.18)
    return jnp.clip(values, -limit, limit).astype(held_as)


def setup_inputs(seed: int = 0) -> dict:
    key_list = jax.random.split(jax.random.key(seed), 19)
    return {
        "tokens": centred(key_list[0], (ROWS, LENGTH, D), 1.0, 6.0, ((0, 4), (1, 8))),
        "segment_ids": draw_segment_ids(jax.random.fold_in(key_list[18], 71), 0),
        "cotangent": centred(key_list[2], (ROWS, LENGTH, D), 1.0, 6.0, ((0, 4), (1, 8))),
        "norm_one": jnp.clip(1.0 + 0.1 * jax.random.normal(key_list[3], (D,), jnp.float32), 0.5, 1.5).astype(jnp.bfloat16),
        "branch_weight": centred(key_list[4], (D, WIDTH), D ** -0.5, 0.125, ((0, 32),)),
        "input_proj": centred(key_list[5], (D, WIDTH), D ** -0.5, 0.125, ((0, 32),)),
        "conv_weight": centred(key_list[6], (KW, WIDTH), KW ** -0.5, 3.0, ((1, 32),)),
        "conv_bias": centred(key_list[7], (WIDTH,), 0.5, 3.0, ((0, 32),)),
        "rate_weight": centred(key_list[8], (WIDTH, BS), BS ** -0.5, 0.5, ((0, 32),)),
        "igate_weight": centred(key_list[9], (WIDTH, BS), BS ** -0.5, 0.5, ((0, 32),)),
        "rate_bias": centred(key_list[10], (WIDTH,), 1.0, 4.0, ((0, 32),)),
        "igate_bias": centred(key_list[11], (WIDTH,), 1.0, 4.0, ((0, 32),)),
        "decay_param": draw_decay_param(jax.random.fold_in(key_list[18], 71), 0),
        "out_proj": centred(key_list[13], (WIDTH, D), (WIDTH // 16) ** -0.5, 0.5, ((0, 32),)),
        "norm_two": jnp.clip(1.0 + 0.1 * jax.random.normal(key_list[14], (D,), jnp.float32), 0.5, 1.5).astype(jnp.bfloat16),
        "mlp_gate": centred(key_list[15], (D, FF), D ** -0.5, 0.125, ((0, 32),)),
        "mlp_up": centred(key_list[16], (D, FF), D ** -0.5, 0.125, ((0, 32),)),
        "mlp_down": centred(key_list[17], (FF, D), (FF // 4) ** -0.5, 0.15625, ((0, 32),)),
    }


@jax.custom_vjp
def low(v):
    return lax.optimization_barrier(v.astype(jnp.bfloat16)).astype(jnp.float32)

@jax.custom_vjp
def low_back(v):
    return v

def low_keep(v):
    return (low(v), None)

def low_pass(kept, grad):
    return (grad,)

def back_keep(v):
    return (v, None)

def back_low(kept, grad):
    return (low(grad),)
low.defvjp(low_keep, low_pass)
low_back.defvjp(back_keep, back_low)
eps_value = 1e-06
rate_scale = 8.0
floor_value = 0.001

def gelu_tanh(value):
    return jax.nn.gelu(value, approximate=True)

def matmul(left, right):
    return jnp.dot(left, right, precision=lax.Precision.HIGHEST)

def rms_scale(values, gain):
    return values * lax.rsqrt(lax.optimization_barrier(jnp.mean(values * values, axis=-1, keepdims=True)) + eps_value) * gain

def block_mix(inputs, weights):
    count = inputs.shape[0]
    blocks = weights.reshape(HEADS, BS, BS)
    mixed = jnp.einsum('thi,hio->tho', inputs.reshape(count, HEADS, BS), blocks, precision=lax.Precision.HIGHEST)
    return mixed.reshape(count, HEADS * BS)

def gate_terms(rate_pre, igate_pre, conv_value, decay_value, start_flags):
    rate = jax.nn.sigmoid(rate_pre)
    igate = jax.nn.sigmoid(igate_pre)
    log_keep = -rate_scale * jax.nn.softplus(-decay_value) * rate
    keep = jnp.exp(log_keep)
    multiplier = jnp.where(start_flags, 1.0, jnp.sqrt(jnp.maximum(-jnp.expm1(2.0 * log_keep), floor_value)))
    return (jnp.where(start_flags, 0.0, keep), multiplier * igate * conv_value)

def combine(earlier, later):
    return (earlier[0] * later[0], later[1] + later[0] * earlier[1])

def forward(inputs, seg_row, params):
    gain_one, w_branch, w_input, w_conv, b_conv, w_rate, w_igate, b_rate, b_igate, decay_value, w_out, gain_two, w_gate, w_up, w_down = params
    normed_one = low(rms_scale(inputs, gain_one))
    branch = gelu_tanh(low_back(matmul(normed_one, w_branch)))
    conv_in = low_back(low(matmul(normed_one, w_input)))
    prev_ids = jnp.concatenate([jnp.full((1,), -1, jnp.int32), seg_row[:-1].astype(jnp.int32)])
    start_flags = (seg_row != prev_ids)[:, None]
    conv_sum = b_conv + w_conv[0] * conv_in
    for shift_by in range(1, KW):
        moved = jnp.concatenate([jnp.zeros((shift_by, WIDTH), jnp.float32), conv_in[:-shift_by]], axis=0)
        moved_ids = jnp.concatenate([jnp.full((shift_by,), -1, jnp.int32), seg_row[:-shift_by].astype(jnp.int32)])
        conv_sum = conv_sum + w_conv[shift_by] * moved * (moved_ids == seg_row).astype(jnp.float32)[:, None]
    conv_value = low_back(low(conv_sum))
    rate_pre = low_back(block_mix(conv_value, w_rate) + b_rate)
    igate_pre = low_back(block_mix(conv_value, w_igate) + b_igate)
    keep_eff, drive = gate_terms(rate_pre, igate_pre, conv_value, decay_value, start_flags)
    unused, state = lax.associative_scan(combine, (keep_eff, drive), axis=0)
    mixed = low(branch * state)
    resid = inputs + low_back(matmul(mixed, w_out))
    normed_two = low(rms_scale(resid, gain_two))
    gate_pre = low_back(matmul(normed_two, w_gate))
    up_value = low_back(matmul(normed_two, w_up))
    hidden = low(gelu_tanh(gate_pre) * up_value)
    return resid + low_back(matmul(hidden, w_down))

def reference(tokens, segment_ids, cotangent, norm_one, branch_weight, input_proj, conv_weight, conv_bias, rate_weight, igate_weight, rate_bias, igate_bias, decay_param, out_proj, norm_two, mlp_gate, mlp_up, mlp_down):
    params = tuple((weight.astype(jnp.float32) for weight in (norm_one, branch_weight, input_proj, conv_weight, conv_bias, rate_weight, igate_weight, rate_bias, igate_bias, decay_param, out_proj, norm_two, mlp_gate, mlp_up, mlp_down)))

    def one_row(totals, row_data):
        row_tokens, row_ids, row_cot = row_data

        def apply_row(inputs, weights):
            return forward(inputs, row_ids, weights)
        row_out, back_fn = jax.vjp(apply_row, row_tokens.astype(jnp.float32), params)
        grad_row, grad_params = back_fn(row_cot.astype(jnp.float32))
        totals = tuple((total + piece for total, piece in zip(totals, grad_params)))
        return (totals, (row_out.astype(jnp.bfloat16), grad_row))
    initial = tuple((jnp.zeros_like(weight) for weight in params))
    totals, outputs = lax.scan(one_row, initial, (tokens, segment_ids, cotangent))
    block_out, grad_tokens = outputs
    return (block_out, grad_tokens, totals[0], totals[1], totals[2], totals[3], totals[4], totals[5], totals[6], totals[7], totals[8], totals[9], totals[10], totals[11], totals[12], totals[13], totals[14])
```

```python
import functools

import jax
import jax.numpy as jnp
from jax import lax
from jax.experimental import pallas as pl
from jax.experimental.pallas import tpu as pltpu
from jax.sharding import PartitionSpec as P

HEADS = 16
BS = 160
AXES = ("dp", "seq")

eps_value = 1e-06
rate_scale = 8.0
floor_value = 0.001
low = jnp.bfloat16
wide = jnp.float32


def gelu_tanh(value):
    return jax.nn.gelu(value, approximate=True)


def dot_nn(left, right):
    return lax.dot_general(left, right, (((1,), (0,)), ((), ())), preferred_element_type=wide)


def dot_nt(left, right):
    return lax.dot_general(left, right, (((1,), (1,)), ((), ())), preferred_element_type=wide)


def dot_tn(left, right):
    return lax.dot_general(left, right, (((0,), (0,)), ((), ())), preferred_element_type=wide)


def lay_out_kernel(count, c_ref, *refs):
    parts, (out_ref, buffer, sem, out_sem) = refs[: 2 * count], refs[2 * count :]
    core = c_ref[0]
    copies = []
    for which in range(2):
        start = (core if which == 0 else 1 - core) * (out_ref.shape[0] // 2)
        for i, part in enumerate(parts[which * count : (which + 1) * count]):
            at = pl.ds(pl.multiple_of(start, 16), part.shape[0])
            j = which * count + i
            into = pltpu.make_async_copy(part, buffer.at[at], sem.at[j])
            into.start()
            copies.append((into, pltpu.make_async_copy(buffer.at[at], out_ref.at[at], out_sem.at[j])))
            start = start + part.shape[0]
    for into, out in copies:
        into.wait()
        out.start()
    for into, out in copies:
        out.wait()


def lay_out(core, own, other):
    rows = 2 * sum(part.shape[0] for part in own)
    shape = (rows,) + own[0].shape[1:]
    anywhere = pl.BlockSpec(memory_space=pl.ANY)
    return pl.pallas_call(
        functools.partial(lay_out_kernel, len(own)),
        out_shape=jax.ShapeDtypeStruct(shape, own[0].dtype),
        in_specs=[pl.BlockSpec(memory_space=pltpu.SMEM)] + [anywhere] * (2 * len(own)),
        out_specs=anywhere,
        scratch_shapes=[
            pltpu.VMEM(shape, own[0].dtype),
            pltpu.SemaphoreType.DMA((2 * len(own),)),
            pltpu.SemaphoreType.DMA((2 * len(own),)),
        ],
        compiler_params=pltpu.CompilerParams(vmem_limit_bytes=32 * 2**20),
    )(core.reshape(1).astype(jnp.int32), *own, *other)


def together(*arrays):
    return lax.optimization_barrier(arrays)


def cut_kernel(k_count, z_count, gate_ref, up_ref, out_ref):
    own = out_ref.shape[3] // (2 * z_count)
    for k in range(k_count):
        for c in range(2):
            for which, ref in enumerate((gate_ref, up_ref)):
                for z in range(z_count):
                    at = ((k * z_count + z) * 2 + c) * own
                    to = (which * z_count + z) * own
                    out_ref[k, c, :, to : to + own] = ref[:, at : at + own]


def join_kernel(k_count, z_count, in_ref, gate_ref, up_ref):
    own = in_ref.shape[3] // (2 * z_count)
    for k in range(k_count):
        for c in range(2):
            for which, ref in enumerate((gate_ref, up_ref)):
                for z in range(z_count):
                    to = ((k * z_count + z) * 2 + c) * own
                    at = (which * z_count + z) * own
                    ref[:, to : to + own] = in_ref[k, c, :, at : at + own].astype(ref.dtype)


def in_vmem(kernel, arrays, out_shape):
    vmem = pl.BlockSpec(memory_space=pltpu.VMEM)
    return pl.pallas_call(
        kernel,
        out_shape=out_shape,
        in_specs=[vmem] * len(arrays),
        out_specs=jax.tree.map(lambda _: vmem, out_shape),
        compiler_params=pltpu.CompilerParams(vmem_limit_bytes=48 * 2**20),
    )(*arrays)


class Place:
    def __init__(self):
        self.k_count = lax.axis_size("dp")
        self.s_count = lax.axis_size("seq")
        self.z_count = self.s_count // 2
        self.k = lax.axis_index("dp")
        self.s = lax.axis_index("seq")
        self.c = self.s % 2
        self.z = self.s // 2
        self.square = self.k_count == 4
        self.z_groups = [
            [k * self.s_count + 2 * z + c for z in range(self.z_count)]
            for k in range(self.k_count)
            for c in range(2)
        ]
        self.plane_groups = [
            [k * self.s_count + 2 * z + c for k in range(self.k_count) for c in range(2)]
            for z in range(self.z_count)
        ]

    def to_k(self, array, flip):
        return lax.ppermute(array, "dp", [(i, i ^ flip) for i in range(self.k_count)])

    def to_core(self, array):
        return lax.ppermute(array, "seq", [(i, i ^ 1) for i in range(self.s_count)])

    def to_z(self, array, by):
        pairs = [(i, i + 2 * by) for i in range(self.s_count) if 0 <= i + 2 * by < self.s_count]
        return lax.ppermute(array, "seq", pairs)

    def by_core(self, own, other):
        return jnp.where(self.c == 0, jnp.stack([own, other]), jnp.stack([other, own]))

    def gather_z(self, array):
        return lax.all_gather(array, AXES, axis_index_groups=self.z_groups, tiled=True)

    def z_pairs(self, pairs):
        return [(2 * a + c, 2 * b + c) for a, b in pairs for c in range(2)]

    def own_apart(self, split, axis):
        shape = [1] * split.ndim
        shape[axis] = self.z_count
        own = (jnp.arange(self.z_count) == self.z).reshape(shape)
        sent = jnp.moveaxis(jnp.where(own, 0.0, split).astype(low), axis, 0)
        kept = lax.dynamic_index_in_dim(split, self.z, axis, False)
        return sent.reshape((-1,) + sent.shape[-1:]), kept.reshape((-1,) + sent.shape[-1:])

    def scatter_z(self, parts):
        total = lax.psum_scatter(
            parts[0], AXES, scatter_dimension=0, axis_index_groups=self.z_groups, tiled=True
        )
        return total, parts[1]


    def sum_far(self, chunk):
        if self.z_count != 4:
            return ()
        pairs = self.z_pairs([(0, 1), (3, 2)])
        return (lax.ppermute(chunk(3 - self.z).astype(low), "seq", pairs),)

    def sum_near(self, chunk):
        if self.z_count != 4:
            return ()
        below = self.to_z(chunk(jnp.minimum(self.z + 1, 3)).astype(low), 1)
        above = self.to_z(chunk(jnp.maximum(self.z - 1, 0)).astype(low), -1)
        return below, above

    def sum_second(self, chunk, far):
        if self.z_count != 4:
            return ()
        second = (chunk(self.z ^ 2).astype(wide) + far[0].astype(wide)).astype(low)
        return (lax.ppermute(second, "seq", self.z_pairs([(0, 2), (1, 3), (2, 0), (3, 1)])),)

    def sum_all(self, chunk, near, second):
        if self.z_count != 4:
            whole = jnp.concatenate([chunk(i) for i in range(self.z_count)], axis=0).astype(low)
            whole = lax.psum_scatter(
                whole, AXES, scatter_dimension=0, axis_index_groups=self.z_groups, tiled=True
            )
            return whole.astype(wide)
        total = chunk(self.z).astype(wide)
        for part in near + second:
            total = total + part.astype(wide)
        return total

    def gather_line_small(self, array):
        if not (self.square and self.z_count == 4):
            whole = lax.all_gather(array, AXES)
            return whole.reshape((self.k_count, self.s_count) + array.shape)
        out = array[None]
        for bit in range(3):
            got = lax.ppermute(out, "seq", [(i, i ^ (1 << bit)) for i in range(8)])
            low_bit = (self.s >> bit) % 2 == 0
            out = jnp.where(low_bit, jnp.concatenate([out, got]), jnp.concatenate([got, out]))
        out = out[None]
        for bit in range(2):
            got = self.to_k(out, 1 << bit)
            low_bit = (self.k >> bit) % 2 == 0
            out = jnp.where(low_bit, jnp.concatenate([out, got]), jnp.concatenate([got, out]))
        return out

    def gather_plane(self, array):
        if not self.square:
            whole = lax.all_gather(array, AXES, axis_index_groups=self.plane_groups)
            whole = whole.reshape((self.k_count, 2) + array.shape)
            return jnp.swapaxes(whole, 0, 1).reshape((-1,) + array.shape[1:])
        half = array.shape[0] // 2
        from_x = self.to_k(array, 1)
        from_y = self.to_k(array, 2)
        far_a = self.to_k(from_x[:half], 2)
        far_b = self.to_k(from_y[half:], 1)
        mine = [array, from_x, from_y, far_a, far_b]
        return lay_out(self.c, mine, [self.to_core(part) for part in mine])

    def gather_plane_small(self, array):
        if not self.square:
            return self.gather_plane(array)
        near = jnp.stack([array, self.to_k(array, 1)])
        mine = jnp.concatenate([near, self.to_k(near, 2)])
        return self.by_core(mine, self.to_core(mine)).reshape((-1,) + array.shape[1:])

    def halves(self, array):
        count = array.shape[0] // 2
        own = lax.dynamic_slice_in_dim(array, self.c * count, count, 0)
        return own, lax.dynamic_slice_in_dim(array, (1 - self.c) * count, count, 0)

    def chip_product(self, left, right, dot, exact=False):
        own, other = self.halves(left)
        sent = dot(other, right)
        sent = self.to_core(sent if exact else sent.astype(low))
        chip = dot(own, right) + sent.astype(wide)
        return chip.reshape(self.k_count, own.shape[0] // self.k_count, -1)

    def sum_plane(self, chip, exact=False):
        if not self.square:
            return lax.psum_scatter(chip, "dp", scatter_dimension=0, tiled=False)
        half = chip.shape[2] // 2

        def send(parts, power, flip):
            if not exact:
                return self.to_k(parts.astype(low), flip).astype(wide), None
            scaled = (parts * jnp.exp2(-power)).astype(jnp.float16)
            power = jnp.broadcast_to(power, power.shape[:-1] + (128,)).astype(jnp.float16)
            got = self.to_k(jnp.concatenate([scaled, power], axis=-1), flip).astype(wide)
            got_power = got[..., half : half + 1]
            return got[..., :half] * jnp.exp2(got_power), got_power

        power = None
        if exact:
            largest = jnp.max(jnp.abs(chip), axis=2, keepdims=True)
            power = jnp.ceil(jnp.log2(jnp.clip(largest, 1e-30, 1e37)))

        def pick(a, i, j):
            return a if a is None else jnp.stack([a[i], a[j]])

        def above(a, i, b, j):
            return a if a is None else jnp.maximum(a[i], b[j]) + 1.0

        got_a, power_a = send(pick(chip[..., :half], 1, 3), pick(power, 1, 3), 1)
        got_b, power_b = send(pick(chip[..., half:], 2, 3), pick(power, 2, 3), 2)
        last_a, _ = send(chip[2, :, :half] + got_a[1], above(power_a, 1, power, 2), 2)
        last_b, _ = send(chip[1, :, half:] + got_b[1], above(power_b, 1, power, 1), 1)
        return jnp.concatenate(
            [chip[0, :, :half] + got_a[0] + last_a, chip[0, :, half:] + got_b[0] + last_b], axis=1
        )

    def exchange_plane(self, array):
        keep = lax.dynamic_index_in_dim(array, self.c, 1, False)
        got = self.to_core(lax.dynamic_index_in_dim(array, 1 - self.c, 1, False))
        pairs = jnp.moveaxis(self.by_core(keep, got), 0, 1)
        if not self.square:
            return lax.all_to_all(pairs, "dp", 0, 0, tiled=True)
        parts = [lax.dynamic_index_in_dim(pairs, self.k, 0, False)]
        for flip in range(1, 4):
            parts.append(self.to_k(lax.dynamic_index_in_dim(pairs, self.k ^ flip, 0, False), flip))
        odd = self.k % 2 == 1
        parts = [jnp.where(odd, parts[i ^ 1], parts[i]) for i in range(4)]
        upper = self.k >= 2
        return jnp.stack([jnp.where(upper, parts[i ^ 2], parts[i]) for i in range(4)])


def scan_loop(rows, span, step, state, reverse):
    for part in (1, 0) if reverse else (0, 1):
        base = part * rows * span

        def one(i, state, base=base):
            return step(base + (span - 1 - i if reverse else i), state)

        state = lax.fori_loop(0, span, one, state, unroll=8)
    return state


def summary_kernel(rows, span, keep_ref, drive_ref, out_ref):
    def step(at, state):
        keep = keep_ref[pl.ds(at, rows, stride=span), :]
        drive = drive_ref[pl.ds(at, rows, stride=span), :]
        return state[0] * keep, state[1] * keep + drive

    shape = (rows, keep_ref.shape[1])
    start = (jnp.ones(shape, wide), jnp.zeros(shape, wide))
    product, end = scan_loop(rows, span, step, start, False)
    out_ref[0] = product
    out_ref[1] = end


def state_kernel(rows, span, keep_ref, drive_ref, start_ref, state_ref, prev_ref):
    def step(at, state):
        prev_ref[pl.ds(at, rows, stride=span), :] = state
        keep = keep_ref[pl.ds(at, rows, stride=span), :]
        drive = drive_ref[pl.ds(at, rows, stride=span), :]
        state = state * keep + drive
        state_ref[pl.ds(at, rows, stride=span), :] = state
        return state

    scan_loop(rows, span, step, start_ref[...], False)


def back_summary_kernel(rows, span, keep_ref, grad_ref, out_ref):
    def step(at, state):
        keep = keep_ref[pl.ds(at, rows, stride=span), :]
        grad = grad_ref[pl.ds(at, rows, stride=span), :]
        return keep * (grad + state)

    out_ref[...] = scan_loop(rows, span, step, jnp.zeros(out_ref.shape, wide), True)


def adjoint_kernel(rows, span, keep_ref, grad_ref, start_ref, adjoint_ref):
    def step(at, state):
        keep = keep_ref[pl.ds(at, rows, stride=span), :]
        adjoint = grad_ref[pl.ds(at, rows, stride=span), :] + state
        adjoint_ref[pl.ds(at, rows, stride=span), :] = adjoint
        return keep * adjoint

    scan_loop(rows, span, step, start_ref[...], True)


def scan_call(kernel, rows, span, arrays, out_shape):
    def block(array):
        lead = array.ndim - 1
        return pl.BlockSpec(array.shape[:-1] + (128,), lambda i, lead=lead: (0,) * lead + (i,))

    return pl.pallas_call(
        functools.partial(kernel, rows, span),
        out_shape=out_shape,
        grid=(pl.cdiv(arrays[0].shape[-1], 128),),
        in_specs=[block(a) for a in arrays],
        out_specs=jax.tree.map(block, out_shape),
        compiler_params=pltpu.CompilerParams(vmem_limit_bytes=48 * 2**20),
    )(*arrays)


def per_device(
    tokens,
    segment_ids,
    cotangent,
    norm_one,
    branch_weight,
    input_proj,
    conv_weight,
    conv_bias,
    rate_weight,
    igate_weight,
    rate_bias,
    igate_bias,
    decay_param,
    out_proj,
    norm_two,
    mlp_gate,
    mlp_up,
    mlp_down,
):
    at = Place()
    k_count, z_count = at.k_count, at.z_count
    group = 2 * k_count
    row_dev, span, width_d = tokens.shape
    tok = row_dev * span
    rows = k_count * row_dev
    tok_all = 2 * rows * span
    d_own = norm_one.shape[0]
    w_own = conv_bias.shape[0]
    f_own = mlp_down.shape[0]
    width_r = branch_weight.shape[1]
    w_slot = width_r // group
    f_slot = f_own * z_count
    taps = conv_weight.shape[0]
    reach = taps - 1
    half_z = z_count // 2

    def by_feature(array):
        split = array.reshape(z_count, k_count, 2 * d_own, array.shape[1])
        return jnp.swapaxes(split, 0, 1).reshape(array.shape)

    small = jnp.concatenate(
        [
            norm_one,
            norm_two,
            conv_weight.reshape(-1),
            conv_bias,
            rate_bias,
            igate_bias,
            decay_param,
        ]
    )
    small_all = at.gather_line_small(small).reshape(k_count * at.s_count, -1)
    gain_one = small_all[:, :d_own].reshape(1, width_d).astype(wide)
    gain_two = small_all[:, d_own : 2 * d_own].reshape(1, width_d).astype(wide)
    mine = lax.dynamic_slice_in_dim(
        small_all[:, 2 * d_own :], at.k * at.s_count + at.c * z_count, z_count, 0
    )
    mine = mine.reshape(z_count, taps + 4, w_own).astype(wide)
    mine = jnp.swapaxes(mine, 0, 1).reshape(taps + 4, w_slot)
    w_conv = mine[:taps]
    b_conv, b_rate, b_igate, decay = (mine[taps + i][None, :] for i in range(4))

    out_cols = width_d + 2 * BS
    out_part = at.gather_z(jnp.concatenate([out_proj, rate_weight, igate_weight], axis=1))
    out_part = out_part.reshape(2, half_z * w_own, out_cols)
    out_keep = lax.dynamic_index_in_dim(out_part, at.c, 0, False)
    out_got = at.to_core(lax.dynamic_index_in_dim(out_part, 1 - at.c, 0, False))
    w3 = at.by_core(
        out_keep.reshape(half_z, w_own, out_cols), out_got.reshape(half_z, w_own, out_cols)
    )
    w3 = jnp.swapaxes(w3, 0, 1).reshape(w_slot, out_cols)
    w_out = w3[:, :width_d]
    heads = w_slot // BS

    def block_diagonal(columns):
        blocks = columns.reshape(heads, BS, 1, BS)
        same = jnp.eye(heads, dtype=low).reshape(heads, 1, heads, 1)
        return (blocks * same).reshape(w_slot, w_slot)

    w_gates = jnp.concatenate(
        [block_diagonal(w3[:, width_d : width_d + BS]), block_diagonal(w3[:, width_d + BS :])], axis=1
    )

    rec_cols = jnp.concatenate(
        [
            branch_weight.reshape(d_own, k_count, 2, w_slot),
            input_proj.reshape(d_own, k_count, 2, w_slot),
        ],
        axis=3,
    )
    rec_cols = at.exchange_plane(jnp.moveaxis(rec_cols, 0, 2))
    rec_cols, tokens, mlp_gate = together(rec_cols, tokens, mlp_gate)
    w1 = by_feature(at.gather_z(rec_cols.reshape(group * d_own, 2 * w_slot)))

    inputs = tokens.reshape(tok, width_d).astype(wide)
    s1 = lax.rsqrt(jnp.mean(inputs * inputs, axis=-1, keepdims=True) + eps_value)
    normed_one = (inputs * s1 * gain_one).astype(low)
    n1_all = at.gather_plane(normed_one)
    mlp_shape = jax.ShapeDtypeStruct((k_count, 2, d_own, 2 * f_slot), low)
    cut = functools.partial(cut_kernel, k_count, z_count)
    mlp_cols = at.exchange_plane(in_vmem(cut, (mlp_gate, mlp_up), mlp_shape))
    seg_code = at.gather_plane_small((segment_ids % 64).astype(low)).reshape(2, rows, span)
    n1_all, mlp_cols, seg_code, cot = together(n1_all, mlp_cols, seg_code, cotangent.reshape(tok, width_d))
    w2 = by_feature(at.gather_z(mlp_cols.reshape(group * d_own, 2 * f_slot)))

    def with_before(array):
        tail = array[:, :, span - reach :]
        return jnp.concatenate([jnp.stack([at.to_z(tail[1], 1), tail[0]]), array], axis=2)

    def with_after(array):
        head = array[:, :, :reach]
        return jnp.concatenate([array, jnp.stack([head[1], at.to_z(head[0], -1)])], axis=2)

    pre_one = dot_nn(n1_all, w1)
    w_down = at.gather_z(mlp_down)
    cot_all = at.gather_plane(cot)
    branch, branch_back = jax.vjp(gelu_tanh, pre_one[:, :w_slot])
    conv_in = pre_one[:, w_slot:].astype(low).reshape(2, rows, span, w_slot)
    ext_in = with_before(conv_in)
    ext_code = with_before(seg_code)
    position = lax.broadcasted_iota(jnp.int32, (2, rows, span), 2)
    position = position + span * lax.broadcasted_iota(jnp.int32, (2, rows, span), 0)
    row_begin = (at.z == 0) & (position == 0)
    starts = (ext_code[:, :, reach - 1 : reach - 1 + span] != seg_code) | row_begin
    conv_sum = b_conv + w_conv[0] * conv_in.astype(wide)
    same_items = [None]
    for shift_by in range(1, taps):
        same_item = ext_code[:, :, reach - shift_by : reach - shift_by + span] == seg_code
        same_item = same_item & ((at.z > 0) | (position >= shift_by))
        same_items.append(same_item.astype(wide)[..., None])
        moved = ext_in[:, :, reach - shift_by : reach - shift_by + span].astype(wide)
        conv_sum = conv_sum + w_conv[shift_by] * moved * same_items[shift_by]
    conv_low = conv_sum.astype(low).reshape(tok_all, w_slot)
    starts = starts.reshape(tok_all, 1)
    gates_pre = dot_nn(conv_low, w_gates)
    rate = jax.nn.sigmoid(gates_pre[:, :w_slot] + b_rate)
    igate = jax.nn.sigmoid(gates_pre[:, w_slot:] + b_igate)
    conv_value = conv_low.astype(wide)
    log_slope = -rate_scale * jax.nn.softplus(-decay)
    log_keep = log_slope * rate
    keep = jnp.exp(log_keep)
    room = -jnp.expm1(2.0 * log_keep)
    mult = jnp.where(starts, 1.0, jnp.sqrt(jnp.maximum(room, floor_value)))
    keep_eff = jnp.where(starts, 0.0, keep)
    drive = mult * igate * conv_value
    flat = jax.ShapeDtypeStruct((tok_all, w_slot), wide)
    ends = jax.ShapeDtypeStruct((rows, w_slot), wide)
    both = jax.ShapeDtypeStruct((2, rows, w_slot), wide)
    summary = scan_call(summary_kernel, rows, span, (keep_eff, drive), both)
    before = [at.to_z(summary, by) for by in range(1, z_count)]
    state_in = jnp.zeros((rows, w_slot), wide)
    for part in reversed(before):
        state_in = part[1] + part[0] * state_in
    state, state_prev = scan_call(
        state_kernel, rows, span, (keep_eff, drive, state_in), (flat, flat)
    )
    mixed = (branch * state).astype(low)
    mixed, cot_all = together(mixed, cot_all)

    chip_one = at.chip_product(mixed, w_out, dot_nn, exact=True)
    resid = inputs + at.sum_plane(chip_one, exact=True)
    resid, w2 = together(resid, w2)

    s2 = lax.rsqrt(jnp.mean(resid * resid, axis=-1, keepdims=True) + eps_value)
    normed_two = (resid * s2 * gain_two).astype(low)
    n2_all, w_down = together(at.gather_plane(normed_two), w_down)
    pre_two = dot_nn(n2_all, w2)
    gate_act, gate_back = jax.vjp(gelu_tanh, pre_two[:, :f_slot])
    up_value = pre_two[:, f_slot:]
    hidden = (gate_act * up_value).astype(low)

    grad_hidden = dot_nt(cot_all, w_down)
    grad_gate_pre = gate_back(grad_hidden * up_value)[0].astype(low)
    grad_up = (grad_hidden * gate_act).astype(low)
    grad_two = jnp.concatenate([grad_gate_pre, grad_up], axis=1)
    chip_two = at.chip_product(grad_two, w2, dot_nt)
    chip_two, hidden_then, grad_two = together(chip_two, hidden, grad_two)

    def rows_split(product):
        return product.reshape(k_count, z_count, 2 * d_own, -1)

    down_part = at.own_apart(dot_tn(hidden_then, cot_all).reshape(z_count, f_own, width_d), 0)
    w2_part = at.own_apart(rows_split(dot_tn(n2_all, grad_two)), 1)
    grad_n2, hidden, w2_part, down_part = together(at.sum_plane(chip_two), hidden, w2_part, down_part)
    down_sum = at.scatter_z(down_part)
    w2_sum = at.scatter_z(w2_part)
    chip_three = at.chip_product(hidden, w_down, dot_nn)
    scaled_two = gain_two * grad_n2
    cot_f = cot.astype(wide)
    mean_two = jnp.mean(scaled_two * resid, axis=-1, keepdims=True)
    grad_resid = cot_f + s2 * scaled_two - resid * (s2 * s2 * s2) * mean_two
    grad_recur = grad_resid.astype(low)
    gr_all = at.gather_plane(grad_recur)
    gr_all, chip_three, down_sum = together(gr_all, chip_three, down_sum)
    block_out = (resid + at.sum_plane(chip_three)).astype(low)

    def summed(pair):
        return pair[0].astype(wide) + pair[1].astype(wide)

    grad_down = summed(down_sum)

    grad_mixed = dot_nt(gr_all, w_out)
    grad_out = dot_tn(mixed, gr_all)
    grad_branch = branch_back(grad_mixed * state)[0].astype(low)
    grad_state = grad_mixed * branch
    back = scan_call(back_summary_kernel, rows, span, (keep_eff, grad_state), ends)
    own = jnp.stack([summary[0], back])
    after = [at.to_z(own, -by) for by in range(1, z_count)]
    carry_in = jnp.zeros((rows, w_slot), wide)
    for part in reversed(after):
        carry_in = part[1] + part[0] * carry_in
    adjoint = scan_call(
        adjoint_kernel, rows, span, (keep_eff, grad_state, carry_in), flat
    )
    not_start = jnp.where(starts, 0.0, 1.0)
    through_mult = jnp.where(
        room > floor_value, adjoint * igate * conv_value * keep * keep / mult, 0.0
    )
    grad_log_keep = not_start * (adjoint * state_prev * keep - through_mult)
    grad_rate_pre = (grad_log_keep * log_slope * rate * (1.0 - rate)).astype(low)
    grad_igate_pre = (adjoint * mult * conv_value * igate * (1.0 - igate)).astype(low)
    grad_decay = jnp.sum(grad_log_keep * rate, axis=0) * (rate_scale * jax.nn.sigmoid(-decay[0]))
    grad_rate_bias = jnp.sum(grad_rate_pre.astype(wide), axis=0)
    grad_igate_bias = jnp.sum(grad_igate_pre.astype(wide), axis=0)
    grad_gates = jnp.concatenate([grad_rate_pre, grad_igate_pre], axis=1)
    grad_gates_w = dot_tn(conv_low, grad_gates).reshape(heads, BS, 2, heads, BS)
    grad_gates_w = jnp.stack([grad_gates_w[h, :, :, h] for h in range(heads)])
    grad_gates_w = grad_gates_w.reshape(w_slot, 2 * BS)
    grad_conv = adjoint * mult * igate + dot_nt(grad_gates, w_gates)
    grad_conv, block_out = together(
        grad_conv.astype(low).reshape(2, rows, span, w_slot), block_out
    )
    grad_conv_f = grad_conv.astype(wide)
    grad_conv_bias = jnp.sum(grad_conv_f, axis=(0, 1, 2))
    tap_grads = [jnp.sum(grad_conv_f * conv_in.astype(wide), axis=(0, 1, 2))]
    for shift_by in range(1, taps):
        moved = ext_in[:, :, reach - shift_by : reach - shift_by + span].astype(wide)
        tap_grads.append(jnp.sum(grad_conv_f * moved * same_items[shift_by], axis=(0, 1, 2)))
    ext_grad = with_after(grad_conv)
    next_code = with_after(seg_code)
    grad_conv_in = w_conv[0] * grad_conv_f
    for shift_by in range(1, taps):
        ahead_same = next_code[:, :, shift_by : shift_by + span] == seg_code
        ahead_same = ahead_same & ((at.z < z_count - 1) | (position < 2 * span - shift_by))
        ahead = ext_grad[:, :, shift_by : shift_by + span].astype(wide)
        grad_conv_in = grad_conv_in + w_conv[shift_by] * ahead * ahead_same.astype(wide)[..., None]
    grad_conv_in = grad_conv_in.astype(low).reshape(tok_all, w_slot)
    grad_conv_in, w2_sum = together(grad_conv_in, w2_sum)
    grad_one = jnp.concatenate([grad_branch, grad_conv_in], axis=1)
    w1_split = rows_split(dot_tn(n1_all, grad_one))

    def w1_chunk(i):
        return lax.dynamic_index_in_dim(w1_split, i, 1, False)

    w1_far, w1_near = at.sum_far(w1_chunk), at.sum_near(w1_chunk)
    grad_w1 = at.sum_all(w1_chunk, w1_near, at.sum_second(w1_chunk, w1_far))
    grad_n1 = at.sum_plane(at.chip_product(grad_one, w1, dot_nt))
    scaled_one = gain_one * grad_n1
    mean_one = jnp.mean(scaled_one * inputs, axis=-1, keepdims=True)
    grad_tokens = grad_resid + s1 * scaled_one - inputs * (s1 * s1 * s1) * mean_one
    grad_tokens = grad_tokens.reshape(row_dev, span, width_d)
    block_out = block_out.reshape(row_dev, span, width_d)

    vectors = jnp.stack(tap_grads + [grad_conv_bias, grad_rate_bias, grad_igate_bias, grad_decay], axis=1)
    rec_rows = jnp.concatenate([grad_out, grad_gates_w, vectors], axis=1).astype(low)
    rec_rows = jnp.pad(rec_rows, ((0, 0), (0, -rec_rows.shape[1] % 128)))
    rec_rows = rec_rows.reshape(half_z, 2, w_own, -1)
    rows_keep = lax.dynamic_index_in_dim(rec_rows, at.c, 1, False)
    rows_got = at.to_core(lax.dynamic_index_in_dim(rec_rows, 1 - at.c, 1, False))
    rec_split = at.by_core(rows_keep, rows_got).reshape(z_count, w_own, -1)
    rec_part, w2_sum = together(at.own_apart(rec_split, 0), w2_sum)
    rec_rows = summed(at.scatter_z(rec_part))
    grad_out_w = rec_rows[:, :width_d]
    grad_rate_w = rec_rows[:, width_d : width_d + BS]
    grad_igate_w = rec_rows[:, width_d + BS : out_cols]
    grad_small = rec_rows[:, out_cols : out_cols + taps + 4].T

    def to_owner(array, columns):
        return at.exchange_plane(array.reshape(k_count, 2, d_own, columns))

    mlp_back = to_owner(summed(w2_sum).astype(low), 2 * f_slot)
    mlp_whole = jax.ShapeDtypeStruct(mlp_gate.shape, wide)
    join = functools.partial(join_kernel, k_count, z_count)
    grad_gate_w, grad_up_w = in_vmem(join, (mlp_back,), (mlp_whole, mlp_whole))
    rec_back = jnp.moveaxis(to_owner(grad_w1, 2 * w_slot), 2, 0).astype(wide)
    grad_branch_w = rec_back[..., :w_slot].reshape(d_own, width_r)
    grad_input_w = rec_back[..., w_slot:].reshape(d_own, width_r)

    def gain_grad(pairs, gain):
        total = sum(jnp.sum(weight.astype(wide) * grad, axis=1) for weight, grad in pairs)
        return total / gain.astype(wide)

    grad_norm_one = gain_grad(((branch_weight, grad_branch_w), (input_proj, grad_input_w)), norm_one)
    grad_norm_two = gain_grad(((mlp_gate, grad_gate_w), (mlp_up, grad_up_w)), norm_two)
    return (
        block_out,
        grad_tokens,
        grad_norm_one,
        grad_branch_w,
        grad_input_w,
        grad_small[:taps],
        grad_small[taps],
        grad_rate_w,
        grad_igate_w,
        grad_small[taps + 1],
        grad_small[taps + 2],
        grad_small[taps + 3],
        grad_out_w,
        grad_norm_two,
        grad_gate_w,
        grad_up_w,
        grad_down,
    )


def solution(mesh):
    rows, matrix = P(AXES), P(AXES, None)
    tokens = P("dp", "seq", None)
    return jax.shard_map(
        per_device,
        mesh=mesh,
        in_specs=(
            tokens,
            P("dp", "seq"),
            tokens,
            rows,
            matrix,
            matrix,
            P(None, AXES),
            rows,
            matrix,
            matrix,
            rows,
            rows,
            rows,
            matrix,
            rows,
            matrix,
            matrix,
            matrix,
        ),
        out_specs=(
            tokens,
            tokens,
            rows,
            matrix,
            matrix,
            P(None, AXES),
            rows,
            matrix,
            matrix,
            rows,
            rows,
            rows,
            matrix,
            rows,
            matrix,
            matrix,
            matrix,
        ),
        check_vma=False,
    )
```

```python
import functools

import jax
import jax.numpy as jnp
from jax import lax
from jax.experimental import pallas as pl
from jax.experimental.pallas import tpu as pltpu
from jax.sharding import PartitionSpec as P

HEADS = 16
BS = 160
AXES = ("dp", "seq")

eps_value = 1e-06
rate_scale = 8.0
floor_value = 0.001
low = jnp.bfloat16
wide = jnp.float32


def gelu_tanh(value):
    return jax.nn.gelu(value, approximate=True)


def dot_nn(left, right):
    return lax.dot_general(left, right, (((1,), (0,)), ((), ())), preferred_element_type=wide)


def dot_nt(left, right):
    return lax.dot_general(left, right, (((1,), (1,)), ((), ())), preferred_element_type=wide)


def dot_tn(left, right):
    return lax.dot_general(left, right, (((0,), (0,)), ((), ())), preferred_element_type=wide)


def lay_out_kernel(count, c_ref, *refs):
    parts, (out_ref, buffer, sem, out_sem) = refs[: 2 * count], refs[2 * count :]
    core = c_ref[0]
    copies = []
    for which in range(2):
        start = (core if which == 0 else 1 - core) * (out_ref.shape[0] // 2)
        for i, part in enumerate(parts[which * count : (which + 1) * count]):
            at = pl.ds(pl.multiple_of(start, 16), part.shape[0])
            j = which * count + i
            into = pltpu.make_async_copy(part, buffer.at[at], sem.at[j])
            into.start()
            copies.append((into, pltpu.make_async_copy(buffer.at[at], out_ref.at[at], out_sem.at[j])))
            start = start + part.shape[0]
    for into, out in copies:
        into.wait()
        out.start()
    for into, out in copies:
        out.wait()


def lay_out(core, own, other):
    rows = 2 * sum(part.shape[0] for part in own)
    shape = (rows,) + own[0].shape[1:]
    anywhere = pl.BlockSpec(memory_space=pl.ANY)
    return pl.pallas_call(
        functools.partial(lay_out_kernel, len(own)),
        out_shape=jax.ShapeDtypeStruct(shape, own[0].dtype),
        in_specs=[pl.BlockSpec(memory_space=pltpu.SMEM)] + [anywhere] * (2 * len(own)),
        out_specs=anywhere,
        scratch_shapes=[
            pltpu.VMEM(shape, own[0].dtype),
            pltpu.SemaphoreType.DMA((2 * len(own),)),
            pltpu.SemaphoreType.DMA((2 * len(own),)),
        ],
        compiler_params=pltpu.CompilerParams(vmem_limit_bytes=32 * 2**20),
    )(core.reshape(1).astype(jnp.int32), *own, *other)


def together(*arrays):
    return lax.optimization_barrier(arrays)


def cut_kernel(k_count, z_count, gate_ref, up_ref, out_ref):
    own = out_ref.shape[3] // (2 * z_count)
    for k in range(k_count):
        for c in range(2):
            for which, ref in enumerate((gate_ref, up_ref)):
                for z in range(z_count):
                    at = ((k * z_count + z) * 2 + c) * own
                    to = (which * z_count + z) * own
                    out_ref[k, c, :, to : to + own] = ref[:, at : at + own]


def join_kernel(k_count, z_count, in_ref, gate_ref, up_ref):
    own = in_ref.shape[3] // (2 * z_count)
    for k in range(k_count):
        for c in range(2):
            for which, ref in enumerate((gate_ref, up_ref)):
                for z in range(z_count):
                    to = ((k * z_count + z) * 2 + c) * own
                    at = (which * z_count + z) * own
                    ref[:, to : to + own] = in_ref[k, c, :, at : at + own].astype(ref.dtype)


def in_vmem(kernel, arrays, out_shape):
    vmem = pl.BlockSpec(memory_space=pltpu.VMEM)
    return pl.pallas_call(
        kernel,
        out_shape=out_shape,
        in_specs=[vmem] * len(arrays),
        out_specs=jax.tree.map(lambda _: vmem, out_shape),
        compiler_params=pltpu.CompilerParams(vmem_limit_bytes=48 * 2**20),
    )(*arrays)


class Place:
    def __init__(self):
        self.k_count = lax.axis_size("dp")
        self.s_count = lax.axis_size("seq")
        self.z_count = self.s_count // 2
        self.k = lax.axis_index("dp")
        self.s = lax.axis_index("seq")
        self.c = self.s % 2
        self.z = self.s // 2
        self.square = self.k_count == 4
        self.z_groups = [
            [k * self.s_count + 2 * z + c for z in range(self.z_count)]
            for k in range(self.k_count)
            for c in range(2)
        ]
        self.plane_groups = [
            [k * self.s_count + 2 * z + c for k in range(self.k_count) for c in range(2)]
            for z in range(self.z_count)
        ]

    def to_k(self, array, flip):
        return lax.ppermute(array, "dp", [(i, i ^ flip) for i in range(self.k_count)])

    def to_core(self, array):
        return lax.ppermute(array, "seq", [(i, i ^ 1) for i in range(self.s_count)])

    def to_z(self, array, by):
        pairs = [(i, i + 2 * by) for i in range(self.s_count) if 0 <= i + 2 * by < self.s_count]
        return lax.ppermute(array, "seq", pairs)

    def by_core(self, own, other):
        return jnp.where(self.c == 0, jnp.stack([own, other]), jnp.stack([other, own]))

    def gather_z(self, array):
        return lax.all_gather(array, AXES, axis_index_groups=self.z_groups, tiled=True)

    def z_pairs(self, pairs):
        return [(2 * a + c, 2 * b + c) for a, b in pairs for c in range(2)]

    def own_apart(self, split, axis):
        shape = [1] * split.ndim
        shape[axis] = self.z_count
        own = (jnp.arange(self.z_count) == self.z).reshape(shape)
        sent = jnp.moveaxis(jnp.where(own, 0.0, split).astype(low), axis, 0)
        kept = lax.dynamic_index_in_dim(split, self.z, axis, False)
        return sent.reshape((-1,) + sent.shape[-1:]), kept.reshape((-1,) + sent.shape[-1:])

    def scatter_z(self, parts):
        total = lax.psum_scatter(
            parts[0], AXES, scatter_dimension=0, axis_index_groups=self.z_groups, tiled=True
        )
        return total, parts[1]


    def sum_far(self, chunk):
        if self.z_count != 4:
            return ()
        pairs = self.z_pairs([(0, 1), (3, 2)])
        return (lax.ppermute(chunk(3 - self.z).astype(low), "seq", pairs),)

    def sum_near(self, chunk):
        if self.z_count != 4:
            return ()
        below = self.to_z(chunk(jnp.minimum(self.z + 1, 3)).astype(low), 1)
        above = self.to_z(chunk(jnp.maximum(self.z - 1, 0)).astype(low), -1)
        return below, above

    def sum_second(self, chunk, far):
        if self.z_count != 4:
            return ()
        second = (chunk(self.z ^ 2).astype(wide) + far[0].astype(wide)).astype(low)
        return (lax.ppermute(second, "seq", self.z_pairs([(0, 2), (1, 3), (2, 0), (3, 1)])),)

    def sum_all(self, sent, kept, near, second):
        total = kept.astype(wide)
        if self.z_count != 4:
            whole = lax.psum_scatter(
                sent.reshape(-1, sent.shape[-1]),
                AXES,
                scatter_dimension=0,
                axis_index_groups=self.z_groups,
                tiled=True,
            )
            return total + whole.astype(wide)
        for part in near + second:
            total = total + part.astype(wide)
        return total

    def gather_seq_small(self, array):
        if self.s_count != 8:
            return lax.all_gather(array, "seq")
        out = array[None]
        for bit in range(3):
            got = lax.ppermute(out, "seq", [(i, i ^ (1 << bit)) for i in range(8)])
            low_bit = (self.s >> bit) % 2 == 0
            out = jnp.where(low_bit, jnp.concatenate([out, got]), jnp.concatenate([got, out]))
        return out

    def gather_dp_small(self, array):
        if not self.square:
            return lax.all_gather(array, "dp")
        out = array[None]
        for bit in range(2):
            got = self.to_k(out, 1 << bit)
            low_bit = (self.k >> bit) % 2 == 0
            out = jnp.where(low_bit, jnp.concatenate([out, got]), jnp.concatenate([got, out]))
        return out

    def gather_plane(self, array):
        if not self.square:
            whole = lax.all_gather(array, AXES, axis_index_groups=self.plane_groups)
            whole = whole.reshape((self.k_count, 2) + array.shape)
            return jnp.swapaxes(whole, 0, 1).reshape((-1,) + array.shape[1:])
        return self.gather_end(self.gather_far(self.gather_near(array)))

    def gather_near(self, array):
        if not self.square:
            return (array,)
        return array, self.to_k(array, 1), self.to_k(array, 2)

    def gather_far(self, near):
        if not self.square:
            return near
        array, from_x, from_y = near
        half = array.shape[0] // 2
        return array, from_x, from_y, self.to_k(from_x[:half], 2), self.to_k(from_y[half:], 1)

    def gather_end(self, mine):
        if not self.square:
            return self.gather_plane(mine[0])
        return lay_out(self.c, mine, [self.to_core(part) for part in mine])

    def gather_tail(self, tail):
        if not self.square:
            tail = jnp.swapaxes(self.gather_plane(tail[None]).reshape((2, -1) + tail.shape), 0, 1)
            return self.to_z(tail[:, 1].reshape((-1,) + tail.shape[3:]), 1)
        tail = self.to_z(tail, 1)
        tail = jnp.where(self.c == 1, tail, self.to_core(tail))
        tail = jnp.concatenate([tail, self.to_k(tail, 1)])
        return jnp.concatenate([tail, self.to_k(tail, 2)])

    def gather_plane_small(self, array):
        if not self.square:
            return self.gather_plane(array)
        near = jnp.stack([array, self.to_k(array, 1)])
        mine = jnp.concatenate([near, self.to_k(near, 2)])
        return self.by_core(mine, self.to_core(mine)).reshape((-1,) + array.shape[1:])

    def halves(self, array):
        count = array.shape[0] // 2
        own = lax.dynamic_slice_in_dim(array, self.c * count, count, 0)
        return own, lax.dynamic_slice_in_dim(array, (1 - self.c) * count, count, 0)

    def chip_product(self, left, right, dot, exact=False):
        own, other = self.halves(left)
        count = own.shape[0] // 2
        got = []
        for i in range(2):
            part = dot(other[i * count : (i + 1) * count], right)
            if exact:
                part = self.pack(part, self.power_of(part))
                got.append(self.unpack(self.to_core(part))[0])
            else:
                got.append(self.to_core(part.astype(low)).astype(wide))
        chip = []
        for i in range(2):
            part = dot(own[i * count : (i + 1) * count], right) + got[i]
            chip += list(part.reshape(self.k_count // 2, -1, part.shape[-1]))
        return chip

    def power_of(self, values):
        largest = jnp.max(jnp.abs(values), axis=-1, keepdims=True)
        return jnp.ceil(jnp.log2(jnp.clip(largest, 1e-30, 1e37)))

    def pack(self, parts, power):
        scaled = (parts * jnp.exp2(-power)).astype(jnp.float16)
        power = jnp.broadcast_to(power, power.shape[:-1] + (128,)).astype(jnp.float16)
        return jnp.concatenate([scaled, power], axis=-1)

    def unpack(self, got):
        got = got.astype(wide)
        width = got.shape[-1] - 128
        power = got[..., width : width + 1]
        return got[..., :width] * jnp.exp2(power), power

    def chip_parts(self, left, right, side, between=None):
        if not self.square:
            return self.chip_product(left, right, dot_nt if side else dot_nn), None
        count = left.shape[0] // 8
        other = other_call(self.c, left, right, count, side)
        got = self.to_core(other)
        extra = None
        if between is not None:
            left, extra = between(other, left)
        return own_call(self.c, left, right, got, count, side), extra

    def near_parts(self, parts):
        if not self.square:
            return self.near_plane(parts)
        chip, next_a, next_b, a, b = parts
        return (chip, next_a, next_b, *together(self.to_k(a, 1), self.to_k(b, 2)))

    def near_product(self, left, right, between=None):
        parts, extra = self.chip_parts(left, right, 1, between)
        return self.near_parts(parts), extra

    def far_product(self, near):
        if not self.square:
            return self.far_plane(near)
        chip, next_a, next_b, got_a, got_b = near
        half = next_a.shape[1]
        got_a, got_b = got_a.astype(wide), got_b.astype(wide)
        own_a, own_b = chip[:, :half] + got_a[0], chip[:, half:] + got_b[0]
        return self.last_plane(next_a + got_a[1], next_b + got_b[1], None, None, own_a, own_b)

    def near_plane(self, chip, exact=False):
        if not self.square:
            return (lax.psum_scatter(jnp.stack(chip), "dp", scatter_dimension=0, tiled=False),)
        half = chip[0].shape[1] // 2
        power = [self.power_of(part) for part in chip] if exact else None

        def pick(a, i, j):
            return a if a is None else jnp.stack([a[i], a[j]])

        got_a = self.send_plane(jnp.stack([chip[1][:, :half], chip[3][:, :half]]), pick(power, 1, 3), 1)
        got_b = self.send_plane(jnp.stack([chip[2][:, half:], chip[3][:, half:]]), pick(power, 2, 3), 2)
        got_a, got_b = together(got_a, got_b)
        return chip, power, got_a, got_b

    def send_plane(self, parts, power, flip):
        if power is None:
            return self.to_k(parts.astype(low), flip), None
        return self.unpack(self.to_k(self.pack(parts, power), flip))

    def far_plane(self, near):
        if not self.square:
            return near[0]
        chip, power, (got_a, power_a), (got_b, power_b) = near
        half = chip[0].shape[1] // 2
        got_a, got_b = got_a.astype(wide), got_b.astype(wide)

        def above(a, i, b, j):
            return a if a is None else jnp.maximum(a[i], b[j]) + 1.0

        next_a, next_b = chip[2][:, :half] + got_a[1], chip[1][:, half:] + got_b[1]
        return self.last_plane(
            next_a,
            next_b,
            above(power_a, 1, power, 2),
            above(power_b, 1, power, 1),
            chip[0][:, :half] + got_a[0],
            chip[0][:, half:] + got_b[0],
        )

    def last_plane(self, next_a, next_b, power_a, power_b, own_a, own_b):
        if power_a is None:
            next_a, next_b = together(next_a.astype(low), next_b.astype(low))
            last_a, last_b = self.to_k(next_a, 2).astype(wide), self.to_k(next_b, 1).astype(wide)
        else:
            next_a, next_b = together(self.pack(next_a, power_a), self.pack(next_b, power_b))
            last_a, last_b = self.unpack(self.to_k(next_a, 2))[0], self.unpack(self.to_k(next_b, 1))[0]
        return jnp.concatenate([own_a + last_a, own_b + last_b], axis=1)

    def sum_plane(self, chip, exact=False):
        return self.far_plane(self.near_plane(chip, exact))

    def exchange_plane(self, array):
        return self.exchange_dp(self.exchange_core(array))

    def exchange_core(self, array):
        keep = lax.dynamic_index_in_dim(array, self.c, 1, False)
        got = self.to_core(lax.dynamic_index_in_dim(array, 1 - self.c, 1, False))
        return jnp.moveaxis(self.by_core(keep, got), 0, 1)

    def exchange_dp(self, pairs):
        if not self.square:
            return lax.all_to_all(pairs, "dp", 0, 0, tiled=True)
        parts = [lax.dynamic_index_in_dim(pairs, self.k, 0, False)]
        for flip in range(1, 4):
            parts.append(self.to_k(lax.dynamic_index_in_dim(pairs, self.k ^ flip, 0, False), flip))
        odd = self.k % 2 == 1
        parts = [jnp.where(odd, parts[i ^ 1], parts[i]) for i in range(4)]
        upper = self.k >= 2
        return jnp.stack([jnp.where(upper, parts[i ^ 2], parts[i]) for i in range(4)])


def gelu_pair(x):
    slope = 0.7978845608028654
    inner = jnp.tanh(slope * (x + 0.044715 * x * x * x))
    half = 0.5 * (1.0 + inner)
    return x * half, half + 0.5 * x * (1.0 - inner * inner) * slope * (1.0 + 0.134145 * x * x)


def rms_normed(values, gain):
    values = values.astype(wide)
    scale = lax.rsqrt(jnp.mean(values * values, axis=1, keepdims=True) + eps_value)
    return (values * scale * gain).astype(low)


def ordered(values, order):
    if order is None:
        return values
    size = values.shape[1] // len(order)
    return jnp.concatenate([values[:, i * size : (i + 1) * size] for i in order], axis=1)


def minus_expm1(x):
    near = 1.0
    for i in range(8, 1, -1):
        near = 1.0 + near * x * (1.0 / i)
    return jnp.where(x > -0.5, -x * near, 1.0 - jnp.exp(x))


def gates_of(conv_low, w_gates, params, not_start):
    width = conv_low.shape[1]
    pre = jnp.dot(conv_low, w_gates, preferred_element_type=wide)
    rate = jax.nn.sigmoid(pre[:, :width] + params[5:6])
    igate = jax.nn.sigmoid(pre[:, width:] + params[6:7])
    log_keep = params[7:8] * rate
    room = minus_expm1(2.0 * log_keep)
    mult = jnp.where(not_start > 0.5, jnp.sqrt(jnp.maximum(room, floor_value)), 1.0)
    return rate, igate, jnp.exp(log_keep), room, mult


def put_lanes(ref, at, value):
    for j in range(ref.shape[0]):
        part = value[:, 128 * j : 128 * (j + 1)]
        ref[j, at, : part.shape[1]] = part


def get_lanes(ref, at, width):
    parts = [ref[j, at, : min(128, width - 128 * j)] for j in range(ref.shape[0])]
    return jnp.concatenate(parts, axis=1)


def lane_shape(tokens, width, kind=wide):
    return jax.ShapeDtypeStruct((pl.cdiv(width, 128), tokens, 128), kind)


def conv_kernel(
    rows, span, order, x_ref, w_ref, halo_ref, gain_ref, params_ref, gates_ref,
    normed_ref, masks_ref, branch_ref, in_ref, low_ref, keep_ref, drive_ref, sums_ref, before_ref, tail, line,
):
    step = pl.program_id(0)
    width = in_ref.shape[1]
    count = x_ref.shape[0]
    row_dev = count // span

    @pl.when(step == 0)
    def _():
        normed = rms_normed(halo_ref[...], gain_ref[...])
        before = jnp.dot(ordered(normed, order), w_ref[:, width:], preferred_element_type=wide)
        tail[...] = before.astype(low).astype(wide)
        before_ref[...] = tail[...]

    features = gain_ref.shape[1]
    normed = rms_normed(x_ref[:, :features], gain_ref[...])
    normed_ref[...] = normed
    masks_ref[...] = x_ref[:, features : features + 8].astype(wide)
    pre = jnp.dot(ordered(normed, order), w_ref[...], preferred_element_type=wide)
    branch_ref[...] = pre[:, :width]
    conv_in = pre[:, width:].astype(low)
    in_ref[...] = conv_in
    conv_in = conv_in.astype(wide)
    params = params_ref[...]
    for row in range(row_dev):
        at = slice(row * span, (row + 1) * span)
        own = conv_in[at]
        place = pl.ds(pl.multiple_of((lax.rem(step * row_dev + row, rows)) * 8, 8), 8)
        line[:8] = tail[place]
        line[8:] = own
        tail[place] = own[span - 8 :]
        masks = masks_ref[at]
        total = params[4:5] + params[0:1] * own
        for by in range(1, 4):
            total = total + params[by : by + 1] * line[8 - by : 8 - by + span] * masks[:, by - 1 : by]
        conv_low = total.astype(low)
        low_ref[at] = conv_low
        not_start = masks[:, 3:4]
        rate, igate, keep, room, mult = gates_of(conv_low, gates_ref[...], params, not_start)
        to = pl.ds(pl.multiple_of((step * row_dev + row) * span, 8), span)
        put_lanes(keep_ref, to, keep * not_start)
        put_lanes(drive_ref, to, mult * igate * conv_low.astype(wide))

    @pl.when(step == pl.num_programs(0) - 1)
    def _():
        lanes = keep_ref.shape[0]

        def one(i, state):
            out = []
            for j in range(lanes):
                keep = keep_ref.at[j][pl.ds(i, rows, stride=span), :]
                drive = drive_ref.at[j][pl.ds(i, rows, stride=span), :]
                out.append((state[j][0] * keep, state[j][1] * keep + drive))
            return tuple(out)

        shape = (rows, 128)
        state = tuple((jnp.ones(shape, wide), jnp.zeros(shape, wide)) for _ in range(lanes))
        for half in range(2):
            base = half * rows * span
            state = lax.fori_loop(0, span, lambda i, s, base=base: one(base + i, s), state, unroll=8)
        for j in range(lanes):
            sums_ref[0, j] = state[j][0]
            sums_ref[1, j] = state[j][1]


def state_kernel(rows, span, keep_ref, drive_ref, start_ref, branch_ref, state_ref, mixed_ref):
    lanes = keep_ref.shape[0]
    width = mixed_ref.shape[1]

    def one(i, state):
        out = []
        for j in range(lanes):
            at = pl.ds(i, rows, stride=span)
            value = state[j] * keep_ref.at[j][at, :] + drive_ref.at[j][at, :]
            state_ref.at[j][at, :] = value
            out.append(value)
        return tuple(out)

    state = tuple(start_ref[j] for j in range(lanes))
    for half in range(2):
        base = half * rows * span
        state = lax.fori_loop(0, span, lambda i, s, base=base: one(base + i, s), state, unroll=8)

    @pl.loop(0, 2 * rows)
    def _(block):
        at = pl.ds(pl.multiple_of(block * span, 16), span)
        value, _ = gelu_pair(branch_ref[at])
        mixed_ref[at] = (value * get_lanes(state_ref, at, width)).astype(low)


def mlp_kernel(x_ref, cot_ref, w_ref, down_ref, hidden_ref, grad_ref):
    width = hidden_ref.shape[1]
    pre = jnp.dot(x_ref[...], w_ref[...], preferred_element_type=wide)
    grad = lax.dot_general(
        cot_ref[...], down_ref[...], (((1,), (1,)), ((), ())), preferred_element_type=wide
    )
    up = pre[:, width:]
    value, slope = gelu_pair(pre[:, :width])
    hidden_ref[...] = (value * up).astype(low)
    grad_ref[:, :width] = (grad * up * slope).astype(low)
    grad_ref[:, width:] = (grad * value).astype(low)


def other_kernel(side, core_ref, x_ref, w_ref, out_ref):
    product = lax.dot_general(
        x_ref[...], w_ref[...], (((1,), (side,)), ((), ())), preferred_element_type=wide
    )
    out_ref[...] = product.astype(low)


def own_kernel(side, core_ref, x_ref, w_ref, got_ref, chip_ref, next_a_ref, next_b_ref, a_ref, b_ref):
    step = pl.program_id(0)
    product = lax.dot_general(
        x_ref[...], w_ref[...], (((1,), (side,)), ((), ())), preferred_element_type=wide
    )
    product = product + got_ref[...].astype(wide)
    half = product.shape[1] // 2

    @pl.when(step == 0)
    def _():
        chip_ref[...] = product

    @pl.when(step == 1)
    def _():
        next_b_ref[...] = product[:, half:]

    @pl.when(step == 2)
    def _():
        next_a_ref[...] = product[:, :half]

    @pl.when((step == 1) | (step == 3))
    def _():
        a_ref[0] = product[:, :half].astype(low)

    @pl.when(step >= 2)
    def _():
        b_ref[0] = product[:, half:].astype(low)


def back_kernel(
    rows, span, x_ref, w_ref, branch_ref, state_ref, keep_ref, grad_branch_ref, grad_state_ref, sum_ref
):
    step = pl.program_id(0)
    lanes, _, _ = keep_ref.shape
    width = w_ref.shape[0]
    count = x_ref.shape[0]
    mixed = lax.dot_general(
        x_ref[...], w_ref[...], (((1,), (1,)), ((), ())), preferred_element_type=wide
    )
    for row in range(count // span):
        at = slice(row * span, (row + 1) * span)
        to = pl.ds(pl.multiple_of(step * count + row * span, 8), span)
        value, slope = gelu_pair(branch_ref[at])
        state = get_lanes(state_ref, to, width)
        grad_branch_ref[at] = (mixed[at] * state * slope).astype(low)
        put_lanes(grad_state_ref, to, mixed[at] * value)

    @pl.when(step == pl.num_programs(0) - 1)
    def _():
        def one(i, state):
            out = []
            for j in range(lanes):
                at = pl.ds(i, rows, stride=span)
                out.append(keep_ref.at[j][at, :] * (grad_state_ref.at[j][at, :] + state[j]))
            return tuple(out)

        state = tuple(jnp.zeros((rows, 128), wide) for _ in range(lanes))
        for half in (1, 0):
            last = half * rows * span + span - 1
            state = lax.fori_loop(0, span, lambda i, s, last=last: one(last - i, s), state, unroll=8)
        for j in range(lanes):
            sum_ref[j] = state[j]


def adjoint_kernel(
    rows, span, keep_ref, grad_ref, carry_ref, state_ref, start_ref, low_ref, gates_ref, params_ref,
    masks_ref, in_ref, before_ref, grad_conv_ref, small_ref, adjoint, through, gates_grad_ref, sums_ref, line,
):
    lanes = keep_ref.shape[0]
    width = low_ref.shape[1]

    def one(i, state, before):
        out = []
        for j in range(lanes):
            at = pl.ds(i, rows, stride=span)
            value = grad_ref.at[j][at, :] + state[j]
            adjoint.at[j][at, :] = value
            through.at[j][at, :] = value * before(j)
            out.append(keep_ref.at[j][at, :] * value)
        return tuple(out)

    state = tuple(carry_ref[j] for j in range(lanes))
    for half in (1, 0):
        first = half * rows * span

        def inner(i, s, first=first):
            at = first + span - 1 - i
            return one(at, s, lambda j: state_ref.at[j][pl.ds(at - 1, rows, stride=span), :])

        state = lax.fori_loop(0, span - 1, inner, state, unroll=8)
        if half:
            state = one(first, state, lambda j: state_ref.at[j][pl.ds(span - 1, rows, stride=span), :])
        else:
            state = one(first, state, lambda j: start_ref[j])

    params = params_ref[...]
    gates_grad_ref[...] = jnp.zeros(gates_grad_ref.shape, wide)
    sums_ref[...] = jnp.zeros(sums_ref.shape, wide)

    @pl.loop(0, 2 * rows)
    def _(block):
        at = pl.ds(pl.multiple_of(block * span, 16), span)
        conv_low = low_ref[at]
        conv_value = conv_low.astype(wide)
        not_start = masks_ref[at][:, 3:4]
        rate, igate, keep, room, mult = gates_of(conv_low, gates_ref[...], params, not_start)
        adj = get_lanes(adjoint, at, width)
        thr = get_lanes(through, at, width)
        spread = jnp.where(room > floor_value, adj * igate * conv_value * keep * keep / mult, 0.0)
        grad_log = not_start * (thr * keep - spread)
        grad_rate = (grad_log * params[7:8] * rate * (1.0 - rate)).astype(low)
        scaled = adj * mult
        grad_igate = (scaled * conv_value * igate * (1.0 - igate)).astype(low)
        both = jnp.concatenate([grad_rate, grad_igate], axis=1)
        grad_conv = scaled * igate + lax.dot_general(
            both, gates_ref[...], (((1,), (1,)), ((), ())), preferred_element_type=wide
        )
        grad_conv = grad_conv.astype(low)
        grad_conv_ref[at] = grad_conv
        gates_grad_ref[...] += lax.dot_general(
            conv_low, both, (((0,), (0,)), ((), ())), preferred_element_type=wide
        )
        masks = masks_ref[at]
        grad_conv = grad_conv.astype(wide)
        conv_in = in_ref[at].astype(wide)
        within = lax.rem(block, rows)
        line[:8] = before_ref[pl.ds(pl.multiple_of(within * 8, 8), 8)]

        @pl.when(block >= rows)
        def _():
            last = pl.ds(pl.multiple_of(within * span + span - 16, 16), 16)
            line[:8] = in_ref[last].astype(wide)[8:]

        line[8:] = conv_in
        values = [grad_conv * conv_in]
        for by in range(1, 4):
            values.append(grad_conv * line[8 - by : 8 - by + span] * masks[:, by - 1 : by])
        values += [grad_conv, grad_rate.astype(wide), grad_igate.astype(wide), grad_log * rate * params[8:9]]
        for i, value in enumerate(values):
            sums_ref[i : i + 1] += jnp.sum(value, axis=0, keepdims=True)

    block = small_ref.shape[1] // 2 - 64
    for head in range(width // block):
        at = slice(head * block, (head + 1) * block)
        small_ref[at, :block] = gates_grad_ref[at, at].astype(low)
        then = slice(width + head * block, width + (head + 1) * block)
        small_ref[at, block : 2 * block] = gates_grad_ref[at, then].astype(low)
    small_ref[:, 2 * block :] = sums_ref[...].T[:width].astype(low)


def conv_back_kernel(rows, span, grad_ref, halo_ref, masks_ref, halo_masks_ref, params_ref, one_ref, line):
    params = params_ref[...]

    def work(block, grad_next, masks_next):
        at = pl.ds(pl.multiple_of(block * span, 16), span)
        own = grad_ref[at].astype(wide)
        total = params[0:1] * own
        masks = masks_ref[at]
        for by in range(1, 4):
            line[:span] = own * masks[:, by - 1 : by]
            line[span:] = grad_next * masks_next[:, by - 1 : by]
            total = total + params[by : by + 1] * line[by : by + span]
        one_ref[at] = total.astype(low)

    @pl.loop(0, rows)
    def _(block):
        then = pl.ds(pl.multiple_of((block + rows) * span, 16), 16)
        work(block, grad_ref[then].astype(wide)[:8], masks_ref[then][:8])

    @pl.loop(0, rows)
    def _(block):
        then = pl.ds(pl.multiple_of(block * 16, 16), 16)
        work(block + rows, halo_ref[then].astype(wide)[:8], halo_masks_ref[then][:8])


def whole_block(array):
    return pl.BlockSpec(array.shape, lambda *i, n=len(array.shape): (0,) * n)


def token_block(array, count):
    return pl.BlockSpec((count,) + array.shape[1:], lambda i, n=len(array.shape): (i,) + (0,) * (n - 1))


def half_of(core, x, count, width):
    return pl.BlockSpec((count, width), lambda k, core_ref: (core_ref[0] * (x.shape[0] // (2 * count)) + k, 0))


def half_call(kernel, core, x, w, count, extra, outputs):
    def spec(array, block, index):
        return pl.BlockSpec(block, lambda k, core_ref: index(k))

    return pl.pallas_call(
        kernel,
        out_shape=[array for array, _, _ in outputs],
        grid_spec=pltpu.PrefetchScalarGridSpec(
            num_scalar_prefetch=1,
            grid=(x.shape[0] // (2 * count),),
            in_specs=[
                half_of(core, x, count, x.shape[1]),
                pl.BlockSpec(w.shape, lambda k, core_ref: (0, 0)),
            ]
            + [spec(*one) for one in extra],
            out_specs=[spec(*one) for one in outputs],
        ),
        cost_estimate=pl.CostEstimate(flops=0, bytes_accessed=0, transcendentals=0),
        compiler_params=pltpu.CompilerParams(vmem_limit_bytes=56 * 2**20),
    )(core.reshape(1).astype(jnp.int32), x, w, *[array for array, _, _ in extra])


def other_call(core, x, w, count, side):
    width = w.shape[1 - side]
    out = jax.ShapeDtypeStruct((x.shape[0] // 2, width), low)
    kernel = functools.partial(other_kernel, side)
    return half_call(kernel, 1 - core, x, w, count, [], [(out, (count, width), lambda k: (k, 0))])[0]


def own_call(core, x, w, got, count, side):
    width = w.shape[1 - side]
    a = jax.ShapeDtypeStruct((2, count, width // 2), low)
    chip = jax.ShapeDtypeStruct((count, width), wide)
    after = jax.ShapeDtypeStruct((count, width // 2), wide)
    return half_call(
        functools.partial(own_kernel, side),
        core,
        x,
        w,
        count,
        [(got, (count, width), lambda k: (k, 0))],
        [
            (chip, chip.shape, lambda k: (0, 0)),
            (after, after.shape, lambda k: (0, 0)),
            (after, after.shape, lambda k: (0, 0)),
            (a, (1, count, width // 2), lambda k: (k // 2, 0, 0)),
            (a, (1, count, width // 2), lambda k: (k // 3, 0, 0)),
        ],
    )


def rows_kernel(turned, core_ref, x_ref, grad_ref, sent_ref, kept_ref):
    count = kept_ref.shape[1]
    total = lax.dot_general(
        x_ref[...], grad_ref[...], (((int(turned),), (0,)), ((), ())), preferred_element_type=wide
    )
    planes = sent_ref.shape[0]
    first = lax.rem(pl.program_id(0), core_ref[1]) * planes
    for i in range(planes):
        part = total[i * count : (i + 1) * count]
        mine = first + i == core_ref[0]
        sent_ref[i, 0] = jnp.where(mine, jnp.zeros_like(part), part).astype(low)

        @pl.when(mine)
        def _(part=part):
            kept_ref[0] = part


def rows_call(z, z_count, k_count, x, grad, turned):
    tokens, features = x.shape[::-1] if turned else x.shape
    count = features // (z_count * k_count)
    planes = max(2, 128 // count)
    width = grad.shape[1]
    per = z_count // planes
    sent = jax.ShapeDtypeStruct((z_count, k_count, count, width), low)
    kept = jax.ShapeDtypeStruct((k_count, count, width), wide)
    block = (planes * count, tokens) if turned else (tokens, planes * count)
    return pl.pallas_call(
        functools.partial(rows_kernel, turned),
        out_shape=[sent, kept],
        grid_spec=pltpu.PrefetchScalarGridSpec(
            num_scalar_prefetch=1,
            grid=(k_count * per,),
            in_specs=[
                pl.BlockSpec(block, lambda i, ref: (i, 0) if turned else (0, i)),
                pl.BlockSpec(grad.shape, lambda i, ref: (0, 0)),
            ],
            out_specs=[
                pl.BlockSpec((planes, 1, count, width), lambda i, ref: (i % per, i // per, 0, 0)),
                pl.BlockSpec((1, count, width), lambda i, ref: (i // per, 0, 0)),
            ],
        ),
        cost_estimate=pl.CostEstimate(flops=0, bytes_accessed=0, transcendentals=0),
        compiler_params=pltpu.CompilerParams(vmem_limit_bytes=56 * 2**20),
    )(jnp.stack([z, jnp.int32(per)]).astype(jnp.int32), x, grad)


def turn_kernel(x_ref, out_ref):
    out_ref[...] = x_ref[...].T


def turn(x):
    block = 256
    return pl.pallas_call(
        turn_kernel,
        out_shape=jax.ShapeDtypeStruct(x.shape[::-1], x.dtype),
        grid=(x.shape[1] // block,),
        in_specs=[pl.BlockSpec((x.shape[0], block), lambda i: (0, i))],
        out_specs=pl.BlockSpec((block, x.shape[0]), lambda i: (i, 0)),
        cost_estimate=pl.CostEstimate(flops=0, bytes_accessed=0, transcendentals=0),
        compiler_params=pltpu.CompilerParams(vmem_limit_bytes=48 * 2**20),
    )(x)


def down_kernel(core_ref, hidden_ref, cot_ref, sent_ref, kept_ref):
    total = lax.dot_general(
        cot_ref[...], hidden_ref[...], (((0,), (0,)), ((), ())), preferred_element_type=wide
    )
    total = total.T
    count = kept_ref.shape[0]
    for i in range(sent_ref.shape[0]):
        part = total[i * count : (i + 1) * count]
        mine = core_ref[0] == i
        sent_ref[i] = jnp.where(mine, jnp.zeros_like(part), part).astype(low)

        @pl.when(mine)
        def _(part=part):
            kept_ref[...] = part


def down_call(z, z_count, hidden, cot):
    tokens, features = cot.shape
    count = hidden.shape[1] // z_count
    columns = 256
    sent = jax.ShapeDtypeStruct((z_count, count, features), low)
    kept = jax.ShapeDtypeStruct((count, features), wide)
    return pl.pallas_call(
        down_kernel,
        out_shape=[sent, kept],
        grid_spec=pltpu.PrefetchScalarGridSpec(
            num_scalar_prefetch=1,
            grid=(features // columns,),
            in_specs=[
                pl.BlockSpec(hidden.shape, lambda i, ref: (0, 0)),
                pl.BlockSpec((tokens, columns), lambda i, ref: (0, i)),
            ],
            out_specs=[
                pl.BlockSpec((z_count, count, columns), lambda i, ref: (0, 0, i)),
                pl.BlockSpec((count, columns), lambda i, ref: (0, i)),
            ],
        ),
        cost_estimate=pl.CostEstimate(flops=0, bytes_accessed=0, transcendentals=0),
        compiler_params=pltpu.CompilerParams(vmem_limit_bytes=56 * 2**20),
    )(z.reshape(1).astype(jnp.int32), hidden, cot)


def kernel_call(kernel, steps, inputs, outputs, scratch=()):
    def spec(array, count):
        return whole_block(array) if count is None else token_block(array, count)

    return pl.pallas_call(
        kernel,
        out_shape=[array for array, _ in outputs],
        grid=(steps,),
        in_specs=[spec(array, count) for array, count in inputs],
        out_specs=[spec(array, count) for array, count in outputs],
        scratch_shapes=scratch,
        cost_estimate=pl.CostEstimate(flops=0, bytes_accessed=0, transcendentals=0),
        compiler_params=pltpu.CompilerParams(vmem_limit_bytes=56 * 2**20),
    )(*[array for array, _ in inputs])


def per_device(
    tokens,
    segment_ids,
    cotangent,
    norm_one,
    branch_weight,
    input_proj,
    conv_weight,
    conv_bias,
    rate_weight,
    igate_weight,
    rate_bias,
    igate_bias,
    decay_param,
    out_proj,
    norm_two,
    mlp_gate,
    mlp_up,
    mlp_down,
):
    at = Place()
    k_count, z_count = at.k_count, at.z_count
    group = 2 * k_count
    row_dev, span, width_d = tokens.shape
    tok = row_dev * span
    rows = k_count * row_dev
    tok_all = 2 * rows * span
    d_own = norm_one.shape[0]
    w_own = conv_bias.shape[0]
    f_own = mlp_down.shape[0]
    width_r = branch_weight.shape[1]
    w_slot = width_r // group
    f_slot = f_own * z_count
    taps = conv_weight.shape[0]
    reach = taps - 1
    half_z = z_count // 2

    def by_feature(array):
        split = array.reshape(z_count, -1, 2 * d_own, array.shape[1])
        return jnp.swapaxes(split, 0, 1).reshape(array.shape)

    small = jnp.concatenate(
        [
            norm_one,
            norm_two,
            conv_weight.reshape(-1),
            conv_bias,
            rate_bias,
            igate_bias,
            decay_param,
        ]
    )
    rec_cols = jnp.concatenate(
        [
            branch_weight.reshape(d_own, k_count, 2, w_slot),
            input_proj.reshape(d_own, k_count, 2, w_slot),
        ],
        axis=3,
    )
    rec_cols = at.exchange_plane(jnp.moveaxis(rec_cols, 0, 2))
    out_part = at.gather_z(out_proj)
    rec_cols, out_part = together(rec_cols, out_part)
    w1 = at.gather_z(rec_cols.reshape(group * d_own, 2 * w_slot))

    gate_rows = jnp.concatenate([rate_weight, igate_weight], axis=1)
    small = jnp.pad(small, (0, -small.shape[0] % (2 * BS))).reshape(-1, 2 * BS)
    gate_rows = at.gather_seq_small(jnp.concatenate([gate_rows, small]))
    small = gate_rows[:, w_own:].reshape(at.s_count, -1)
    gains = at.gather_dp_small(small[:, : 2 * d_own]).reshape(k_count * at.s_count, -1)
    gain_one = gains[:, :d_own].reshape(1, width_d).astype(wide)
    gain_two = gains[:, d_own:].reshape(1, width_d).astype(wide)
    mine = lax.dynamic_slice_in_dim(small[:, 2 * d_own :], at.c * z_count, z_count, 0)
    mine = mine[:, : (taps + 4) * w_own].reshape(z_count, taps + 4, w_own).astype(wide)
    mine = jnp.swapaxes(mine, 0, 1).reshape(taps + 4, w_slot)
    w_conv = mine[:taps]
    b_conv, b_rate, b_igate, decay = (mine[taps + i][None, :] for i in range(4))
    log_slope = -rate_scale * jax.nn.softplus(-decay)
    decay_slope = rate_scale * jax.nn.sigmoid(-decay)
    params = jnp.concatenate([w_conv, b_conv, b_rate, b_igate, log_slope] + [decay_slope] * 8)
    gate_rows = lax.dynamic_slice_in_dim(gate_rows[:, :w_own], at.c * z_count, z_count, 0)
    gate_rows = gate_rows.reshape(w_slot, 2 * BS)
    heads = w_slot // BS

    def block_diagonal(columns):
        blocks = columns.reshape(heads, BS, 1, BS)
        same = jnp.eye(heads, dtype=low).reshape(heads, 1, heads, 1)
        return (blocks * same).reshape(w_slot, w_slot)

    w_gates = jnp.concatenate([block_diagonal(gate_rows[:, :BS]), block_diagonal(gate_rows[:, BS:])], axis=1)

    seg_code = (segment_ids % 64).astype(low)
    pairs = [(i, i + 1) for i in range(at.s_count - 1)]
    ext_code = jnp.concatenate([lax.ppermute(seg_code[:, span - reach :], "seq", pairs), seg_code], axis=1)
    position = lax.broadcasted_iota(jnp.int32, (row_dev, span), 1)
    masks = [
        (ext_code[:, reach - by : reach - by + span] == seg_code) & ((at.s > 0) | (position >= by))
        for by in range(1, taps)
    ]
    masks = jnp.stack(masks + [masks[0]] * (9 - taps), axis=-1).astype(low).reshape(tok, 8)
    tokens = tokens.reshape(tok, width_d)
    beside = jnp.concatenate([tokens, jnp.pad(masks, ((0, 0), (0, 120)))], axis=1)
    tail = tokens.reshape(row_dev, span, width_d)[:, span - 8 :].reshape(row_dev * 8, width_d)
    tail = at.gather_tail(tail)
    beside, tail, params, gate_rows, gain_one, gain_two, mlp_gate = together(
        beside, tail, params, gate_rows, gain_one, gain_two, mlp_gate
    )
    order = None
    if 2 * d_own % 128 == 0:
        order = [k * z_count + z for z in range(z_count) for k in range(k_count)]
    beside_near = at.gather_near(beside)
    inputs = tokens.astype(wide)
    s1 = lax.rsqrt(jnp.mean(inputs * inputs, axis=-1, keepdims=True) + eps_value)
    mlp_shape = jax.ShapeDtypeStruct((k_count, 2, d_own, 2 * f_slot), low)
    cut = functools.partial(cut_kernel, k_count, z_count)
    mlp_pairs = at.exchange_core(in_vmem(cut, (mlp_gate, mlp_up), mlp_shape))
    beside_near, mlp_pairs, w_gates = together(beside_near, mlp_pairs, w_gates)
    beside_far = at.gather_far(beside_near)
    mlp_cols = at.exchange_dp(mlp_pairs)
    cot = cotangent.reshape(tok, width_d)
    tokens_all, mlp_cols, cot = together(at.gather_end(beside_far), mlp_cols, cot)
    shape = jax.ShapeDtypeStruct

    half_rows = group * d_own // 2
    w2_parts = [
        at.gather_z(part.reshape(half_rows, 2 * f_slot))
        for part in (mlp_cols[: k_count // 2], mlp_cols[k_count // 2 :])
    ]

    steps = tok_all // tok
    cot_near = at.gather_near(cot)
    flat32, flat16 = shape((tok_all, w_slot), wide), shape((tok_all, w_slot), low)
    lanes = lane_shape(tok_all, w_slot)
    ends = shape((lanes.shape[0], rows, 128), wide)
    n1_all, masks, branch_pre, conv_in, conv_low, keep_eff, drive, summary, conv_before = kernel_call(
        functools.partial(conv_kernel, rows, span, order),
        steps,
        [(tokens_all, tok), (w1 if order else by_feature(w1), None), (tail, None), (gain_one, None), (params, None), (w_gates, None)],
        [(shape((tok_all, width_d), low), tok), (shape((tok_all, 8), wide), tok), (flat32, tok), (flat16, tok), (flat16, tok), (lanes, None), (lanes, None), (shape((2,) + ends.shape, wide), None), (shape((rows * 8, w_slot), wide), None)],
        [pltpu.VMEM((rows * 8, w_slot), wide), pltpu.VMEM((span + 8, w_slot), wide)],
    )
    w_down = at.gather_z(mlp_down)
    summary, cot_near, out_part, w1 = together(summary, cot_near, out_part, w1)
    w1 = by_feature(w1)
    out_part = out_part.reshape(2, half_z * w_own, width_d)
    out_keep = lax.dynamic_index_in_dim(out_part, at.c, 0, False)
    out_got = at.to_core(lax.dynamic_index_in_dim(out_part, 1 - at.c, 0, False))
    w_out = at.by_core(
        out_keep.reshape(half_z, w_own, width_d), out_got.reshape(half_z, w_own, width_d)
    )
    w_out = jnp.swapaxes(w_out, 0, 1).reshape(w_slot, width_d)
    cot_far = at.gather_far(cot_near)
    before = [at.to_z(summary, by) for by in range(1, z_count)]
    state_in = jnp.zeros(ends.shape, wide)
    for part in reversed(before):
        state_in = part[1] + part[0] * state_in
    state, mixed = kernel_call(
        functools.partial(state_kernel, rows, span),
        1,
        [(keep_eff, None), (drive, None), (state_in, None), (branch_pre, None)],
        [(lanes, None), (flat16, None)],
    )
    masks_after = at.to_z(masks.reshape(2, rows, span, 8)[0, :, :16], -1).reshape(rows * 16, 8)
    mixed, cot_far, w2_parts[0], masks_after = together(mixed, cot_far, w2_parts[0], masks_after)

    chip_one = at.chip_product(mixed, w_out, dot_nn, exact=True)
    near_sum, cot_far = together(at.near_plane(chip_one, exact=True), cot_far)
    n1_turned = turn(n1_all)
    cot_all = at.gather_end(cot_far)
    resid, cot_all, n1_turned = together(inputs + at.far_plane(near_sum), cot_all, n1_turned)
    resid, w2_parts[1] = together(resid, w2_parts[1])
    w2 = jnp.concatenate([by_feature(part) for part in w2_parts])

    s2 = lax.rsqrt(jnp.mean(resid * resid, axis=-1, keepdims=True) + eps_value)
    normed_two = (resid * s2 * gain_two).astype(low)
    n2_near, w2 = together(at.gather_near(normed_two), w2)
    n2_all, w_down = together(at.gather_end(at.gather_far(n2_near)), w_down)
    hidden, grad_two = kernel_call(
        mlp_kernel,
        steps,
        [(n2_all, tok), (cot_all, tok), (w2, None), (w_down, None)],
        [(shape((tok_all, f_slot), low), tok), (shape((tok_all, 2 * f_slot), low), tok)],
    )
    def rows_apart(x, grad, turned=False):
        sent, kept = rows_call(at.z, z_count, k_count, x, grad, turned)
        return sent.reshape(-1, sent.shape[-1]), kept.reshape(-1, kept.shape[-1])

    near_two, _ = at.near_product(grad_two, w2)
    chip_two, grad_two = together(near_two[0], grad_two)
    w2_part = rows_apart(n2_all, grad_two)
    near_two, w2_part, hidden = together(near_two, w2_part, hidden)
    w2_sum = at.scatter_z(w2_part)
    grad_n2 = at.far_product(near_two)
    down_sent, down_kept = down_call(at.z, z_count, hidden, cot_all)
    down_part = down_sent.reshape(-1, width_d), down_kept
    grad_n2, down_part = together(grad_n2, down_part)
    down_sum = at.scatter_z(down_part)
    scaled_two = gain_two * grad_n2
    cot_f = cot.astype(wide)
    mean_two = jnp.mean(scaled_two * resid, axis=-1, keepdims=True)
    grad_resid = cot_f + s2 * scaled_two - resid * (s2 * s2 * s2) * mean_two
    grad_recur = grad_resid.astype(low)
    grad_recur, hidden = together(grad_recur, hidden)
    chip_three, _ = at.chip_parts(hidden, w_down, 0)
    gr_near, chip_three = together(at.gather_near(grad_recur), chip_three)
    gr_all = at.gather_end(at.gather_far(gr_near))

    def summed(pair):
        return pair[0].astype(wide) + pair[1].astype(wide)

    def to_owner(array, columns):
        return at.exchange_plane(array.reshape(k_count, 2, d_own, columns))


    grad_branch, grad_state, back = kernel_call(
        functools.partial(back_kernel, rows, span),
        steps,
        [(gr_all, tok), (w_out, None), (branch_pre, tok), (state, None), (keep_eff, None)],
        [(flat16, tok), (lanes, None), (ends, None)],
    )
    back, mixed, chip_three, w2_sum = together(back, mixed, chip_three, w2_sum)

    def by_owner(array):
        split = array.reshape(half_z, 2, w_own, -1)
        keep = lax.dynamic_index_in_dim(split, at.c, 1, False)
        got = at.to_core(lax.dynamic_index_in_dim(split, 1 - at.c, 1, False))
        return at.by_core(keep, got).reshape(z_count, w_own, -1)

    own = jnp.stack([summary[0], back])
    after = [at.to_z(own, -by) for by in range(1, z_count)]
    grad_out = dot_tn(mixed, gr_all)
    after, grad_out = together(after, grad_out)
    carry_in = jnp.zeros(ends.shape, wide)
    for part in reversed(after):
        carry_in = part[1] + part[0] * carry_in
    near_three = at.near_parts(chip_three)
    mlp_pairs = at.exchange_core(summed(w2_sum).reshape(k_count, 2, d_own, 2 * f_slot))
    carry_in, mlp_pairs, near_three = together(carry_in, mlp_pairs, near_three)
    mlp_back = at.exchange_dp(mlp_pairs)
    grad_conv, rec_small = kernel_call(
        functools.partial(adjoint_kernel, rows, span),
        1,
        [
            (array, None)
            for array in (keep_eff, grad_state, carry_in, state, state_in, conv_low, w_gates, params, masks, conv_in, conv_before)
        ],
        [(flat16, None), (shape((w_slot, 2 * BS + 128), low), None)],
        [
            pltpu.VMEM(lanes.shape, wide),
            pltpu.VMEM(lanes.shape, wide),
            pltpu.VMEM((w_slot, 2 * w_slot), wide),
            pltpu.VMEM((128, w_slot), wide),
            pltpu.VMEM((span + 8, w_slot), wide),
        ],
    )
    grad_conv, near_three, mlp_back, down_sum = together(grad_conv, near_three, mlp_back, down_sum)
    block_out = (resid + at.far_product(near_three)).astype(low)
    head = at.to_z(grad_conv.reshape(2, rows, span, w_slot)[0, :, :16], -1).reshape(rows * 16, w_slot)
    rec_part = at.own_apart(by_owner(jnp.concatenate([grad_out.astype(low), rec_small], axis=1)), 0)
    head, rec_part = together(head, rec_part)
    rec_sum = at.scatter_z(rec_part)
    (grad_conv_in,) = kernel_call(
        functools.partial(conv_back_kernel, rows, span),
        1,
        [(array, None) for array in (grad_conv, head, masks, masks_after, params)],
        [(flat16, None)],
        [pltpu.VMEM((span + 8, w_slot), wide)],
    )
    grad_one = jnp.concatenate([grad_branch, grad_conv_in], axis=1)

    def product_between(other, left):
        other, then = together(other, left)
        parts = rows_apart(n1_turned, then, True)
        return together(left, parts)

    near_one, w1_part = at.near_product(grad_one, w1, product_between)
    if w1_part is None:
        w1_part = rows_apart(n1_turned, grad_one, True)
    w1_sum = at.scatter_z(w1_part)
    grad_n1 = at.far_product(near_one)
    w1_sum, grad_n1, block_out, rec_sum = together(w1_sum, grad_n1, block_out, rec_sum)
    rec_back = at.exchange_plane(summed(w1_sum).reshape(k_count, 2, d_own, 2 * w_slot))
    scaled_one = gain_one * grad_n1
    mean_one = jnp.mean(scaled_one * inputs, axis=-1, keepdims=True)
    grad_tokens = grad_resid + s1 * scaled_one - inputs * (s1 * s1 * s1) * mean_one
    grad_tokens = grad_tokens.reshape(row_dev, span, width_d)
    block_out = block_out.reshape(row_dev, span, width_d)

    rec_rows = summed(rec_sum)
    grad_out_w = rec_rows[:, :width_d]
    grad_rate_w = rec_rows[:, width_d : width_d + BS]
    grad_igate_w = rec_rows[:, width_d + BS : width_d + 2 * BS]
    grad_small = rec_rows[:, width_d + 2 * BS : width_d + 2 * BS + taps + 4].T
    grad_down = summed(down_sum)
    mlp_whole = jax.ShapeDtypeStruct(mlp_gate.shape, wide)
    join = functools.partial(join_kernel, k_count, z_count)
    grad_gate_w, grad_up_w = in_vmem(join, (mlp_back,), (mlp_whole, mlp_whole))
    rec_back = jnp.moveaxis(rec_back, 2, 0)
    grad_branch_w = rec_back[..., :w_slot].reshape(d_own, width_r)
    grad_input_w = rec_back[..., w_slot:].reshape(d_own, width_r)

    def gain_grad(pairs, gain):
        total = sum(jnp.sum(weight.astype(wide) * grad, axis=1) for weight, grad in pairs)
        return total / gain.astype(wide)

    grad_norm_one = gain_grad(((branch_weight, grad_branch_w), (input_proj, grad_input_w)), norm_one)
    grad_norm_two = gain_grad(((mlp_gate, grad_gate_w), (mlp_up, grad_up_w)), norm_two)
    return (
        block_out,
        grad_tokens,
        grad_norm_one,
        grad_branch_w,
        grad_input_w,
        grad_small[:taps],
        grad_small[taps],
        grad_rate_w,
        grad_igate_w,
        grad_small[taps + 1],
        grad_small[taps + 2],
        grad_small[taps + 3],
        grad_out_w,
        grad_norm_two,
        grad_gate_w,
        grad_up_w,
        grad_down,
    )


def solution(mesh):
    rows, matrix = P(AXES), P(AXES, None)
    tokens = P("dp", "seq", None)
    return jax.shard_map(
        per_device,
        mesh=mesh,
        in_specs=(
            tokens,
            P("dp", "seq"),
            tokens,
            rows,
            matrix,
            matrix,
            P(None, AXES),
            rows,
            matrix,
            matrix,
            rows,
            rows,
            rows,
            matrix,
            rows,
            matrix,
            matrix,
            matrix,
        ),
        out_specs=(
            tokens,
            tokens,
            rows,
            matrix,
            matrix,
            P(None, AXES),
            rows,
            matrix,
            matrix,
            rows,
            rows,
            rows,
            matrix,
            rows,
            matrix,
            matrix,
            matrix,
        ),
        check_vma=False,
    )
```

```python
import functools

import jax
import jax.numpy as jnp
from jax import lax
from jax.experimental import pallas as pl
from jax.experimental.pallas import tpu as pltpu
from jax.sharding import PartitionSpec as P

HEADS = 16
BS = 160
AXES = ("dp", "seq")

eps_value = 1e-06
rate_scale = 8.0
floor_value = 0.001
low = jnp.bfloat16
wide = jnp.float32


def gelu_tanh(value):
    return jax.nn.gelu(value, approximate=True)


def dot_nn(left, right):
    return lax.dot_general(left, right, (((1,), (0,)), ((), ())), preferred_element_type=wide)


def dot_nt(left, right):
    return lax.dot_general(left, right, (((1,), (1,)), ((), ())), preferred_element_type=wide)


def dot_tn(left, right):
    return lax.dot_general(left, right, (((0,), (0,)), ((), ())), preferred_element_type=wide)


def lay_out_kernel(count, c_ref, *refs):
    parts, (out_ref, buffer, sem, out_sem) = refs[: 2 * count], refs[2 * count :]
    core = c_ref[0]
    copies = []
    for which in range(2):
        start = (core if which == 0 else 1 - core) * (out_ref.shape[0] // 2)
        for i, part in enumerate(parts[which * count : (which + 1) * count]):
            at = pl.ds(pl.multiple_of(start, 16), part.shape[0])
            j = which * count + i
            into = pltpu.make_async_copy(part, buffer.at[at], sem.at[j])
            into.start()
            copies.append((into, pltpu.make_async_copy(buffer.at[at], out_ref.at[at], out_sem.at[j])))
            start = start + part.shape[0]
    for into, out in copies:
        into.wait()
        out.start()
    for into, out in copies:
        out.wait()


def lay_out(core, own, other):
    rows = 2 * sum(part.shape[0] for part in own)
    shape = (rows,) + own[0].shape[1:]
    anywhere = pl.BlockSpec(memory_space=pl.ANY)
    return pl.pallas_call(
        functools.partial(lay_out_kernel, len(own)),
        out_shape=jax.ShapeDtypeStruct(shape, own[0].dtype),
        in_specs=[pl.BlockSpec(memory_space=pltpu.SMEM)] + [anywhere] * (2 * len(own)),
        out_specs=anywhere,
        scratch_shapes=[
            pltpu.VMEM(shape, own[0].dtype),
            pltpu.SemaphoreType.DMA((2 * len(own),)),
            pltpu.SemaphoreType.DMA((2 * len(own),)),
        ],
        compiler_params=pltpu.CompilerParams(vmem_limit_bytes=32 * 2**20),
    )(core.reshape(1).astype(jnp.int32), *own, *other)


def together(*arrays):
    return lax.optimization_barrier(arrays)


def cut_kernel(k_count, z_count, gate_ref, up_ref, out_ref):
    own = out_ref.shape[3] // (2 * z_count)
    for k in range(k_count):
        for c in range(2):
            for which, ref in enumerate((gate_ref, up_ref)):
                for z in range(z_count):
                    at = ((k * z_count + z) * 2 + c) * own
                    to = (which * z_count + z) * own
                    out_ref[k, c, :, to : to + own] = ref[:, at : at + own]


def join_kernel(k_count, z_count, in_ref, gate_ref, up_ref):
    own = in_ref.shape[3] // (2 * z_count)
    for k in range(k_count):
        for c in range(2):
            for which, ref in enumerate((gate_ref, up_ref)):
                for z in range(z_count):
                    to = ((k * z_count + z) * 2 + c) * own
                    at = (which * z_count + z) * own
                    ref[:, to : to + own] = in_ref[k, c, :, at : at + own].astype(ref.dtype)


def in_vmem(kernel, arrays, out_shape):
    vmem = pl.BlockSpec(memory_space=pltpu.VMEM)
    return pl.pallas_call(
        kernel,
        out_shape=out_shape,
        in_specs=[vmem] * len(arrays),
        out_specs=jax.tree.map(lambda _: vmem, out_shape),
        compiler_params=pltpu.CompilerParams(vmem_limit_bytes=48 * 2**20),
    )(*arrays)


class Place:
    def __init__(self):
        self.k_count = lax.axis_size("dp")
        self.s_count = lax.axis_size("seq")
        self.z_count = self.s_count // 2
        self.k = lax.axis_index("dp")
        self.s = lax.axis_index("seq")
        self.c = self.s % 2
        self.z = self.s // 2
        self.square = self.k_count == 4
        self.z_groups = [
            [k * self.s_count + 2 * z + c for z in range(self.z_count)]
            for k in range(self.k_count)
            for c in range(2)
        ]
        self.plane_groups = [
            [k * self.s_count + 2 * z + c for k in range(self.k_count) for c in range(2)]
            for z in range(self.z_count)
        ]

    def to_k(self, array, flip):
        return lax.ppermute(array, "dp", [(i, i ^ flip) for i in range(self.k_count)])

    def to_core(self, array):
        return lax.ppermute(array, "seq", [(i, i ^ 1) for i in range(self.s_count)])

    def to_z(self, array, by):
        pairs = [(i, i + 2 * by) for i in range(self.s_count) if 0 <= i + 2 * by < self.s_count]
        return lax.ppermute(array, "seq", pairs)

    def by_core(self, own, other):
        return jnp.where(self.c == 0, jnp.stack([own, other]), jnp.stack([other, own]))

    def gather_z(self, array):
        return lax.all_gather(array, AXES, axis_index_groups=self.z_groups, tiled=True)

    def z_pairs(self, pairs):
        return [(2 * a + c, 2 * b + c) for a, b in pairs for c in range(2)]

    def own_apart(self, split, axis):
        shape = [1] * split.ndim
        shape[axis] = self.z_count
        own = (jnp.arange(self.z_count) == self.z).reshape(shape)
        sent = jnp.moveaxis(jnp.where(own, 0.0, split).astype(low), axis, 0)
        kept = lax.dynamic_index_in_dim(split, self.z, axis, False)
        return sent.reshape((-1,) + sent.shape[-1:]), kept.reshape((-1,) + sent.shape[-1:])

    def scatter_z(self, parts):
        total = lax.psum_scatter(
            parts[0], AXES, scatter_dimension=0, axis_index_groups=self.z_groups, tiled=True
        )
        return total, parts[1]


    def sum_far(self, chunk):
        if self.z_count != 4:
            return ()
        pairs = self.z_pairs([(0, 1), (3, 2)])
        return (lax.ppermute(chunk(3 - self.z).astype(low), "seq", pairs),)

    def sum_near(self, chunk):
        if self.z_count != 4:
            return ()
        below = self.to_z(chunk(jnp.minimum(self.z + 1, 3)).astype(low), 1)
        above = self.to_z(chunk(jnp.maximum(self.z - 1, 0)).astype(low), -1)
        return below, above

    def sum_second(self, chunk, far):
        if self.z_count != 4:
            return ()
        second = (chunk(self.z ^ 2).astype(wide) + far[0].astype(wide)).astype(low)
        return (lax.ppermute(second, "seq", self.z_pairs([(0, 2), (1, 3), (2, 0), (3, 1)])),)

    def sum_all(self, sent, kept, near, second):
        total = kept.astype(wide)
        if self.z_count != 4:
            whole = lax.psum_scatter(
                sent.reshape(-1, sent.shape[-1]),
                AXES,
                scatter_dimension=0,
                axis_index_groups=self.z_groups,
                tiled=True,
            )
            return total + whole.astype(wide)
        for part in near + second:
            total = total + part.astype(wide)
        return total

    def gather_seq_small(self, array):
        if self.s_count != 8:
            return lax.all_gather(array, "seq")
        out = array[None]
        for bit in range(3):
            got = lax.ppermute(out, "seq", [(i, i ^ (1 << bit)) for i in range(8)])
            low_bit = (self.s >> bit) % 2 == 0
            out = jnp.where(low_bit, jnp.concatenate([out, got]), jnp.concatenate([got, out]))
        return out

    def gather_dp_small(self, array):
        if not self.square:
            return lax.all_gather(array, "dp")
        out = array[None]
        for bit in range(2):
            got = self.to_k(out, 1 << bit)
            low_bit = (self.k >> bit) % 2 == 0
            out = jnp.where(low_bit, jnp.concatenate([out, got]), jnp.concatenate([got, out]))
        return out

    def gather_plane(self, array):
        if not self.square:
            whole = lax.all_gather(array, AXES, axis_index_groups=self.plane_groups)
            whole = whole.reshape((self.k_count, 2) + array.shape)
            return jnp.swapaxes(whole, 0, 1).reshape((-1,) + array.shape[1:])
        return self.gather_end(self.gather_far(self.gather_near(array)))

    def gather_near(self, array):
        if not self.square:
            return (array,)
        return array, self.to_k(array, 1), self.to_k(array, 2)

    def gather_far(self, near):
        if not self.square:
            return near
        array, from_x, from_y = near
        half = array.shape[0] // 2
        return array, from_x, from_y, self.to_k(from_x[:half], 2), self.to_k(from_y[half:], 1)

    def gather_end(self, mine):
        if not self.square:
            return self.gather_plane(mine[0])
        return lay_out(self.c, mine, [self.to_core(part) for part in mine])

    def gather_rows(self, array):
        if not self.square:
            return lax.all_gather(array, "dp", tiled=True)
        array = jnp.concatenate([array, self.to_k(array, 1)])
        return jnp.concatenate([array, self.to_k(array, 2)])

    def gather_plane_small(self, array):
        if not self.square:
            return self.gather_plane(array)
        near = jnp.stack([array, self.to_k(array, 1)])
        mine = jnp.concatenate([near, self.to_k(near, 2)])
        return self.by_core(mine, self.to_core(mine)).reshape((-1,) + array.shape[1:])

    def halves(self, array):
        count = array.shape[0] // 2
        own = lax.dynamic_slice_in_dim(array, self.c * count, count, 0)
        return own, lax.dynamic_slice_in_dim(array, (1 - self.c) * count, count, 0)

    def chip_product(self, left, right, dot, exact=False):
        own, other = self.halves(left)
        count = own.shape[0] // 2
        got = []
        for i in range(2):
            part = dot(other[i * count : (i + 1) * count], right)
            if exact:
                part = self.pack(part, self.power_of(part))
                got.append(self.unpack(self.to_core(part))[0])
            else:
                got.append(self.to_core(part.astype(low)).astype(wide))
        chip = []
        for i in range(2):
            part = dot(own[i * count : (i + 1) * count], right) + got[i]
            chip += list(part.reshape(self.k_count // 2, -1, part.shape[-1]))
        return chip

    def power_of(self, values):
        largest = jnp.max(jnp.abs(values), axis=-1, keepdims=True)
        return jnp.ceil(jnp.log2(jnp.clip(largest, 1e-30, 1e37)))

    def pack(self, parts, power):
        scaled = (parts * jnp.exp2(-power)).astype(jnp.float16)
        power = jnp.broadcast_to(power, power.shape[:-1] + (128,)).astype(jnp.float16)
        return jnp.concatenate([scaled, power], axis=-1)

    def unpack(self, got):
        got = got.astype(wide)
        width = got.shape[-1] - 128
        power = got[..., width : width + 1]
        return got[..., :width] * jnp.exp2(power), power

    def chip_send(self, left, right, side):
        if not self.square:
            return None, None
        other = other_call(self.c, left, right, left.shape[0] // 8, side)
        return other, self.to_core(other)

    def chip_own(self, left, right, got, side):
        if not self.square:
            return self.chip_product(left, right, dot_nt if side else dot_nn)
        return own_call(self.c, left, right, got, left.shape[0] // 8, side)

    def near_parts(self, parts):
        if not self.square:
            return self.near_plane(parts)
        chip, next_a, next_b, a, b = parts
        return (chip, next_a, next_b, *together(self.to_k(a, 1), self.to_k(b, 2)))

    def far_product(self, near):
        if not self.square:
            return self.far_plane(near)
        chip, next_a, next_b, got_a, got_b = near
        half = next_a.shape[1]
        got_a, got_b = got_a.astype(wide), got_b.astype(wide)
        own_a, own_b = chip[:, :half] + got_a[0], chip[:, half:] + got_b[0]
        return self.last_plane(next_a + got_a[1], next_b + got_b[1], None, None, own_a, own_b)

    def near_plane(self, chip, exact=False):
        if not self.square:
            return (lax.psum_scatter(jnp.stack(chip), "dp", scatter_dimension=0, tiled=False),)
        half = chip[0].shape[1] // 2
        power = [self.power_of(part) for part in chip] if exact else None

        def pick(a, i, j):
            return a if a is None else jnp.stack([a[i], a[j]])

        got_a = self.send_plane(jnp.stack([chip[1][:, :half], chip[3][:, :half]]), pick(power, 1, 3), 1)
        got_b = self.send_plane(jnp.stack([chip[2][:, half:], chip[3][:, half:]]), pick(power, 2, 3), 2)
        got_a, got_b = together(got_a, got_b)
        return chip, power, got_a, got_b

    def send_plane(self, parts, power, flip):
        if power is None:
            return self.to_k(parts.astype(low), flip), None
        return self.unpack(self.to_k(self.pack(parts, power), flip))

    def far_plane(self, near):
        if not self.square:
            return near[0]
        chip, power, (got_a, power_a), (got_b, power_b) = near
        half = chip[0].shape[1] // 2
        got_a, got_b = got_a.astype(wide), got_b.astype(wide)

        def above(a, i, b, j):
            return a if a is None else jnp.maximum(a[i], b[j]) + 1.0

        next_a, next_b = chip[2][:, :half] + got_a[1], chip[1][:, half:] + got_b[1]
        return self.last_plane(
            next_a,
            next_b,
            above(power_a, 1, power, 2),
            above(power_b, 1, power, 1),
            chip[0][:, :half] + got_a[0],
            chip[0][:, half:] + got_b[0],
        )

    def last_plane(self, next_a, next_b, power_a, power_b, own_a, own_b):
        if power_a is None:
            next_a, next_b = together(next_a.astype(low), next_b.astype(low))
            last_a, last_b = self.to_k(next_a, 2).astype(wide), self.to_k(next_b, 1).astype(wide)
        else:
            next_a, next_b = together(self.pack(next_a, power_a), self.pack(next_b, power_b))
            last_a, last_b = self.unpack(self.to_k(next_a, 2))[0], self.unpack(self.to_k(next_b, 1))[0]
        return jnp.concatenate([own_a + last_a, own_b + last_b], axis=1)

    def sum_plane(self, chip, exact=False):
        return self.far_plane(self.near_plane(chip, exact))

    def exchange_plane(self, array):
        return self.exchange_dp(self.exchange_core(array))

    def exchange_core(self, array):
        keep = lax.dynamic_index_in_dim(array, self.c, 1, False)
        got = self.to_core(lax.dynamic_index_in_dim(array, 1 - self.c, 1, False))
        return jnp.moveaxis(self.by_core(keep, got), 0, 1)

    def exchange_dp(self, pairs):
        if not self.square:
            return lax.all_to_all(pairs, "dp", 0, 0, tiled=True)
        parts = [lax.dynamic_index_in_dim(pairs, self.k, 0, False)]
        for flip in range(1, 4):
            parts.append(self.to_k(lax.dynamic_index_in_dim(pairs, self.k ^ flip, 0, False), flip))
        odd = self.k % 2 == 1
        parts = [jnp.where(odd, parts[i ^ 1], parts[i]) for i in range(4)]
        upper = self.k >= 2
        return jnp.stack([jnp.where(upper, parts[i ^ 2], parts[i]) for i in range(4)])


def gelu_pair(x):
    slope = 0.7978845608028654
    inner = jnp.tanh(slope * (x + 0.044715 * x * x * x))
    half = 0.5 * (1.0 + inner)
    return x * half, half + 0.5 * x * (1.0 - inner * inner) * slope * (1.0 + 0.134145 * x * x)


def rms_normed(values, gain):
    values = values.astype(wide)
    scale = lax.rsqrt(jnp.mean(values * values, axis=1, keepdims=True) + eps_value)
    return (values * scale * gain).astype(low)


def ordered(values, order):
    if order is None:
        return values
    size = values.shape[1] // len(order)
    return jnp.concatenate([values[:, i * size : (i + 1) * size] for i in order], axis=1)


def minus_expm1(x):
    near = 1.0
    for i in range(8, 1, -1):
        near = 1.0 + near * x * (1.0 / i)
    return jnp.where(x > -0.5, -x * near, 1.0 - jnp.exp(x))


def gates_of(conv_low, w_gates, params, not_start):
    width = conv_low.shape[1]
    pre = jnp.dot(conv_low, w_gates, preferred_element_type=wide)
    rate = jax.nn.sigmoid(pre[:, :width] + params[5:6])
    igate = jax.nn.sigmoid(pre[:, width:] + params[6:7])
    log_keep = params[7:8] * rate
    room = minus_expm1(2.0 * log_keep)
    mult = jnp.where(not_start > 0.5, jnp.sqrt(jnp.maximum(room, floor_value)), 1.0)
    return rate, igate, jnp.exp(log_keep), room, mult


def shifted(values, by, fill):
    count = values.shape[0]
    size = abs(by)
    if size % 8 == 0:
        free = jnp.full((size, values.shape[1]), fill, values.dtype)
        if by > 0:
            return jnp.concatenate([free, values[: count - size]])
        return jnp.concatenate([values[size:], free])
    place = lax.broadcasted_iota(jnp.int32, values.shape, 0)
    moved = pltpu.roll(values, by % count, 0)
    return jnp.where(place >= by if by > 0 else place < count - size, moved, fill)


def scan_rows(keep, drive, sign):
    by = 1
    while by < keep.shape[0]:
        drive = drive + keep * shifted(drive, sign * by, 0.0)
        keep = keep * shifted(keep, sign * by, 1.0)
        by *= 2
    return keep, drive


def conv_kernel(
    rows, span, order, x_ref, w_ref, halo_ref, gain_ref, params_ref, gates_ref,
    normed_ref, masks_ref, branch_ref, in_ref, low_ref, keep_ref, part_ref, run_ref, sums_ref, before_ref, tail, line, ends,
):
    step = pl.program_id(0)
    width = in_ref.shape[1]
    count = x_ref.shape[0]
    row_dev = count // span

    @pl.when(step == 0)
    def _():
        normed = rms_normed(halo_ref[...], gain_ref[...])
        before = jnp.dot(ordered(normed, order), w_ref[:, width:], preferred_element_type=wide)
        tail[...] = before.astype(low).astype(wide)
        before_ref[...] = tail[...]

    features = gain_ref.shape[1]
    normed = rms_normed(x_ref[:, :features], gain_ref[...])
    normed_ref[...] = normed
    masks_ref[...] = x_ref[:, features : features + 8].astype(wide)
    pre = jnp.dot(ordered(normed, order), w_ref[...], preferred_element_type=wide)
    branch_ref[...] = pre[:, :width]
    conv_in = pre[:, width:].astype(low)
    in_ref[...] = conv_in
    conv_in = conv_in.astype(wide)
    params = params_ref[...]
    for row in range(row_dev):
        at = slice(row * span, (row + 1) * span)
        own = conv_in[at]
        place = pl.ds(pl.multiple_of((lax.rem(step * row_dev + row, rows)) * 8, 8), 8)
        line[:8] = tail[place]
        line[8:] = own
        tail[place] = own[span - 8 :]
        masks = masks_ref[at]
        total = params[4:5] + params[0:1] * own
        for by in range(1, 4):
            total = total + params[by : by + 1] * line[8 - by : 8 - by + span] * masks[:, by - 1 : by]
        conv_low = total.astype(low)
        low_ref[at] = conv_low
        not_start = masks[:, 3:4]
        rate, igate, keep, room, mult = gates_of(conv_low, gates_ref[...], params, not_start)
        keep = keep * not_start
        keep_ref[at] = keep
        run, part = scan_rows(keep, mult * igate * conv_low.astype(wide), 1)

        @pl.when(step * row_dev < rows)
        def _(run=run, part=part, place=place, at=at):
            run_ref[at] = run
            part_ref[at] = part
            ends[0, place] = run[span - 8 :]
            ends[1, place] = part[span - 8 :]

        @pl.when(step * row_dev >= rows)
        def _(run=run, part=part, place=place, at=at):
            part = part + run * ends[1, place][7:8]
            run = run * ends[0, place][7:8]
            run_ref[at] = run
            part_ref[at] = part
            sums_ref[0, place] = run[span - 8 :]
            sums_ref[1, place] = part[span - 8 :]


def state_kernel(rows, span, part_ref, run_ref, start_ref, branch_ref, state_ref, mixed_ref):
    step = pl.program_id(0)
    row_dev = part_ref.shape[0] // span
    for row in range(row_dev):
        at = slice(row * span, (row + 1) * span)
        place = pl.ds(pl.multiple_of((lax.rem(step * row_dev + row, rows)) * 8, 8), 8)
        state = part_ref[at] + run_ref[at] * start_ref[place][7:8]
        state_ref[at] = state
        value, _ = gelu_pair(branch_ref[at])
        mixed_ref[at] = (value * state).astype(low)


def mlp_kernel(x_ref, cot_ref, w_ref, down_ref, hidden_ref, grad_ref):
    width = hidden_ref.shape[1]
    pre = jnp.dot(x_ref[...], w_ref[...], preferred_element_type=wide)
    grad = lax.dot_general(
        cot_ref[...], down_ref[...], (((1,), (1,)), ((), ())), preferred_element_type=wide
    )
    up = pre[:, width:]
    value, slope = gelu_pair(pre[:, :width])
    hidden_ref[...] = (value * up).astype(low)
    grad_ref[:, :width] = (grad * up * slope).astype(low)
    grad_ref[:, width:] = (grad * value).astype(low)


def other_kernel(side, core_ref, x_ref, w_ref, out_ref):
    product = lax.dot_general(
        x_ref[...], w_ref[...], (((1,), (side,)), ((), ())), preferred_element_type=wide
    )
    out_ref[...] = product.astype(low)


def own_kernel(side, core_ref, x_ref, w_ref, got_ref, chip_ref, next_a_ref, next_b_ref, a_ref, b_ref):
    step = pl.program_id(0)
    product = lax.dot_general(
        x_ref[...], w_ref[...], (((1,), (side,)), ((), ())), preferred_element_type=wide
    )
    product = product + got_ref[...].astype(wide)
    half = product.shape[1] // 2

    @pl.when(step == 0)
    def _():
        chip_ref[...] = product

    @pl.when(step == 1)
    def _():
        next_b_ref[...] = product[:, half:]

    @pl.when(step == 2)
    def _():
        next_a_ref[...] = product[:, :half]

    @pl.when((step == 1) | (step == 3))
    def _():
        a_ref[0] = product[:, :half].astype(low)

    @pl.when(step >= 2)
    def _():
        b_ref[0] = product[:, half:].astype(low)


def back_kernel(
    rows, span, x_ref, w_ref, branch_ref, state_ref, keep_ref, grad_branch_ref, part_ref, run_ref, sum_ref, ends
):
    step = pl.program_id(0)
    count = x_ref.shape[0]
    row_dev = count // span
    mixed = lax.dot_general(
        x_ref[...], w_ref[...], (((1,), (1,)), ((), ())), preferred_element_type=wide
    )
    late = step * row_dev < rows
    for row in range(row_dev):
        at = slice(row * span, (row + 1) * span)
        block = (pl.num_programs(0) - 1 - step) * row_dev + row
        place = pl.ds(pl.multiple_of(lax.rem(block, rows) * 8, 8), 8)
        value, slope = gelu_pair(branch_ref[at])
        grad_branch_ref[at] = (mixed[at] * state_ref[at] * slope).astype(low)
        grad = mixed[at] * value
        keep = keep_ref[at]
        run, part = scan_rows(keep, keep * grad, -1)

        @pl.when(late)
        def _(run=run, part=part, grad=grad, place=place, at=at):
            ends[0, place] = run[:8]
            ends[1, place] = part[:8]
            run_ref[at] = shifted(run, -1, 1.0)
            part_ref[at] = grad + shifted(part, -1, 0.0)

        @pl.when(jnp.logical_not(late))
        def _(run=run, part=part, grad=grad, place=place, at=at):
            next_run, next_part = ends[0, place][:1], ends[1, place][:1]
            part = part + run * next_part
            run = run * next_run
            last = lax.broadcasted_iota(jnp.int32, run.shape, 0) == span - 1
            run_ref[at] = jnp.where(last, next_run, shifted(run, -1, 1.0))
            part_ref[at] = grad + jnp.where(last, next_part, shifted(part, -1, 0.0))
            sum_ref[place] = part[:8]


def adjoint_kernel(
    rows, span, part_ref, run_ref, carry_ref, state_ref, start_ref, low_ref, gates_ref, params_ref,
    masks_ref, in_ref, before_ref, grad_conv_ref, small_ref, gates_grad_ref, sums_ref, line, ends, tail,
):
    step = pl.program_id(0)
    width = low_ref.shape[1]
    row_dev = low_ref.shape[0] // span
    params = params_ref[...]

    @pl.when(step == 0)
    def _():
        gates_grad_ref[...] = jnp.zeros(gates_grad_ref.shape, wide)
        sums_ref[...] = jnp.zeros(sums_ref.shape, wide)
        ends[...] = start_ref[...]
        tail[...] = before_ref[...]

    for row in range(row_dev):
        at = slice(row * span, (row + 1) * span)
        place = pl.ds(pl.multiple_of((lax.rem(step * row_dev + row, rows)) * 8, 8), 8)
        conv_low = low_ref[at]
        conv_value = conv_low.astype(wide)
        masks = masks_ref[at]
        not_start = masks[:, 3:4]
        rate, igate, keep, room, mult = gates_of(conv_low, gates_ref[...], params, not_start)
        adj = part_ref[at] + run_ref[at] * carry_ref[place][:1]
        state = state_ref[at]
        line[:8] = ends[place]
        line[8:] = state
        ends[place] = state[span - 8 :]
        through = adj * line[7 : 7 + span]
        spread = jnp.where(room > floor_value, adj * igate * conv_value * keep * keep / mult, 0.0)
        grad_log = not_start * (through * keep - spread)
        grad_rate = (grad_log * params[7:8] * rate * (1.0 - rate)).astype(low)
        scaled = adj * mult
        grad_igate = (scaled * conv_value * igate * (1.0 - igate)).astype(low)
        both = jnp.concatenate([grad_rate, grad_igate], axis=1)
        grad_conv = scaled * igate + lax.dot_general(
            both, gates_ref[...], (((1,), (1,)), ((), ())), preferred_element_type=wide
        )
        grad_conv = grad_conv.astype(low)
        grad_conv_ref[at] = grad_conv
        gates_grad_ref[...] += lax.dot_general(
            conv_low, both, (((0,), (0,)), ((), ())), preferred_element_type=wide
        )
        grad_conv = grad_conv.astype(wide)
        conv_in = in_ref[at].astype(wide)
        line[:8] = tail[place]
        line[8:] = conv_in
        tail[place] = conv_in[span - 8 :]
        values = [grad_conv * conv_in]
        for by in range(1, 4):
            values.append(grad_conv * line[8 - by : 8 - by + span] * masks[:, by - 1 : by])
        values += [grad_conv, grad_rate.astype(wide), grad_igate.astype(wide), grad_log * rate * params[8:9]]
        for i, value in enumerate(values):
            sums_ref[i : i + 1] += jnp.sum(value, axis=0, keepdims=True)

    @pl.when(step == pl.num_programs(0) - 1)
    def _():
        block = small_ref.shape[1] // 2 - 64
        for head in range(width // block):
            at = slice(head * block, (head + 1) * block)
            small_ref[at, :block] = gates_grad_ref[at, at].astype(low)
            then = slice(width + head * block, width + (head + 1) * block)
            small_ref[at, block : 2 * block] = gates_grad_ref[at, then].astype(low)
        small_ref[:, 2 * block :] = sums_ref[...].T[:width].astype(low)


def conv_back_kernel(rows, span, grad_ref, halo_ref, masks_ref, halo_masks_ref, branch_ref, params_ref, one_ref, line):
    params = params_ref[...]

    def work(block, grad_next, masks_next):
        at = pl.ds(pl.multiple_of(block * span, 16), span)
        own = grad_ref[at].astype(wide)
        total = params[0:1] * own
        masks = masks_ref[at]
        for by in range(1, 4):
            line[:span] = own * masks[:, by - 1 : by]
            line[span:] = grad_next * masks_next[:, by - 1 : by]
            total = total + params[by : by + 1] * line[by : by + span]
        width = branch_ref.shape[1]
        one_ref[at, :width] = branch_ref[at]
        one_ref[at, width:] = total.astype(low)

    @pl.loop(0, rows)
    def _(block):
        then = pl.ds(pl.multiple_of((block + rows) * span, 16), 16)
        work(block, grad_ref[then].astype(wide)[:8], masks_ref[then][:8])

    @pl.loop(0, rows)
    def _(block):
        then = pl.ds(pl.multiple_of(block * 16, 16), 16)
        work(block + rows, halo_ref[then].astype(wide)[:8], halo_masks_ref[then][:8])


def whole_block(array):
    return pl.BlockSpec(array.shape, lambda *i, n=len(array.shape): (0,) * n)


def token_block(array, count, steps, backwards):
    def index(i):
        return (steps - 1 - i if backwards else i,) + (0,) * (len(array.shape) - 1)

    return pl.BlockSpec((count,) + array.shape[1:], index)


def half_of(core, x, count, width):
    return pl.BlockSpec((count, width), lambda k, core_ref: (core_ref[0] * (x.shape[0] // (2 * count)) + k, 0))


def half_call(kernel, core, x, w, count, extra, outputs):
    def spec(array, block, index):
        return pl.BlockSpec(block, lambda k, core_ref: index(k))

    return pl.pallas_call(
        kernel,
        out_shape=[array for array, _, _ in outputs],
        grid_spec=pltpu.PrefetchScalarGridSpec(
            num_scalar_prefetch=1,
            grid=(x.shape[0] // (2 * count),),
            in_specs=[
                half_of(core, x, count, x.shape[1]),
                pl.BlockSpec(w.shape, lambda k, core_ref: (0, 0)),
            ]
            + [spec(*one) for one in extra],
            out_specs=[spec(*one) for one in outputs],
        ),
        cost_estimate=pl.CostEstimate(flops=0, bytes_accessed=0, transcendentals=0),
        compiler_params=pltpu.CompilerParams(vmem_limit_bytes=56 * 2**20),
    )(core.reshape(1).astype(jnp.int32), x, w, *[array for array, _, _ in extra])


def other_call(core, x, w, count, side):
    width = w.shape[1 - side]
    out = jax.ShapeDtypeStruct((x.shape[0] // 2, width), low)
    kernel = functools.partial(other_kernel, side)
    return half_call(kernel, 1 - core, x, w, count, [], [(out, (count, width), lambda k: (k, 0))])[0]


def own_call(core, x, w, got, count, side):
    width = w.shape[1 - side]
    a = jax.ShapeDtypeStruct((2, count, width // 2), low)
    chip = jax.ShapeDtypeStruct((count, width), wide)
    after = jax.ShapeDtypeStruct((count, width // 2), wide)
    return half_call(
        functools.partial(own_kernel, side),
        core,
        x,
        w,
        count,
        [(got, (count, width), lambda k: (k, 0))],
        [
            (chip, chip.shape, lambda k: (0, 0)),
            (after, after.shape, lambda k: (0, 0)),
            (after, after.shape, lambda k: (0, 0)),
            (a, (1, count, width // 2), lambda k: (k // 2, 0, 0)),
            (a, (1, count, width // 2), lambda k: (k // 3, 0, 0)),
        ],
    )


def rows_kernel(core_ref, x_ref, grad_ref, sent_ref, kept_ref):
    count = kept_ref.shape[1]
    total = lax.dot_general(
        x_ref[...], grad_ref[...], (((0,), (0,)), ((), ())), preferred_element_type=wide
    )
    planes = sent_ref.shape[0]
    first = lax.rem(pl.program_id(0), core_ref[1]) * planes
    for i in range(planes):
        part = total[i * count : (i + 1) * count]
        mine = first + i == core_ref[0]
        sent_ref[i, 0] = jnp.where(mine, jnp.zeros_like(part), part).astype(low)

        @pl.when(mine)
        def _(part=part):
            kept_ref[0] = part


def rows_call(z, z_count, k_count, x, grad):
    tokens, features = x.shape
    count = features // (z_count * k_count)
    planes = max(2, 128 // count)
    width = grad.shape[1]
    per = z_count // planes
    sent = jax.ShapeDtypeStruct((z_count, k_count, count, width), low)
    kept = jax.ShapeDtypeStruct((k_count, count, width), wide)
    return pl.pallas_call(
        rows_kernel,
        out_shape=[sent, kept],
        grid_spec=pltpu.PrefetchScalarGridSpec(
            num_scalar_prefetch=1,
            grid=(k_count * per,),
            in_specs=[
                pl.BlockSpec((tokens, planes * count), lambda i, ref: (0, i)),
                pl.BlockSpec(grad.shape, lambda i, ref: (0, 0)),
            ],
            out_specs=[
                pl.BlockSpec((planes, 1, count, width), lambda i, ref: (i % per, i // per, 0, 0)),
                pl.BlockSpec((1, count, width), lambda i, ref: (i // per, 0, 0)),
            ],
        ),
        cost_estimate=pl.CostEstimate(flops=0, bytes_accessed=0, transcendentals=0),
        compiler_params=pltpu.CompilerParams(vmem_limit_bytes=56 * 2**20),
    )(jnp.stack([z, jnp.int32(per)]).astype(jnp.int32), x, grad)


def down_kernel(core_ref, hidden_ref, cot_ref, sent_ref, kept_ref):
    total = lax.dot_general(
        cot_ref[...], hidden_ref[...], (((0,), (0,)), ((), ())), preferred_element_type=wide
    )
    total = total.T
    count = kept_ref.shape[0]
    for i in range(sent_ref.shape[0]):
        part = total[i * count : (i + 1) * count]
        mine = core_ref[0] == i
        sent_ref[i] = jnp.where(mine, jnp.zeros_like(part), part).astype(low)

        @pl.when(mine)
        def _(part=part):
            kept_ref[...] = part


def down_call(z, z_count, hidden, cot):
    tokens, features = cot.shape
    count = hidden.shape[1] // z_count
    columns = 256
    sent = jax.ShapeDtypeStruct((z_count, count, features), low)
    kept = jax.ShapeDtypeStruct((count, features), wide)
    return pl.pallas_call(
        down_kernel,
        out_shape=[sent, kept],
        grid_spec=pltpu.PrefetchScalarGridSpec(
            num_scalar_prefetch=1,
            grid=(features // columns,),
            in_specs=[
                pl.BlockSpec(hidden.shape, lambda i, ref: (0, 0)),
                pl.BlockSpec((tokens, columns), lambda i, ref: (0, i)),
            ],
            out_specs=[
                pl.BlockSpec((z_count, count, columns), lambda i, ref: (0, 0, i)),
                pl.BlockSpec((count, columns), lambda i, ref: (0, i)),
            ],
        ),
        cost_estimate=pl.CostEstimate(flops=0, bytes_accessed=0, transcendentals=0),
        compiler_params=pltpu.CompilerParams(vmem_limit_bytes=56 * 2**20),
    )(z.reshape(1).astype(jnp.int32), hidden, cot)


def kernel_call(kernel, steps, inputs, outputs, scratch=(), backwards=False):
    def spec(array, count):
        return whole_block(array) if count is None else token_block(array, count, steps, backwards)

    return pl.pallas_call(
        kernel,
        out_shape=[array for array, _ in outputs],
        grid=(steps,),
        in_specs=[spec(array, count) for array, count in inputs],
        out_specs=[spec(array, count) for array, count in outputs],
        scratch_shapes=scratch,
        cost_estimate=pl.CostEstimate(flops=0, bytes_accessed=0, transcendentals=0),
        compiler_params=pltpu.CompilerParams(vmem_limit_bytes=56 * 2**20),
    )(*[array for array, _ in inputs])


def per_device(
    tokens,
    segment_ids,
    cotangent,
    norm_one,
    branch_weight,
    input_proj,
    conv_weight,
    conv_bias,
    rate_weight,
    igate_weight,
    rate_bias,
    igate_bias,
    decay_param,
    out_proj,
    norm_two,
    mlp_gate,
    mlp_up,
    mlp_down,
):
    at = Place()
    k_count, z_count = at.k_count, at.z_count
    group = 2 * k_count
    row_dev, span, width_d = tokens.shape
    tok = row_dev * span
    rows = k_count * row_dev
    tok_all = 2 * rows * span
    d_own = norm_one.shape[0]
    w_own = conv_bias.shape[0]
    f_own = mlp_down.shape[0]
    width_r = branch_weight.shape[1]
    w_slot = width_r // group
    f_slot = f_own * z_count
    taps = conv_weight.shape[0]
    reach = taps - 1
    half_z = z_count // 2

    def by_feature(array):
        split = array.reshape(z_count, -1, 2 * d_own, array.shape[1])
        return jnp.swapaxes(split, 0, 1).reshape(array.shape)

    small = jnp.concatenate(
        [
            norm_one,
            norm_two,
            conv_weight.reshape(-1),
            conv_bias,
            rate_bias,
            igate_bias,
            decay_param,
        ]
    )
    rec_cols = jnp.concatenate(
        [
            branch_weight.reshape(d_own, k_count, 2, w_slot),
            input_proj.reshape(d_own, k_count, 2, w_slot),
        ],
        axis=3,
    )
    rec_pairs = at.exchange_core(jnp.moveaxis(rec_cols, 0, 2))

    seg_code = (segment_ids % 64).astype(low)
    pairs = [(i, i + 1) for i in range(at.s_count - 1)]
    before = lax.ppermute(seg_code[:, span - reach :], "seq", pairs)
    tokens = tokens.reshape(tok, width_d)
    tail = tokens.reshape(row_dev, span, width_d)[:, span - 8 :].reshape(row_dev * 8, width_d)
    tail = at.to_z(tail, 1)

    small = jnp.pad(small, (0, -small.shape[0] % 128)).reshape(-1, 128)
    small_rows = small.shape[0]
    small = jnp.pad(small, ((0, w_own - small_rows), (0, 0)))
    out_rows = jnp.concatenate([out_proj, rate_weight, igate_weight, small], axis=1)
    out_rows, before, tail = together(out_rows, before, tail)
    out_part = at.gather_z(out_rows)

    rec_cols = at.exchange_dp(rec_pairs)
    order = None
    if 2 * d_own % 128 == 0:
        order = [k * z_count + z for z in range(z_count) for k in range(k_count)]
    ext_code = jnp.concatenate([before, seg_code], axis=1)
    position = lax.broadcasted_iota(jnp.int32, (row_dev, span), 1)
    masks = [
        (ext_code[:, reach - by : reach - by + span] == seg_code) & ((at.s > 0) | (position >= by))
        for by in range(1, taps)
    ]
    masks = jnp.stack(masks + [masks[0]] * (9 - taps), axis=-1).astype(low).reshape(tok, 8)
    beside = jnp.concatenate([tokens, jnp.pad(masks, ((0, 0), (0, 120)))], axis=1)
    beside, rec_cols = together(beside, rec_cols)
    w1 = at.gather_z(rec_cols.reshape(group * d_own, 2 * w_slot))
    beside_near = at.gather_near(beside)
    tail = jnp.where(at.c == 1, tail, at.to_core(tail))
    inputs = tokens.astype(wide)
    s1 = lax.rsqrt(jnp.mean(inputs * inputs, axis=-1, keepdims=True) + eps_value)
    mlp_shape = jax.ShapeDtypeStruct((k_count, 2, d_own, 2 * f_slot), low)
    cut = functools.partial(cut_kernel, k_count, z_count)
    mlp_pairs = at.exchange_core(in_vmem(cut, (mlp_gate, mlp_up), mlp_shape))
    beside_near, tail, mlp_pairs, out_part = together(beside_near, tail, mlp_pairs, out_part)
    tail = at.gather_rows(tail)

    out_split = out_part.reshape(2, half_z, w_own, -1)

    def of_slot(columns):
        part = out_split[..., columns]
        keep = lax.dynamic_index_in_dim(part, at.c, 0, False)
        got = at.to_core(lax.dynamic_index_in_dim(part, 1 - at.c, 0, False))
        return jnp.swapaxes(at.by_core(keep, got), 0, 1).reshape(w_slot, -1)

    gate_rows = of_slot(slice(width_d, width_d + 2 * BS))
    small = out_part.reshape(z_count, w_own, -1)[:, :small_rows, width_d + 2 * BS :].reshape(z_count, -1)
    small = jnp.swapaxes(at.by_core(small, at.to_core(small)), 0, 1).reshape(at.s_count, -1)
    gains = at.gather_dp_small(small[:, : 2 * d_own]).reshape(k_count * at.s_count, -1)
    mine = lax.dynamic_slice_in_dim(small[:, 2 * d_own :], at.c * z_count, z_count, 0)
    mine = mine[:, : (taps + 4) * w_own].reshape(z_count, taps + 4, w_own).astype(wide)
    mine = jnp.swapaxes(mine, 0, 1).reshape(taps + 4, w_slot)
    w_conv = mine[:taps]
    b_conv, b_rate, b_igate, decay = (mine[taps + i][None, :] for i in range(4))
    log_slope = -rate_scale * jax.nn.softplus(-decay)
    decay_slope = rate_scale * jax.nn.sigmoid(-decay)
    params = jnp.concatenate([w_conv, b_conv, b_rate, b_igate, log_slope] + [decay_slope] * 8)
    beside_near, tail, gains, gate_rows = together(beside_near, tail, gains, gate_rows)
    heads = w_slot // BS

    def block_diagonal(columns):
        blocks = columns.reshape(heads, BS, 1, BS)
        same = jnp.eye(heads, dtype=low).reshape(heads, 1, heads, 1)
        return (blocks * same).reshape(w_slot, w_slot)

    w_gates = jnp.concatenate([block_diagonal(gate_rows[:, :BS]), block_diagonal(gate_rows[:, BS:])], axis=1)

    beside_far, mlp_pairs, w_gates, params = together(
        at.gather_far(beside_near), mlp_pairs, w_gates, params
    )
    gain_one = gains[:, :d_own].reshape(1, width_d).astype(wide)
    gain_two = gains[:, d_own:].reshape(1, width_d).astype(wide)
    mlp_cols = at.exchange_dp(mlp_pairs)
    cot = cotangent.reshape(tok, width_d)
    tokens_all, mlp_cols, cot = together(at.gather_end(beside_far), mlp_cols, cot)
    shape = jax.ShapeDtypeStruct

    half_rows = group * d_own // 2
    w2_parts = [
        at.gather_z(part.reshape(half_rows, 2 * f_slot))
        for part in (mlp_cols[: k_count // 2], mlp_cols[k_count // 2 :])
    ]

    steps = tok_all // tok
    cot_near = at.gather_near(cot)
    flat32, flat16 = shape((tok_all, w_slot), wide), shape((tok_all, w_slot), low)
    ends = shape((rows * 8, w_slot), wide)

    def by_row(array):
        return jnp.repeat(array, 8, axis=0)

    n1_all, masks, branch_pre, conv_in, conv_low, keep_eff, part, run, summary, conv_before = kernel_call(
        functools.partial(conv_kernel, rows, span, order),
        steps,
        [(tokens_all, tok), (w1 if order else by_feature(w1), None), (tail, None), (gain_one, None), (params, None), (w_gates, None)],
        [(shape((tok_all, width_d), low), tok), (shape((tok_all, 8), wide), tok), (flat32, tok), (flat16, tok), (flat16, tok)]
        + [(flat32, tok)] * 3
        + [(shape((2,) + ends.shape, wide), None), (ends, None)],
        [
            pltpu.VMEM(ends.shape, wide),
            pltpu.VMEM((span + 8, w_slot), wide),
            pltpu.VMEM((2,) + ends.shape, wide),
        ],
    )
    summary = summary.reshape(2, rows, 8, w_slot)[:, :, 7]
    w_down = at.gather_z(mlp_down)
    summary, cot_near, out_split, w1 = together(summary, cot_near, out_split, w1)
    w1 = by_feature(w1)
    w_out = of_slot(slice(0, width_d))
    cot_far = at.gather_far(cot_near)
    before = [at.to_z(summary, by) for by in range(1, z_count)]
    state_in = jnp.zeros((rows, w_slot), wide)
    for one in reversed(before):
        state_in = one[1] + one[0] * state_in
    state_in = by_row(state_in)
    state, mixed = kernel_call(
        functools.partial(state_kernel, rows, span),
        steps,
        [(part, tok), (run, tok), (state_in, None), (branch_pre, tok)],
        [(flat32, tok), (flat16, tok)],
    )
    masks_after = at.to_z(masks.reshape(2, rows, span, 8)[0, :, :16], -1).reshape(rows * 16, 8)
    mixed, cot_far, w2_parts[0], masks_after, w1 = together(mixed, cot_far, w2_parts[0], masks_after, w1)

    chip_one = at.chip_product(mixed, w_out, dot_nn, exact=True)
    near_sum, cot_far = together(at.near_plane(chip_one, exact=True), cot_far)
    cot_all = at.gather_end(cot_far)
    resid, cot_all = together(inputs + at.far_plane(near_sum), cot_all)
    resid, w2_parts[1] = together(resid, w2_parts[1])
    w2 = jnp.concatenate([by_feature(part) for part in w2_parts])

    s2 = lax.rsqrt(jnp.mean(resid * resid, axis=-1, keepdims=True) + eps_value)
    normed_two = (resid * s2 * gain_two).astype(low)
    n2_near, w2 = together(at.gather_near(normed_two), w2)
    n2_all, w_down = together(at.gather_end(at.gather_far(n2_near)), w_down)
    hidden, grad_two = kernel_call(
        mlp_kernel,
        steps,
        [(n2_all, tok), (cot_all, tok), (w2, None), (w_down, None)],
        [(shape((tok_all, f_slot), low), tok), (shape((tok_all, 2 * f_slot), low), tok)],
    )
    def rows_apart(x, grad):
        sent, kept = rows_call(at.z, z_count, k_count, x, grad)
        return sent.reshape(-1, sent.shape[-1]), kept.reshape(-1, kept.shape[-1])

    _, got_two = at.chip_send(grad_two, w2, 1)
    near_two = at.near_parts(at.chip_own(grad_two, w2, got_two, 1))
    chip_two, grad_two = together(near_two[0], grad_two)
    w2_part = rows_apart(n2_all, grad_two)
    near_two, w2_part, hidden = together(near_two, w2_part, hidden)
    w2_sum = at.scatter_z(w2_part)
    grad_n2 = at.far_product(near_two)
    other_three, got_three = at.chip_send(hidden, w_down, 0)
    grad_n2, other_three, hidden = together(grad_n2, other_three, hidden)
    scaled_two = gain_two * grad_n2
    cot_f = cot.astype(wide)
    mean_two = jnp.mean(scaled_two * resid, axis=-1, keepdims=True)
    grad_resid = cot_f + s2 * scaled_two - resid * (s2 * s2 * s2) * mean_two
    grad_recur = grad_resid.astype(low)
    grad_recur, hidden = together(grad_recur, hidden)
    chip_three = at.chip_own(hidden, w_down, got_three, 0)
    down_sent, down_kept = down_call(at.z, z_count, hidden, cot_all)
    down_part = down_sent.reshape(-1, width_d), down_kept
    gr_near, chip_three, down_part = together(at.gather_near(grad_recur), chip_three, down_part)
    down_sum = at.scatter_z(down_part)
    gr_all, chip_three = together(at.gather_end(at.gather_far(gr_near)), chip_three)

    def summed(pair):
        return pair[0].astype(wide) + pair[1].astype(wide)

    def to_owner(array, columns):
        return at.exchange_plane(array.reshape(k_count, 2, d_own, columns))


    grad_branch, back_part, back_run, back = kernel_call(
        functools.partial(back_kernel, rows, span),
        steps,
        [(gr_all, tok), (w_out, None), (branch_pre, tok), (state, tok), (keep_eff, tok)],
        [(flat16, tok), (flat32, tok), (flat32, tok), (ends, None)],
        [pltpu.VMEM((2,) + ends.shape, wide)],
        backwards=True,
    )
    back = back.reshape(rows, 8, w_slot)[:, 0]
    back, mixed, near_three = together(back, mixed, at.near_parts(chip_three))

    def by_owner(array):
        split = array.reshape(half_z, 2, w_own, -1)
        keep = lax.dynamic_index_in_dim(split, at.c, 1, False)
        got = at.to_core(lax.dynamic_index_in_dim(split, 1 - at.c, 1, False))
        return at.by_core(keep, got).reshape(z_count, w_own, -1)

    own = jnp.stack([summary[0], back])
    after = [at.to_z(own, -by) for by in range(1, z_count)]
    grad_out = dot_tn(mixed, gr_all)
    after, grad_out, w2_sum = together(after, grad_out, w2_sum)
    carry_in = jnp.zeros((rows, w_slot), wide)
    for part in reversed(after):
        carry_in = part[1] + part[0] * carry_in
    mlp_pairs = at.exchange_core(summed(w2_sum).reshape(k_count, 2, d_own, 2 * f_slot))
    carry_in, mlp_pairs = together(carry_in, mlp_pairs)
    mlp_back = at.exchange_dp(mlp_pairs)
    grad_conv, rec_small = kernel_call(
        functools.partial(adjoint_kernel, rows, span),
        steps,
        [
            (back_part, tok),
            (back_run, tok),
            (by_row(carry_in), None),
            (state, tok),
            (state_in, None),
            (conv_low, tok),
            (w_gates, None),
            (params, None),
            (masks, tok),
            (conv_in, tok),
            (conv_before, None),
        ],
        [(flat16, tok), (shape((w_slot, 2 * BS + 128), low), None)],
        [
            pltpu.VMEM((w_slot, 2 * w_slot), wide),
            pltpu.VMEM((128, w_slot), wide),
            pltpu.VMEM((span + 8, w_slot), wide),
            pltpu.VMEM(ends.shape, wide),
            pltpu.VMEM(ends.shape, wide),
        ],
    )
    grad_conv, near_three, mlp_back = together(grad_conv, near_three, mlp_back)
    block_out = (resid + at.far_product(near_three)).astype(low)
    head = at.to_z(grad_conv.reshape(2, rows, span, w_slot)[0, :, :16], -1).reshape(rows * 16, w_slot)
    rec_part = at.own_apart(by_owner(jnp.concatenate([grad_out.astype(low), rec_small], axis=1)), 0)
    head, rec_part = together(head, rec_part)
    rec_sum = at.scatter_z(rec_part)
    (grad_one,) = kernel_call(
        functools.partial(conv_back_kernel, rows, span),
        1,
        [(array, None) for array in (grad_conv, head, masks, masks_after, grad_branch, params)],
        [(shape((tok_all, 2 * w_slot), low), None)],
        [pltpu.VMEM((span + 8, w_slot), wide)],
    )

    grad_one, block_out = together(grad_one, block_out)
    other_one, got_one = at.chip_send(grad_one, w1, 1)
    other_one, then = together(other_one, grad_one)
    w1_part = rows_apart(n1_all, then)
    then, w1_part = together(then, w1_part)
    near_one = at.near_parts(at.chip_own(then, w1, got_one, 1))
    w1_sum = at.scatter_z(w1_part)
    mlp_whole = jax.ShapeDtypeStruct(mlp_gate.shape, wide)
    join = functools.partial(join_kernel, k_count, z_count)
    grad_gate_w, grad_up_w = in_vmem(join, (mlp_back,), (mlp_whole, mlp_whole))
    near_one, grad_gate_w, grad_up_w, down_sum = together(near_one, grad_gate_w, grad_up_w, down_sum)
    grad_n1 = at.far_product(near_one)
    w1_sum, grad_n1, rec_sum = together(w1_sum, grad_n1, rec_sum)
    rec_pairs = at.exchange_core(summed(w1_sum).reshape(k_count, 2, d_own, 2 * w_slot))
    rec_pairs, grad_n1, rec_sum = together(rec_pairs, grad_n1, rec_sum)
    rec_back = at.exchange_dp(rec_pairs)
    scaled_one = gain_one * grad_n1
    mean_one = jnp.mean(scaled_one * inputs, axis=-1, keepdims=True)
    grad_tokens = grad_resid + s1 * scaled_one - inputs * (s1 * s1 * s1) * mean_one
    grad_tokens = grad_tokens.reshape(row_dev, span, width_d)
    block_out = block_out.reshape(row_dev, span, width_d)

    rec_rows = summed(rec_sum)
    grad_out_w = rec_rows[:, :width_d]
    grad_rate_w = rec_rows[:, width_d : width_d + BS]
    grad_igate_w = rec_rows[:, width_d + BS : width_d + 2 * BS]
    grad_small = rec_rows[:, width_d + 2 * BS : width_d + 2 * BS + taps + 4].T
    grad_down = summed(down_sum)
    rec_back = jnp.moveaxis(rec_back, 2, 0)
    grad_branch_w = rec_back[..., :w_slot].reshape(d_own, width_r)
    grad_input_w = rec_back[..., w_slot:].reshape(d_own, width_r)

    def gain_grad(pairs, gain):
        total = sum(jnp.sum(weight.astype(wide) * grad, axis=1) for weight, grad in pairs)
        return total / gain.astype(wide)

    grad_norm_one = gain_grad(((branch_weight, grad_branch_w), (input_proj, grad_input_w)), norm_one)
    grad_norm_two = gain_grad(((mlp_gate, grad_gate_w), (mlp_up, grad_up_w)), norm_two)
    return (
        block_out,
        grad_tokens,
        grad_norm_one,
        grad_branch_w,
        grad_input_w,
        grad_small[:taps],
        grad_small[taps],
        grad_rate_w,
        grad_igate_w,
        grad_small[taps + 1],
        grad_small[taps + 2],
        grad_small[taps + 3],
        grad_out_w,
        grad_norm_two,
        grad_gate_w,
        grad_up_w,
        grad_down,
    )


def solution(mesh):
    rows, matrix = P(AXES), P(AXES, None)
    tokens = P("dp", "seq", None)
    return jax.shard_map(
        per_device,
        mesh=mesh,
        in_specs=(
            tokens,
            P("dp", "seq"),
            tokens,
            rows,
            matrix,
            matrix,
            P(None, AXES),
            rows,
            matrix,
            matrix,
            rows,
            rows,
            rows,
            matrix,
            rows,
            matrix,
            matrix,
            matrix,
        ),
        out_specs=(
            tokens,
            tokens,
            rows,
            matrix,
            matrix,
            P(None, AXES),
            rows,
            matrix,
            matrix,
            rows,
            rows,
            rows,
            matrix,
            rows,
            matrix,
            matrix,
            matrix,
        ),
        check_vma=False,
    )
```

```python
import functools

import jax
import jax.numpy as jnp
from jax import lax
from jax.experimental import pallas as pl
from jax.experimental.pallas import tpu as pltpu
from jax.sharding import PartitionSpec as P

HEADS = 16
BS = 160
AXES = ("dp", "seq")

eps_value = 1e-06
rate_scale = 8.0
floor_value = 0.001
low = jnp.bfloat16
wide = jnp.float32


def gelu_tanh(value):
    return jax.nn.gelu(value, approximate=True)


def dot_nn(left, right):
    return lax.dot_general(left, right, (((1,), (0,)), ((), ())), preferred_element_type=wide)


def dot_nt(left, right):
    return lax.dot_general(left, right, (((1,), (1,)), ((), ())), preferred_element_type=wide)


def dot_tn(left, right):
    return lax.dot_general(left, right, (((0,), (0,)), ((), ())), preferred_element_type=wide)


def lay_out_kernel(count, c_ref, *refs):
    parts, (out_ref, buffer, sem, out_sem) = refs[: 2 * count], refs[2 * count :]
    core = c_ref[0]
    copies = []
    for which in range(2):
        start = (core if which == 0 else 1 - core) * (out_ref.shape[0] // 2)
        for i, part in enumerate(parts[which * count : (which + 1) * count]):
            at = pl.ds(pl.multiple_of(start, 16), part.shape[0])
            j = which * count + i
            into = pltpu.make_async_copy(part, buffer.at[at], sem.at[j])
            into.start()
            copies.append((into, pltpu.make_async_copy(buffer.at[at], out_ref.at[at], out_sem.at[j])))
            start = start + part.shape[0]
    for into, out in copies:
        into.wait()
        out.start()
    for into, out in copies:
        out.wait()


def lay_out(core, own, other):
    rows = 2 * sum(part.shape[0] for part in own)
    shape = (rows,) + own[0].shape[1:]
    anywhere = pl.BlockSpec(memory_space=pl.ANY)
    return pl.pallas_call(
        functools.partial(lay_out_kernel, len(own)),
        out_shape=jax.ShapeDtypeStruct(shape, own[0].dtype),
        in_specs=[pl.BlockSpec(memory_space=pltpu.SMEM)] + [anywhere] * (2 * len(own)),
        out_specs=anywhere,
        scratch_shapes=[
            pltpu.VMEM(shape, own[0].dtype),
            pltpu.SemaphoreType.DMA((2 * len(own),)),
            pltpu.SemaphoreType.DMA((2 * len(own),)),
        ],
        compiler_params=pltpu.CompilerParams(vmem_limit_bytes=32 * 2**20),
    )(core.reshape(1).astype(jnp.int32), *own, *other)


def together(*arrays):
    return lax.optimization_barrier(arrays)


def cut_kernel(k_count, z_count, gate_ref, up_ref, out_ref):
    own = out_ref.shape[3] // (2 * z_count)
    for k in range(k_count):
        for c in range(2):
            for which, ref in enumerate((gate_ref, up_ref)):
                for z in range(z_count):
                    at = ((k * z_count + z) * 2 + c) * own
                    to = (which * z_count + z) * own
                    out_ref[k, c, :, to : to + own] = ref[:, at : at + own]


def join_kernel(k_count, z_count, in_ref, gate_ref, up_ref):
    own = in_ref.shape[3] // (2 * z_count)
    for k in range(k_count):
        for c in range(2):
            for which, ref in enumerate((gate_ref, up_ref)):
                for z in range(z_count):
                    to = ((k * z_count + z) * 2 + c) * own
                    at = (which * z_count + z) * own
                    ref[:, to : to + own] = in_ref[k, c, :, at : at + own].astype(ref.dtype)


def in_vmem(kernel, arrays, out_shape):
    vmem = pl.BlockSpec(memory_space=pltpu.VMEM)
    return pl.pallas_call(
        kernel,
        out_shape=out_shape,
        in_specs=[vmem] * len(arrays),
        out_specs=jax.tree.map(lambda _: vmem, out_shape),
        compiler_params=pltpu.CompilerParams(vmem_limit_bytes=48 * 2**20),
    )(*arrays)


class Place:
    def __init__(self):
        self.k_count = lax.axis_size("dp")
        self.s_count = lax.axis_size("seq")
        self.z_count = self.s_count // 2
        self.k = lax.axis_index("dp")
        self.s = lax.axis_index("seq")
        self.c = self.s % 2
        self.z = self.s // 2
        self.square = self.k_count == 4
        self.z_groups = [
            [k * self.s_count + 2 * z + c for z in range(self.z_count)]
            for k in range(self.k_count)
            for c in range(2)
        ]
        self.plane_groups = [
            [k * self.s_count + 2 * z + c for k in range(self.k_count) for c in range(2)]
            for z in range(self.z_count)
        ]

    def to_k(self, array, flip):
        return lax.ppermute(array, "dp", [(i, i ^ flip) for i in range(self.k_count)])

    def to_core(self, array):
        return lax.ppermute(array, "seq", [(i, i ^ 1) for i in range(self.s_count)])

    def to_z(self, array, by):
        pairs = [(i, i + 2 * by) for i in range(self.s_count) if 0 <= i + 2 * by < self.s_count]
        return lax.ppermute(array, "seq", pairs)

    def by_core(self, own, other):
        return jnp.where(self.c == 0, jnp.stack([own, other]), jnp.stack([other, own]))

    def gather_z(self, array):
        return lax.all_gather(array, AXES, axis_index_groups=self.z_groups, tiled=True)

    def z_pairs(self, pairs):
        return [(2 * a + c, 2 * b + c) for a, b in pairs for c in range(2)]

    def own_apart(self, split, axis):
        shape = [1] * split.ndim
        shape[axis] = self.z_count
        own = (jnp.arange(self.z_count) == self.z).reshape(shape)
        sent = jnp.moveaxis(jnp.where(own, 0.0, split).astype(low), axis, 0)
        kept = lax.dynamic_index_in_dim(split, self.z, axis, False)
        return sent.reshape((-1,) + sent.shape[-1:]), kept.reshape((-1,) + sent.shape[-1:])

    def scatter_z(self, parts):
        total = lax.psum_scatter(
            parts[0], AXES, scatter_dimension=0, axis_index_groups=self.z_groups, tiled=True
        )
        return total, parts[1]


    def sum_far(self, chunk):
        if self.z_count != 4:
            return ()
        pairs = self.z_pairs([(0, 1), (3, 2)])
        return (lax.ppermute(chunk(3 - self.z).astype(low), "seq", pairs),)

    def sum_near(self, chunk):
        if self.z_count != 4:
            return ()
        below = self.to_z(chunk(jnp.minimum(self.z + 1, 3)).astype(low), 1)
        above = self.to_z(chunk(jnp.maximum(self.z - 1, 0)).astype(low), -1)
        return below, above

    def sum_second(self, chunk, far):
        if self.z_count != 4:
            return ()
        second = (chunk(self.z ^ 2).astype(wide) + far[0].astype(wide)).astype(low)
        return (lax.ppermute(second, "seq", self.z_pairs([(0, 2), (1, 3), (2, 0), (3, 1)])),)

    def sum_all(self, sent, kept, near, second):
        total = kept.astype(wide)
        if self.z_count != 4:
            whole = lax.psum_scatter(
                sent.reshape(-1, sent.shape[-1]),
                AXES,
                scatter_dimension=0,
                axis_index_groups=self.z_groups,
                tiled=True,
            )
            return total + whole.astype(wide)
        for part in near + second:
            total = total + part.astype(wide)
        return total

    def gather_seq_small(self, array):
        if self.s_count != 8:
            return lax.all_gather(array, "seq")
        out = array[None]
        for bit in range(3):
            got = lax.ppermute(out, "seq", [(i, i ^ (1 << bit)) for i in range(8)])
            low_bit = (self.s >> bit) % 2 == 0
            out = jnp.where(low_bit, jnp.concatenate([out, got]), jnp.concatenate([got, out]))
        return out

    def gather_dp_small(self, array):
        if not self.square:
            return lax.all_gather(array, "dp")
        out = array[None]
        for bit in range(2):
            got = self.to_k(out, 1 << bit)
            low_bit = (self.k >> bit) % 2 == 0
            out = jnp.where(low_bit, jnp.concatenate([out, got]), jnp.concatenate([got, out]))
        return out

    def gather_plane(self, array):
        if not self.square:
            whole = lax.all_gather(array, AXES, axis_index_groups=self.plane_groups)
            whole = whole.reshape((self.k_count, 2) + array.shape)
            return jnp.swapaxes(whole, 0, 1).reshape((-1,) + array.shape[1:])
        return self.gather_end(self.gather_far(self.gather_near(array)))

    def gather_near(self, array):
        if not self.square:
            return (array,)
        return array, self.to_k(array, 1), self.to_k(array, 2)

    def gather_far(self, near):
        if not self.square:
            return near
        array, from_x, from_y = near
        half = array.shape[0] // 2
        return array, from_x, from_y, self.to_k(from_x[:half], 2), self.to_k(from_y[half:], 1)

    def gather_core(self, mine):
        if not self.square:
            return [self.gather_plane(mine[0])], None
        return list(mine), [self.to_core(part) for part in mine]

    def gather_end(self, mine):
        if not self.square:
            return self.gather_plane(mine[0])
        return lay_out(self.c, mine, [self.to_core(part) for part in mine])

    def gather_rows(self, array):
        if not self.square:
            return lax.all_gather(array, "dp", tiled=True)
        array = jnp.concatenate([array, self.to_k(array, 1)])
        return jnp.concatenate([array, self.to_k(array, 2)])

    def gather_plane_small(self, array):
        if not self.square:
            return self.gather_plane(array)
        near = jnp.stack([array, self.to_k(array, 1)])
        mine = jnp.concatenate([near, self.to_k(near, 2)])
        return self.by_core(mine, self.to_core(mine)).reshape((-1,) + array.shape[1:])

    def halves(self, array):
        count = array.shape[0] // 2
        own = lax.dynamic_slice_in_dim(array, self.c * count, count, 0)
        return own, lax.dynamic_slice_in_dim(array, (1 - self.c) * count, count, 0)

    def chip_product(self, left, right, dot, exact=False):
        own, other = self.halves(left)
        count = own.shape[0] // 2
        got = []
        for i in range(2):
            part = dot(other[i * count : (i + 1) * count], right)
            if exact:
                part = self.pack(part, self.power_of(part))
                got.append(self.unpack(self.to_core(part))[0])
            else:
                got.append(self.to_core(part.astype(low)).astype(wide))
        chip = []
        for i in range(2):
            part = dot(own[i * count : (i + 1) * count], right) + got[i]
            chip += list(part.reshape(self.k_count // 2, -1, part.shape[-1]))
        return chip

    def power_of(self, values):
        largest = jnp.max(jnp.abs(values), axis=-1, keepdims=True)
        return jnp.ceil(jnp.log2(jnp.clip(largest, 1e-30, 1e37)))

    def pack(self, parts, power):
        scaled = (parts * jnp.exp2(-power)).astype(jnp.float16)
        power = jnp.broadcast_to(power, power.shape[:-1] + (128,)).astype(jnp.float16)
        return jnp.concatenate([scaled, power], axis=-1)

    def unpack(self, got):
        got = got.astype(wide)
        width = got.shape[-1] - 128
        power = got[..., width : width + 1]
        return got[..., :width] * jnp.exp2(power), power

    def chip_send(self, left, right, side):
        if not self.square:
            return None, None
        other = other_call(self.c, left, right, left.shape[0] // 8, side)
        return other, self.to_core(other)

    def chip_own(self, left, right, got, side):
        if not self.square:
            return self.chip_product(left, right, dot_nt if side else dot_nn)
        return own_call(self.c, left, right, got, left.shape[0] // 8, side)

    def near_parts(self, parts):
        if not self.square:
            return self.near_plane(parts)
        chip, next_a, next_b, a, b = parts
        return (chip, next_a, next_b, *together(self.to_k(a, 1), self.to_k(b, 2)))

    def far_product(self, near):
        if not self.square:
            return self.far_plane(near)
        chip, next_a, next_b, got_a, got_b = near
        half = next_a.shape[1]
        got_a, got_b = got_a.astype(wide), got_b.astype(wide)
        own_a, own_b = chip[:, :half] + got_a[0], chip[:, half:] + got_b[0]
        return self.last_plane(next_a + got_a[1], next_b + got_b[1], None, None, own_a, own_b)

    def near_plane(self, chip, exact=False):
        if not self.square:
            return (lax.psum_scatter(jnp.stack(chip), "dp", scatter_dimension=0, tiled=False),)
        half = chip[0].shape[1] // 2
        power = [self.power_of(part) for part in chip] if exact else None

        def pick(a, i, j):
            return a if a is None else jnp.stack([a[i], a[j]])

        got_a = self.send_plane(jnp.stack([chip[1][:, :half], chip[3][:, :half]]), pick(power, 1, 3), 1)
        got_b = self.send_plane(jnp.stack([chip[2][:, half:], chip[3][:, half:]]), pick(power, 2, 3), 2)
        got_a, got_b = together(got_a, got_b)
        return chip, power, got_a, got_b

    def send_plane(self, parts, power, flip):
        if power is None:
            return self.to_k(parts.astype(low), flip), None
        return self.unpack(self.to_k(self.pack(parts, power), flip))

    def far_plane(self, near):
        if not self.square:
            return near[0]
        chip, power, (got_a, power_a), (got_b, power_b) = near
        half = chip[0].shape[1] // 2
        got_a, got_b = got_a.astype(wide), got_b.astype(wide)

        def above(a, i, b, j):
            return a if a is None else jnp.maximum(a[i], b[j]) + 1.0

        next_a, next_b = chip[2][:, :half] + got_a[1], chip[1][:, half:] + got_b[1]
        return self.last_plane(
            next_a,
            next_b,
            above(power_a, 1, power, 2),
            above(power_b, 1, power, 1),
            chip[0][:, :half] + got_a[0],
            chip[0][:, half:] + got_b[0],
        )

    def last_plane(self, next_a, next_b, power_a, power_b, own_a, own_b):
        if power_a is None:
            next_a, next_b = together(next_a.astype(low), next_b.astype(low))
            last_a, last_b = self.to_k(next_a, 2).astype(wide), self.to_k(next_b, 1).astype(wide)
        else:
            next_a, next_b = together(self.pack(next_a, power_a), self.pack(next_b, power_b))
            last_a, last_b = self.unpack(self.to_k(next_a, 2))[0], self.unpack(self.to_k(next_b, 1))[0]
        return jnp.concatenate([own_a + last_a, own_b + last_b], axis=1)

    def sum_plane(self, chip, exact=False):
        return self.far_plane(self.near_plane(chip, exact))

    def exchange_plane(self, array):
        return self.exchange_dp(self.exchange_core(array))

    def exchange_core(self, array):
        keep = lax.dynamic_index_in_dim(array, self.c, 1, False)
        got = self.to_core(lax.dynamic_index_in_dim(array, 1 - self.c, 1, False))
        return jnp.moveaxis(self.by_core(keep, got), 0, 1)

    def exchange_dp(self, pairs):
        if not self.square:
            return lax.all_to_all(pairs, "dp", 0, 0, tiled=True)
        parts = [lax.dynamic_index_in_dim(pairs, self.k, 0, False)]
        for flip in range(1, 4):
            parts.append(self.to_k(lax.dynamic_index_in_dim(pairs, self.k ^ flip, 0, False), flip))
        odd = self.k % 2 == 1
        parts = [jnp.where(odd, parts[i ^ 1], parts[i]) for i in range(4)]
        upper = self.k >= 2
        return jnp.stack([jnp.where(upper, parts[i ^ 2], parts[i]) for i in range(4)])


def gelu_pair(x):
    slope = 0.7978845608028654
    inner = jnp.tanh(slope * (x + 0.044715 * x * x * x))
    half = 0.5 * (1.0 + inner)
    return x * half, half + 0.5 * x * (1.0 - inner * inner) * slope * (1.0 + 0.134145 * x * x)


def rms_normed(values, gain):
    values = values.astype(wide)
    scale = lax.rsqrt(jnp.mean(values * values, axis=1, keepdims=True) + eps_value)
    return (values * scale * gain).astype(low)


def ordered(values, order):
    if order is None:
        return values
    size = values.shape[1] // len(order)
    return jnp.concatenate([values[:, i * size : (i + 1) * size] for i in order], axis=1)


def minus_expm1(x):
    near = 1.0
    for i in range(8, 1, -1):
        near = 1.0 + near * x * (1.0 / i)
    return jnp.where(x > -0.5, -x * near, 1.0 - jnp.exp(x))


def gates_of(conv_low, w_gates, params, not_start):
    width = conv_low.shape[1]
    pre = jnp.dot(conv_low, w_gates, preferred_element_type=wide)
    rate = jax.nn.sigmoid(pre[:, :width] + params[5:6])
    igate = jax.nn.sigmoid(pre[:, width:] + params[6:7])
    log_keep = params[7:8] * rate
    room = minus_expm1(2.0 * log_keep)
    mult = jnp.where(not_start > 0.5, jnp.sqrt(jnp.maximum(room, floor_value)), 1.0)
    return rate, igate, jnp.exp(log_keep), room, mult


def shifted(values, by, fill):
    count = values.shape[0]
    size = abs(by)
    if size % 8 == 0:
        free = jnp.full((size, values.shape[1]), fill, values.dtype)
        if by > 0:
            return jnp.concatenate([free, values[: count - size]])
        return jnp.concatenate([values[size:], free])
    place = lax.broadcasted_iota(jnp.int32, values.shape, 0)
    moved = pltpu.roll(values, by % count, 0)
    return jnp.where(place >= by if by > 0 else place < count - size, moved, fill)


def scan_rows(keep, drive, sign):
    by = 1
    while by < keep.shape[0]:
        drive = drive + keep * shifted(drive, sign * by, 0.0)
        keep = keep * shifted(keep, sign * by, 1.0)
        by *= 2
    return keep, drive


def conv_kernel(
    rows, span, order, x_ref, w_ref, halo_ref, gain_ref, params_ref, gates_ref,
    normed_ref, masks_ref, branch_ref, in_ref, low_ref, keep_ref, part_ref, run_ref, sums_ref, before_ref, tail, line, ends,
):
    step = pl.program_id(0)
    width = in_ref.shape[1]
    count = x_ref.shape[0]
    row_dev = count // span

    @pl.when(step == 0)
    def _():
        normed = rms_normed(halo_ref[...], gain_ref[...])
        before = jnp.dot(ordered(normed, order), w_ref[:, width:], preferred_element_type=wide)
        tail[...] = before.astype(low).astype(wide)
        before_ref[...] = tail[...]

    features = gain_ref.shape[1]
    normed = rms_normed(x_ref[:, :features], gain_ref[...])
    normed_ref[...] = normed
    masks_ref[...] = x_ref[:, features : features + 8].astype(wide)
    pre = jnp.dot(ordered(normed, order), w_ref[...], preferred_element_type=wide)
    branch_ref[...] = pre[:, :width]
    conv_in = pre[:, width:].astype(low)
    in_ref[...] = conv_in
    conv_in = conv_in.astype(wide)
    params = params_ref[...]
    for row in range(row_dev):
        at = slice(row * span, (row + 1) * span)
        own = conv_in[at]
        place = pl.ds(pl.multiple_of((lax.rem(step * row_dev + row, rows)) * 8, 8), 8)
        line[:8] = tail[place]
        line[8:] = own
        tail[place] = own[span - 8 :]
        masks = masks_ref[at]
        total = params[4:5] + params[0:1] * own
        for by in range(1, 4):
            total = total + params[by : by + 1] * line[8 - by : 8 - by + span] * masks[:, by - 1 : by]
        conv_low = total.astype(low)
        low_ref[at] = conv_low
        not_start = masks[:, 3:4]
        rate, igate, keep, room, mult = gates_of(conv_low, gates_ref[...], params, not_start)
        keep = keep * not_start
        keep_ref[at] = keep
        run, part = scan_rows(keep, mult * igate * conv_low.astype(wide), 1)

        @pl.when(step * row_dev < rows)
        def _(run=run, part=part, place=place, at=at):
            run_ref[at] = run
            part_ref[at] = part
            ends[0, place] = run[span - 8 :]
            ends[1, place] = part[span - 8 :]

        @pl.when(step * row_dev >= rows)
        def _(run=run, part=part, place=place, at=at):
            part = part + run * ends[1, place][7:8]
            run = run * ends[0, place][7:8]
            run_ref[at] = run
            part_ref[at] = part
            sums_ref[0, place] = run[span - 8 :]
            sums_ref[1, place] = part[span - 8 :]


def state_kernel(rows, span, part_ref, run_ref, start_ref, branch_ref, state_ref, mixed_ref):
    step = pl.program_id(0)
    row_dev = part_ref.shape[0] // span
    for row in range(row_dev):
        at = slice(row * span, (row + 1) * span)
        place = pl.ds(pl.multiple_of((lax.rem(step * row_dev + row, rows)) * 8, 8), 8)
        state = part_ref[at] + run_ref[at] * start_ref[place][7:8]
        state_ref[at] = state
        value, _ = gelu_pair(branch_ref[at])
        mixed_ref[at] = (value * state).astype(low)


def mlp_kernel(x_ref, cot_ref, w_ref, down_ref, hidden_ref, grad_ref):
    width = hidden_ref.shape[1]
    pre = jnp.dot(x_ref[...], w_ref[...], preferred_element_type=wide)
    grad = lax.dot_general(
        cot_ref[...], down_ref[...], (((1,), (1,)), ((), ())), preferred_element_type=wide
    )
    up = pre[:, width:]
    value, slope = gelu_pair(pre[:, :width])
    hidden_ref[...] = (value * up).astype(low)
    grad_ref[:, :width] = (grad * up * slope).astype(low)
    grad_ref[:, width:] = (grad * value).astype(low)


def other_kernel(side, core_ref, x_ref, w_ref, out_ref):
    product = lax.dot_general(
        x_ref[...], w_ref[...], (((1,), (side,)), ((), ())), preferred_element_type=wide
    )
    out_ref[...] = product.astype(low)


def own_kernel(side, core_ref, x_ref, w_ref, got_ref, chip_ref, next_a_ref, next_b_ref, a_ref, b_ref):
    step = pl.program_id(0)
    product = lax.dot_general(
        x_ref[...], w_ref[...], (((1,), (side,)), ((), ())), preferred_element_type=wide
    )
    product = product + got_ref[...].astype(wide)
    half = product.shape[1] // 2

    @pl.when(step == 0)
    def _():
        chip_ref[...] = product

    @pl.when(step == 1)
    def _():
        next_b_ref[...] = product[:, half:]

    @pl.when(step == 2)
    def _():
        next_a_ref[...] = product[:, :half]

    @pl.when((step == 1) | (step == 3))
    def _():
        a_ref[0] = product[:, :half].astype(low)

    @pl.when(step >= 2)
    def _():
        b_ref[0] = product[:, half:].astype(low)


def back_kernel(
    rows, span, x_ref, w_ref, branch_ref, state_ref, keep_ref, grad_branch_ref, part_ref, run_ref, sum_ref, ends
):
    step = pl.program_id(0)
    count = x_ref.shape[0]
    row_dev = count // span
    mixed = lax.dot_general(
        x_ref[...], w_ref[...], (((1,), (1,)), ((), ())), preferred_element_type=wide
    )
    late = step * row_dev < rows
    for row in range(row_dev):
        at = slice(row * span, (row + 1) * span)
        block = (pl.num_programs(0) - 1 - step) * row_dev + row
        place = pl.ds(pl.multiple_of(lax.rem(block, rows) * 8, 8), 8)
        value, slope = gelu_pair(branch_ref[at])
        grad_branch_ref[at] = (mixed[at] * state_ref[at] * slope).astype(low)
        grad = mixed[at] * value
        keep = keep_ref[at]
        run, part = scan_rows(keep, keep * grad, -1)

        @pl.when(late)
        def _(run=run, part=part, grad=grad, place=place, at=at):
            ends[0, place] = run[:8]
            ends[1, place] = part[:8]
            run_ref[at] = shifted(run, -1, 1.0)
            part_ref[at] = grad + shifted(part, -1, 0.0)

        @pl.when(jnp.logical_not(late))
        def _(run=run, part=part, grad=grad, place=place, at=at):
            next_run, next_part = ends[0, place][:1], ends[1, place][:1]
            part = part + run * next_part
            run = run * next_run
            last = lax.broadcasted_iota(jnp.int32, run.shape, 0) == span - 1
            run_ref[at] = jnp.where(last, next_run, shifted(run, -1, 1.0))
            part_ref[at] = grad + jnp.where(last, next_part, shifted(part, -1, 0.0))
            sum_ref[place] = part[:8]


def adjoint_kernel(
    rows, span, part_ref, run_ref, carry_ref, state_ref, start_ref, low_ref, gates_ref, params_ref,
    masks_ref, in_ref, before_ref, grad_conv_ref, small_ref, gates_grad_ref, sums_ref, line, ends, tail,
):
    step = pl.program_id(0)
    width = low_ref.shape[1]
    row_dev = low_ref.shape[0] // span
    params = params_ref[...]

    @pl.when(step == 0)
    def _():
        gates_grad_ref[...] = jnp.zeros(gates_grad_ref.shape, wide)
        sums_ref[...] = jnp.zeros(sums_ref.shape, wide)
        ends[...] = start_ref[...]
        tail[...] = before_ref[...]

    for row in range(row_dev):
        at = slice(row * span, (row + 1) * span)
        place = pl.ds(pl.multiple_of((lax.rem(step * row_dev + row, rows)) * 8, 8), 8)
        conv_low = low_ref[at]
        conv_value = conv_low.astype(wide)
        masks = masks_ref[at]
        not_start = masks[:, 3:4]
        rate, igate, keep, room, mult = gates_of(conv_low, gates_ref[...], params, not_start)
        adj = part_ref[at] + run_ref[at] * carry_ref[place][:1]
        state = state_ref[at]
        line[:8] = ends[place]
        line[8:] = state
        ends[place] = state[span - 8 :]
        through = adj * line[7 : 7 + span]
        spread = jnp.where(room > floor_value, adj * igate * conv_value * keep * keep / mult, 0.0)
        grad_log = not_start * (through * keep - spread)
        grad_rate = (grad_log * params[7:8] * rate * (1.0 - rate)).astype(low)
        scaled = adj * mult
        grad_igate = (scaled * conv_value * igate * (1.0 - igate)).astype(low)
        both = jnp.concatenate([grad_rate, grad_igate], axis=1)
        grad_conv = scaled * igate + lax.dot_general(
            both, gates_ref[...], (((1,), (1,)), ((), ())), preferred_element_type=wide
        )
        grad_conv = grad_conv.astype(low)
        grad_conv_ref[at] = grad_conv
        gates_grad_ref[...] += lax.dot_general(
            conv_low, both, (((0,), (0,)), ((), ())), preferred_element_type=wide
        )
        grad_conv = grad_conv.astype(wide)
        conv_in = in_ref[at].astype(wide)
        line[:8] = tail[place]
        line[8:] = conv_in
        tail[place] = conv_in[span - 8 :]
        values = [grad_conv * conv_in]
        for by in range(1, 4):
            values.append(grad_conv * line[8 - by : 8 - by + span] * masks[:, by - 1 : by])
        values += [grad_conv, grad_rate.astype(wide), grad_igate.astype(wide), grad_log * rate * params[8:9]]
        for i, value in enumerate(values):
            sums_ref[i : i + 1] += jnp.sum(value, axis=0, keepdims=True)

    @pl.when(step == pl.num_programs(0) - 1)
    def _():
        block = small_ref.shape[1] // 2 - 64
        for head in range(width // block):
            at = slice(head * block, (head + 1) * block)
            small_ref[at, :block] = gates_grad_ref[at, at].astype(low)
            then = slice(width + head * block, width + (head + 1) * block)
            small_ref[at, block : 2 * block] = gates_grad_ref[at, then].astype(low)
        small_ref[:, 2 * block :] = sums_ref[...].T[:width].astype(low)


def conv_back_kernel(rows, span, grad_ref, halo_ref, masks_ref, halo_masks_ref, branch_ref, params_ref, one_ref, line):
    params = params_ref[...]

    def work(block, grad_next, masks_next):
        at = pl.ds(pl.multiple_of(block * span, 16), span)
        own = grad_ref[at].astype(wide)
        total = params[0:1] * own
        masks = masks_ref[at]
        for by in range(1, 4):
            line[:span] = own * masks[:, by - 1 : by]
            line[span:] = grad_next * masks_next[:, by - 1 : by]
            total = total + params[by : by + 1] * line[by : by + span]
        width = branch_ref.shape[1]
        one_ref[at, :width] = branch_ref[at]
        one_ref[at, width:] = total.astype(low)

    @pl.loop(0, rows)
    def _(block):
        then = pl.ds(pl.multiple_of((block + rows) * span, 16), 16)
        work(block, grad_ref[then].astype(wide)[:8], masks_ref[then][:8])

    @pl.loop(0, rows)
    def _(block):
        then = pl.ds(pl.multiple_of(block * 16, 16), 16)
        work(block + rows, halo_ref[then].astype(wide)[:8], halo_masks_ref[then][:8])


def whole_block(array):
    return pl.BlockSpec(array.shape, lambda *i, n=len(array.shape): (0,) * n)


def token_block(array, count, steps, backwards):
    def index(i):
        return (steps - 1 - i if backwards else i,) + (0,) * (len(array.shape) - 1)

    return pl.BlockSpec((count,) + array.shape[1:], index)


def half_of(core, x, count, width):
    return pl.BlockSpec((count, width), lambda k, core_ref: (core_ref[0] * (x.shape[0] // (2 * count)) + k, 0))


def half_call(kernel, core, x, w, count, extra, outputs):
    def spec(array, block, index):
        return pl.BlockSpec(block, lambda k, core_ref: index(k))

    return pl.pallas_call(
        kernel,
        out_shape=[array for array, _, _ in outputs],
        grid_spec=pltpu.PrefetchScalarGridSpec(
            num_scalar_prefetch=1,
            grid=(x.shape[0] // (2 * count),),
            in_specs=[
                half_of(core, x, count, x.shape[1]),
                pl.BlockSpec(w.shape, lambda k, core_ref: (0, 0)),
            ]
            + [spec(*one) for one in extra],
            out_specs=[spec(*one) for one in outputs],
        ),
        cost_estimate=pl.CostEstimate(flops=0, bytes_accessed=0, transcendentals=0),
        compiler_params=pltpu.CompilerParams(vmem_limit_bytes=60 * 2**20),
    )(core.reshape(1).astype(jnp.int32), x, w, *[array for array, _, _ in extra])


def other_call(core, x, w, count, side):
    width = w.shape[1 - side]
    out = jax.ShapeDtypeStruct((x.shape[0] // 2, width), low)
    kernel = functools.partial(other_kernel, side)
    return half_call(kernel, 1 - core, x, w, count, [], [(out, (count, width), lambda k: (k, 0))])[0]


def own_call(core, x, w, got, count, side):
    width = w.shape[1 - side]
    a = jax.ShapeDtypeStruct((2, count, width // 2), low)
    chip = jax.ShapeDtypeStruct((count, width), wide)
    after = jax.ShapeDtypeStruct((count, width // 2), wide)
    return half_call(
        functools.partial(own_kernel, side),
        core,
        x,
        w,
        count,
        [(got, (count, width), lambda k: (k, 0))],
        [
            (chip, chip.shape, lambda k: (0, 0)),
            (after, after.shape, lambda k: (0, 0)),
            (after, after.shape, lambda k: (0, 0)),
            (a, (1, count, width // 2), lambda k: (k // 2, 0, 0)),
            (a, (1, count, width // 2), lambda k: (k // 3, 0, 0)),
        ],
    )


def rows_kernel(core_ref, x_ref, grad_ref, sent_ref, kept_ref):
    count = kept_ref.shape[1]
    total = lax.dot_general(
        x_ref[...], grad_ref[...], (((0,), (0,)), ((), ())), preferred_element_type=wide
    )
    planes = sent_ref.shape[0]
    first = lax.rem(pl.program_id(0), core_ref[1]) * planes
    for i in range(planes):
        part = total[i * count : (i + 1) * count]
        mine = first + i == core_ref[0]
        sent_ref[i, 0] = jnp.where(mine, jnp.zeros_like(part), part).astype(low)

        @pl.when(mine)
        def _(part=part):
            kept_ref[0] = part


def rows_call(z, z_count, k_count, x, grad):
    tokens, features = x.shape
    count = features // (z_count * k_count)
    planes = max(2, 128 // count)
    width = grad.shape[1]
    per = z_count // planes
    sent = jax.ShapeDtypeStruct((z_count, k_count, count, width), low)
    kept = jax.ShapeDtypeStruct((k_count, count, width), wide)
    return pl.pallas_call(
        rows_kernel,
        out_shape=[sent, kept],
        grid_spec=pltpu.PrefetchScalarGridSpec(
            num_scalar_prefetch=1,
            grid=(k_count * per,),
            in_specs=[
                pl.BlockSpec((tokens, planes * count), lambda i, ref: (0, i)),
                pl.BlockSpec(grad.shape, lambda i, ref: (0, 0)),
            ],
            out_specs=[
                pl.BlockSpec((planes, 1, count, width), lambda i, ref: (i % per, i // per, 0, 0)),
                pl.BlockSpec((1, count, width), lambda i, ref: (i // per, 0, 0)),
            ],
        ),
        cost_estimate=pl.CostEstimate(flops=0, bytes_accessed=0, transcendentals=0),
        compiler_params=pltpu.CompilerParams(vmem_limit_bytes=60 * 2**20),
    )(jnp.stack([z, jnp.int32(per)]).astype(jnp.int32), x, grad)


def down_kernel(core_ref, hidden_ref, cot_ref, sent_ref, kept_ref):
    total = lax.dot_general(
        cot_ref[...], hidden_ref[...], (((0,), (0,)), ((), ())), preferred_element_type=wide
    )
    total = total.T
    count = kept_ref.shape[0]
    for i in range(sent_ref.shape[0]):
        part = total[i * count : (i + 1) * count]
        mine = core_ref[0] == i
        sent_ref[i] = jnp.where(mine, jnp.zeros_like(part), part).astype(low)

        @pl.when(mine)
        def _(part=part):
            kept_ref[...] = part


def down_call(z, z_count, hidden, cot):
    tokens, features = cot.shape
    count = hidden.shape[1] // z_count
    columns = 256
    sent = jax.ShapeDtypeStruct((z_count, count, features), low)
    kept = jax.ShapeDtypeStruct((count, features), wide)
    return pl.pallas_call(
        down_kernel,
        out_shape=[sent, kept],
        grid_spec=pltpu.PrefetchScalarGridSpec(
            num_scalar_prefetch=1,
            grid=(features // columns,),
            in_specs=[
                pl.BlockSpec(hidden.shape, lambda i, ref: (0, 0)),
                pl.BlockSpec((tokens, columns), lambda i, ref: (0, i)),
            ],
            out_specs=[
                pl.BlockSpec((z_count, count, columns), lambda i, ref: (0, 0, i)),
                pl.BlockSpec((count, columns), lambda i, ref: (0, i)),
            ],
        ),
        cost_estimate=pl.CostEstimate(flops=0, bytes_accessed=0, transcendentals=0),
        compiler_params=pltpu.CompilerParams(vmem_limit_bytes=60 * 2**20),
    )(z.reshape(1).astype(jnp.int32), hidden, cot)


def kernel_call(kernel, steps, inputs, outputs, scratch=(), backwards=False):
    def spec(array, count):
        return whole_block(array) if count is None else token_block(array, count, steps, backwards)

    return pl.pallas_call(
        kernel,
        out_shape=[array for array, _ in outputs],
        grid=(steps,),
        in_specs=[spec(array, count) for array, count in inputs],
        out_specs=[spec(array, count) for array, count in outputs],
        scratch_shapes=scratch,
        cost_estimate=pl.CostEstimate(flops=0, bytes_accessed=0, transcendentals=0),
        compiler_params=pltpu.CompilerParams(vmem_limit_bytes=60 * 2**20),
    )(*[array for array, _ in inputs])


def gathered_kernel(kernel, parts, steps, backwards, keep, given, core_ref, *refs):
    own, other = refs[:parts], refs[parts : 2 * parts]
    refs = refs[2 * parts :]
    inputs, refs = refs[:given], refs[given:]
    out_ref, refs = (refs[0], refs[1:]) if keep else (None, refs)
    buffer, sem, out_sem = refs[-3:]
    half = buffer.shape[0] // 2
    count = buffer.shape[0] // steps
    step = pl.program_id(0)
    block = steps - 1 - step if backwards else step

    @pl.when(step == 0)
    def _():
        for which, group in enumerate((own, other)):
            side = core_ref[0] if which == 0 else 1 - core_ref[0]
            start = 0
            for i, part in enumerate(group):
                to = pl.ds(pl.multiple_of(side * half + start, 16), part.shape[0])
                pltpu.make_async_copy(part, buffer.at[to], sem.at[side * parts + i]).start()
                start = start + part.shape[0]

    at = pl.ds(pl.multiple_of(block * count, 16), count)
    side = block // (steps // 2)
    place = lax.rem(block, steps // 2)
    whole = steps // 2 - 1

    @pl.when(place < whole)
    def _():
        pltpu.make_async_copy(buffer.at[at], buffer.at[at], sem.at[side * parts + place]).wait()

    @pl.when(place == whole)
    def _():
        for i in range(whole, parts):
            to = pl.ds(pl.multiple_of(block * count, 16), own[i].shape[0])
            pltpu.make_async_copy(buffer.at[to], buffer.at[to], sem.at[side * parts + i]).wait()

    if keep:
        pltpu.make_async_copy(buffer.at[at], out_ref.at[at], out_sem.at[block]).start()
    kernel(buffer.at[at], *inputs, *refs[:-3])
    if keep:

        @pl.when(step == steps - 1)
        def _():
            for i in range(steps):
                to = pl.ds(i * count, count)
                pltpu.make_async_copy(buffer.at[to], out_ref.at[to], out_sem.at[i]).wait()


def gathered_call(kernel, core, gathered, steps, inputs, outputs, scratch=(), backwards=False, keep=True, cost=0):
    own, other = gathered
    if other is None:
        count = own[0].shape[0] // steps
        results = kernel_call(kernel, steps, [(own[0], count)] + inputs, outputs, scratch, backwards)
        return ([own[0]] if keep else []) + list(results)

    def spec(array, count):
        return whole_block(array) if count is None else token_block(array, count, steps, backwards)

    anywhere = pl.BlockSpec(memory_space=pl.ANY)
    tokens = jax.ShapeDtypeStruct((2 * sum(p.shape[0] for p in own),) + own[0].shape[1:], own[0].dtype)
    return pl.pallas_call(
        functools.partial(gathered_kernel, kernel, len(own), steps, backwards, keep, len(inputs)),
        out_shape=([tokens] if keep else []) + [array for array, _ in outputs],
        grid=(steps,),
        in_specs=[pl.BlockSpec(memory_space=pltpu.SMEM)]
        + [anywhere] * (2 * len(own))
        + [spec(array, count) for array, count in inputs],
        out_specs=([anywhere] if keep else []) + [spec(array, count) for array, count in outputs],
        scratch_shapes=list(scratch)
        + [
            pltpu.VMEM(tokens.shape, tokens.dtype),
            pltpu.SemaphoreType.DMA((2 * len(own),)),
            pltpu.SemaphoreType.DMA((steps,)),
        ],
        cost_estimate=pl.CostEstimate(flops=0, bytes_accessed=cost << 20, transcendentals=0),
        compiler_params=pltpu.CompilerParams(vmem_limit_bytes=60 * 2**20),
    )(core.reshape(1).astype(jnp.int32), *own, *other, *[array for array, _ in inputs])


def per_device(
    tokens,
    segment_ids,
    cotangent,
    norm_one,
    branch_weight,
    input_proj,
    conv_weight,
    conv_bias,
    rate_weight,
    igate_weight,
    rate_bias,
    igate_bias,
    decay_param,
    out_proj,
    norm_two,
    mlp_gate,
    mlp_up,
    mlp_down,
):
    at = Place()
    k_count, z_count = at.k_count, at.z_count
    group = 2 * k_count
    row_dev, span, width_d = tokens.shape
    tok = row_dev * span
    rows = k_count * row_dev
    tok_all = 2 * rows * span
    d_own = norm_one.shape[0]
    w_own = conv_bias.shape[0]
    f_own = mlp_down.shape[0]
    width_r = branch_weight.shape[1]
    w_slot = width_r // group
    f_slot = f_own * z_count
    taps = conv_weight.shape[0]
    reach = taps - 1
    half_z = z_count // 2

    def by_feature(array):
        split = array.reshape(z_count, -1, 2 * d_own, array.shape[1])
        return jnp.swapaxes(split, 0, 1).reshape(array.shape)

    small = jnp.concatenate(
        [
            norm_one,
            norm_two,
            conv_weight.reshape(-1),
            conv_bias,
            rate_bias,
            igate_bias,
            decay_param,
        ]
    )
    rec_cols = jnp.concatenate(
        [
            branch_weight.reshape(d_own, k_count, 2, w_slot),
            input_proj.reshape(d_own, k_count, 2, w_slot),
        ],
        axis=3,
    )
    rec_pairs = at.exchange_core(jnp.moveaxis(rec_cols, 0, 2))

    seg_code = (segment_ids % 64).astype(low)
    pairs = [(i, i + 1) for i in range(at.s_count - 1)]
    before = lax.ppermute(seg_code[:, span - reach :], "seq", pairs)
    tokens = tokens.reshape(tok, width_d)
    tail = tokens.reshape(row_dev, span, width_d)[:, span - 8 :].reshape(row_dev * 8, width_d)
    tail = at.to_z(tail, 1)

    small = jnp.pad(small, (0, -small.shape[0] % 128)).reshape(-1, 128)
    small_rows = small.shape[0]
    small = jnp.pad(small, ((0, w_own - small_rows), (0, 0)))
    out_rows = jnp.concatenate([out_proj, rate_weight, igate_weight, small], axis=1)
    out_rows, before, tail = together(out_rows, before, tail)
    out_part = at.gather_z(out_rows)

    rec_cols = at.exchange_dp(rec_pairs)
    order = None
    if 2 * d_own % 128 == 0:
        order = [k * z_count + z for z in range(z_count) for k in range(k_count)]
    ext_code = jnp.concatenate([before, seg_code], axis=1)
    position = lax.broadcasted_iota(jnp.int32, (row_dev, span), 1)
    masks = [
        (ext_code[:, reach - by : reach - by + span] == seg_code) & ((at.s > 0) | (position >= by))
        for by in range(1, taps)
    ]
    masks = jnp.stack(masks + [masks[0]] * (9 - taps), axis=-1).astype(low).reshape(tok, 8)
    beside = jnp.concatenate([tokens, jnp.pad(masks, ((0, 0), (0, 120)))], axis=1)
    beside, rec_cols = together(beside, rec_cols)
    w1 = at.gather_z(rec_cols.reshape(group * d_own, 2 * w_slot))
    beside_near = at.gather_near(beside)
    tail = jnp.where(at.c == 1, tail, at.to_core(tail))
    inputs = tokens.astype(wide)
    s1 = lax.rsqrt(jnp.mean(inputs * inputs, axis=-1, keepdims=True) + eps_value)
    mlp_shape = jax.ShapeDtypeStruct((k_count, 2, d_own, 2 * f_slot), low)
    cut = functools.partial(cut_kernel, k_count, z_count)
    mlp_pairs = at.exchange_core(in_vmem(cut, (mlp_gate, mlp_up), mlp_shape))
    beside_near, tail, mlp_pairs, out_part = together(beside_near, tail, mlp_pairs, out_part)
    tail = at.gather_rows(tail)

    out_split = out_part.reshape(2, half_z, w_own, -1)

    def of_slot(columns):
        part = out_split[..., columns]
        keep = lax.dynamic_index_in_dim(part, at.c, 0, False)
        got = at.to_core(lax.dynamic_index_in_dim(part, 1 - at.c, 0, False))
        return jnp.swapaxes(at.by_core(keep, got), 0, 1).reshape(w_slot, -1)

    gate_rows = of_slot(slice(width_d, width_d + 2 * BS))
    small = out_part.reshape(z_count, w_own, -1)[:, :small_rows, width_d + 2 * BS :].reshape(z_count, -1)
    small = jnp.swapaxes(at.by_core(small, at.to_core(small)), 0, 1).reshape(at.s_count, -1)
    gains = at.gather_dp_small(small[:, : 2 * d_own]).reshape(k_count * at.s_count, -1)
    mine = lax.dynamic_slice_in_dim(small[:, 2 * d_own :], at.c * z_count, z_count, 0)
    mine = mine[:, : (taps + 4) * w_own].reshape(z_count, taps + 4, w_own).astype(wide)
    mine = jnp.swapaxes(mine, 0, 1).reshape(taps + 4, w_slot)
    w_conv = mine[:taps]
    b_conv, b_rate, b_igate, decay = (mine[taps + i][None, :] for i in range(4))
    log_slope = -rate_scale * jax.nn.softplus(-decay)
    decay_slope = rate_scale * jax.nn.sigmoid(-decay)
    params = jnp.concatenate([w_conv, b_conv, b_rate, b_igate, log_slope] + [decay_slope] * 8)
    beside_near, tail, gains, gate_rows = together(beside_near, tail, gains, gate_rows)
    heads = w_slot // BS

    def block_diagonal(columns):
        blocks = columns.reshape(heads, BS, 1, BS)
        same = jnp.eye(heads, dtype=low).reshape(heads, 1, heads, 1)
        return (blocks * same).reshape(w_slot, w_slot)

    w_gates = jnp.concatenate([block_diagonal(gate_rows[:, :BS]), block_diagonal(gate_rows[:, BS:])], axis=1)

    beside_far, mlp_pairs, w_gates, params = together(
        at.gather_far(beside_near), mlp_pairs, w_gates, params
    )
    gain_one = gains[:, :d_own].reshape(1, width_d).astype(wide)
    gain_two = gains[:, d_own:].reshape(1, width_d).astype(wide)
    mlp_cols = at.exchange_dp(mlp_pairs)
    cot = cotangent.reshape(tok, width_d)
    tokens_parts, mlp_cols, cot = together(at.gather_core(beside_far), mlp_cols, cot)
    shape = jax.ShapeDtypeStruct

    half_rows = group * d_own // 2
    w2_parts = [
        at.gather_z(part.reshape(half_rows, 2 * f_slot))
        for part in (mlp_cols[: k_count // 2], mlp_cols[k_count // 2 :])
    ]

    steps = tok_all // tok
    cot_near = at.gather_near(cot)
    flat32, flat16 = shape((tok_all, w_slot), wide), shape((tok_all, w_slot), low)
    ends = shape((rows * 8, w_slot), wide)

    def by_row(array):
        return jnp.repeat(array, 8, axis=0)

    n1_all, masks, branch_pre, conv_in, conv_low, keep_eff, part, run, summary, conv_before = gathered_call(
        functools.partial(conv_kernel, rows, span, order),
        at.c,
        tokens_parts,
        steps,
        [(w1 if order else by_feature(w1), None), (tail, None), (gain_one, None), (params, None), (w_gates, None)],
        [(shape((tok_all, width_d), low), tok), (shape((tok_all, 8), wide), tok), (flat32, tok), (flat16, tok), (flat16, tok)]
        + [(flat32, tok)] * 3
        + [(shape((2,) + ends.shape, wide), None), (ends, None)],
        [
            pltpu.VMEM(ends.shape, wide),
            pltpu.VMEM((span + 8, w_slot), wide),
            pltpu.VMEM((2,) + ends.shape, wide),
        ],
        keep=False,
    )
    summary = summary.reshape(2, rows, 8, w_slot)[:, :, 7]
    w_down = at.gather_z(mlp_down)
    summary, cot_near, out_split, w1 = together(summary, cot_near, out_split, w1)
    w1 = by_feature(w1)
    w_out = of_slot(slice(0, width_d))
    cot_far = at.gather_far(cot_near)
    before = [at.to_z(summary, by) for by in range(1, z_count)]
    state_in = jnp.zeros((rows, w_slot), wide)
    for one in reversed(before):
        state_in = one[1] + one[0] * state_in
    state_in = by_row(state_in)
    state, mixed = kernel_call(
        functools.partial(state_kernel, rows, span),
        steps,
        [(part, tok), (run, tok), (state_in, None), (branch_pre, tok)],
        [(flat32, tok), (flat16, tok)],
    )
    masks_after = at.to_z(masks.reshape(2, rows, span, 8)[0, :, :16], -1).reshape(rows * 16, 8)
    mixed, cot_far, w2_parts[0], masks_after, w1 = together(mixed, cot_far, w2_parts[0], masks_after, w1)

    chip_one = at.chip_product(mixed, w_out, dot_nn, exact=True)
    near_sum, cot_far = together(at.near_plane(chip_one, exact=True), cot_far)
    cot_all = at.gather_end(cot_far)
    resid = inputs + at.far_plane(near_sum)
    resid, w2_parts[1] = together(resid, w2_parts[1])
    w2 = jnp.concatenate([by_feature(part) for part in w2_parts])

    s2 = lax.rsqrt(jnp.mean(resid * resid, axis=-1, keepdims=True) + eps_value)
    normed_two = (resid * s2 * gain_two).astype(low)
    n2_near, w2, cot_all = together(at.gather_near(normed_two), w2, cot_all)
    n2_parts, w_down = together(at.gather_core(at.gather_far(n2_near)), w_down)
    n2_all, hidden, grad_two = gathered_call(
        mlp_kernel,
        at.c,
        n2_parts,
        steps,
        [(cot_all, tok), (w2, None), (w_down, None)],
        [(shape((tok_all, f_slot), low), tok), (shape((tok_all, 2 * f_slot), low), tok)],
    )
    def rows_apart(x, grad):
        sent, kept = rows_call(at.z, z_count, k_count, x, grad)
        return sent.reshape(-1, sent.shape[-1]), kept.reshape(-1, kept.shape[-1])

    _, got_two = at.chip_send(grad_two, w2, 1)
    near_two = at.near_parts(at.chip_own(grad_two, w2, got_two, 1))
    chip_two, grad_two = together(near_two[0], grad_two)
    w2_part = rows_apart(n2_all, grad_two)
    near_two, w2_part, hidden = together(near_two, w2_part, hidden)
    w2_sum = at.scatter_z(w2_part)
    grad_n2 = at.far_product(near_two)
    other_three, got_three = at.chip_send(hidden, w_down, 0)
    grad_n2, other_three, hidden = together(grad_n2, other_three, hidden)
    scaled_two = gain_two * grad_n2
    cot_f = cot.astype(wide)
    mean_two = jnp.mean(scaled_two * resid, axis=-1, keepdims=True)
    grad_resid = cot_f + s2 * scaled_two - resid * (s2 * s2 * s2) * mean_two
    grad_recur = grad_resid.astype(low)
    grad_recur, hidden = together(grad_recur, hidden)
    chip_three = at.chip_own(hidden, w_down, got_three, 0)
    down_sent, down_kept = down_call(at.z, z_count, hidden, cot_all)
    down_part = down_sent.reshape(-1, width_d), down_kept
    gr_near, chip_three, down_part = together(at.gather_near(grad_recur), chip_three, down_part)
    down_sum = at.scatter_z(down_part)
    gr_parts, chip_three = together(at.gather_core(at.gather_far(gr_near)), chip_three)

    def summed(pair):
        return pair[0].astype(wide) + pair[1].astype(wide)

    def to_owner(array, columns):
        return at.exchange_plane(array.reshape(k_count, 2, d_own, columns))


    gr_all, grad_branch, back_part, back_run, back = gathered_call(
        functools.partial(back_kernel, rows, span),
        at.c,
        gr_parts,
        steps,
        [(w_out, None), (branch_pre, tok), (state, tok), (keep_eff, tok)],
        [(flat16, tok), (flat32, tok), (flat32, tok), (ends, None)],
        [pltpu.VMEM((2,) + ends.shape, wide)],
        backwards=True,
        cost=70,
    )
    back = back.reshape(rows, 8, w_slot)[:, 0]
    back, mixed, near_three = together(back, mixed, at.near_parts(chip_three))

    def by_owner(array):
        split = array.reshape(half_z, 2, w_own, -1)
        keep = lax.dynamic_index_in_dim(split, at.c, 1, False)
        got = at.to_core(lax.dynamic_index_in_dim(split, 1 - at.c, 1, False))
        return at.by_core(keep, got).reshape(z_count, w_own, -1)

    own = jnp.stack([summary[0], back])
    after = [at.to_z(own, -by) for by in range(1, z_count)]
    grad_out = dot_tn(mixed, gr_all)
    after, grad_out, w2_sum = together(after, grad_out, w2_sum)
    carry_in = jnp.zeros((rows, w_slot), wide)
    for part in reversed(after):
        carry_in = part[1] + part[0] * carry_in
    mlp_pairs = at.exchange_core(summed(w2_sum).reshape(k_count, 2, d_own, 2 * f_slot))
    carry_in, mlp_pairs = together(carry_in, mlp_pairs)
    mlp_back = at.exchange_dp(mlp_pairs)
    grad_conv, rec_small = kernel_call(
        functools.partial(adjoint_kernel, rows, span),
        steps,
        [
            (back_part, tok),
            (back_run, tok),
            (by_row(carry_in), None),
            (state, tok),
            (state_in, None),
            (conv_low, tok),
            (w_gates, None),
            (params, None),
            (masks, tok),
            (conv_in, tok),
            (conv_before, None),
        ],
        [(flat16, tok), (shape((w_slot, 2 * BS + 128), low), None)],
        [
            pltpu.VMEM((w_slot, 2 * w_slot), wide),
            pltpu.VMEM((128, w_slot), wide),
            pltpu.VMEM((span + 8, w_slot), wide),
            pltpu.VMEM(ends.shape, wide),
            pltpu.VMEM(ends.shape, wide),
        ],
    )
    grad_conv, near_three, mlp_back = together(grad_conv, near_three, mlp_back)
    block_out = (resid + at.far_product(near_three)).astype(low)
    head = at.to_z(grad_conv.reshape(2, rows, span, w_slot)[0, :, :16], -1).reshape(rows * 16, w_slot)
    rec_part = at.own_apart(by_owner(jnp.concatenate([grad_out.astype(low), rec_small], axis=1)), 0)
    head, rec_part = together(head, rec_part)
    rec_sum = at.scatter_z(rec_part)
    (grad_one,) = kernel_call(
        functools.partial(conv_back_kernel, rows, span),
        1,
        [(array, None) for array in (grad_conv, head, masks, masks_after, grad_branch, params)],
        [(shape((tok_all, 2 * w_slot), low), None)],
        [pltpu.VMEM((span + 8, w_slot), wide)],
    )

    grad_one, block_out = together(grad_one, block_out)
    other_one, got_one = at.chip_send(grad_one, w1, 1)
    other_one, then = together(other_one, grad_one)
    w1_part = rows_apart(n1_all, then)
    then, w1_part = together(then, w1_part)
    near_one = at.near_parts(at.chip_own(then, w1, got_one, 1))
    w1_sum = at.scatter_z(w1_part)
    mlp_whole = jax.ShapeDtypeStruct(mlp_gate.shape, wide)
    join = functools.partial(join_kernel, k_count, z_count)
    grad_gate_w, grad_up_w = in_vmem(join, (mlp_back,), (mlp_whole, mlp_whole))
    near_one, grad_gate_w, grad_up_w, down_sum = together(near_one, grad_gate_w, grad_up_w, down_sum)
    grad_n1 = at.far_product(near_one)
    w1_sum, grad_n1, rec_sum = together(w1_sum, grad_n1, rec_sum)
    rec_pairs = at.exchange_core(summed(w1_sum).reshape(k_count, 2, d_own, 2 * w_slot))
    rec_pairs, grad_n1, rec_sum = together(rec_pairs, grad_n1, rec_sum)
    rec_back = at.exchange_dp(rec_pairs)
    scaled_one = gain_one * grad_n1
    mean_one = jnp.mean(scaled_one * inputs, axis=-1, keepdims=True)
    grad_tokens = grad_resid + s1 * scaled_one - inputs * (s1 * s1 * s1) * mean_one
    grad_tokens = grad_tokens.reshape(row_dev, span, width_d)
    block_out = block_out.reshape(row_dev, span, width_d)

    rec_rows = summed(rec_sum)
    grad_out_w = rec_rows[:, :width_d]
    grad_rate_w = rec_rows[:, width_d : width_d + BS]
    grad_igate_w = rec_rows[:, width_d + BS : width_d + 2 * BS]
    grad_small = rec_rows[:, width_d + 2 * BS : width_d + 2 * BS + taps + 4].T
    grad_down = summed(down_sum)
    rec_back = jnp.moveaxis(rec_back, 2, 0)
    grad_branch_w = rec_back[..., :w_slot].reshape(d_own, width_r)
    grad_input_w = rec_back[..., w_slot:].reshape(d_own, width_r)

    def gain_grad(pairs, gain):
        total = sum(jnp.sum(weight.astype(wide) * grad, axis=1) for weight, grad in pairs)
        return total / gain.astype(wide)

    grad_norm_one = gain_grad(((branch_weight, grad_branch_w), (input_proj, grad_input_w)), norm_one)
    grad_norm_two = gain_grad(((mlp_gate, grad_gate_w), (mlp_up, grad_up_w)), norm_two)
    return (
        block_out,
        grad_tokens,
        grad_norm_one,
        grad_branch_w,
        grad_input_w,
        grad_small[:taps],
        grad_small[taps],
        grad_rate_w,
        grad_igate_w,
        grad_small[taps + 1],
        grad_small[taps + 2],
        grad_small[taps + 3],
        grad_out_w,
        grad_norm_two,
        grad_gate_w,
        grad_up_w,
        grad_down,
    )


def solution(mesh):
    rows, matrix = P(AXES), P(AXES, None)
    tokens = P("dp", "seq", None)
    return jax.shard_map(
        per_device,
        mesh=mesh,
        in_specs=(
            tokens,
            P("dp", "seq"),
            tokens,
            rows,
            matrix,
            matrix,
            P(None, AXES),
            rows,
            matrix,
            matrix,
            rows,
            rows,
            rows,
            matrix,
            rows,
            matrix,
            matrix,
            matrix,
        ),
        out_specs=(
            tokens,
            tokens,
            rows,
            matrix,
            matrix,
            P(None, AXES),
            rows,
            matrix,
            matrix,
            rows,
            rows,
            rows,
            matrix,
            rows,
            matrix,
            matrix,
            matrix,
        ),
        check_vma=False,
    )
```

```python
import functools

import jax
import jax.numpy as jnp
from jax import lax
from jax.experimental import pallas as pl
from jax.experimental.pallas import tpu as pltpu
from jax.sharding import PartitionSpec as P

HEADS = 16
BS = 160
AXES = ("dp", "seq")

eps_value = 1e-06
rate_scale = 8.0
floor_value = 0.001
low = jnp.bfloat16
wide = jnp.float32


def gelu_tanh(value):
    return jax.nn.gelu(value, approximate=True)


def dot_nn(left, right):
    return lax.dot_general(left, right, (((1,), (0,)), ((), ())), preferred_element_type=wide)


def dot_nt(left, right):
    return lax.dot_general(left, right, (((1,), (1,)), ((), ())), preferred_element_type=wide)


def dot_tn(left, right):
    return lax.dot_general(left, right, (((0,), (0,)), ((), ())), preferred_element_type=wide)


def lay_out_kernel(count, c_ref, *refs):
    parts, (out_ref, buffer, sem, out_sem) = refs[: 2 * count], refs[2 * count :]
    core = c_ref[0]
    copies = []
    for which in range(2):
        start = (core if which == 0 else 1 - core) * (out_ref.shape[0] // 2)
        for i, part in enumerate(parts[which * count : (which + 1) * count]):
            at = pl.ds(pl.multiple_of(start, 16), part.shape[0])
            j = which * count + i
            into = pltpu.make_async_copy(part, buffer.at[at], sem.at[j])
            into.start()
            copies.append((into, pltpu.make_async_copy(buffer.at[at], out_ref.at[at], out_sem.at[j])))
            start = start + part.shape[0]
    for into, out in copies:
        into.wait()
        out.start()
    for into, out in copies:
        out.wait()


def lay_out(core, own, other):
    rows = 2 * sum(part.shape[0] for part in own)
    shape = (rows,) + own[0].shape[1:]
    anywhere = pl.BlockSpec(memory_space=pl.ANY)
    return pl.pallas_call(
        functools.partial(lay_out_kernel, len(own)),
        out_shape=jax.ShapeDtypeStruct(shape, own[0].dtype),
        in_specs=[pl.BlockSpec(memory_space=pltpu.SMEM)] + [anywhere] * (2 * len(own)),
        out_specs=anywhere,
        scratch_shapes=[
            pltpu.VMEM(shape, own[0].dtype),
            pltpu.SemaphoreType.DMA((2 * len(own),)),
            pltpu.SemaphoreType.DMA((2 * len(own),)),
        ],
        compiler_params=pltpu.CompilerParams(vmem_limit_bytes=32 * 2**20),
    )(core.reshape(1).astype(jnp.int32), *own, *other)


def together(*arrays):
    return lax.optimization_barrier(arrays)


def cut_kernel(k_count, z_count, gate_ref, up_ref, out_ref):
    own = out_ref.shape[3] // (2 * z_count)
    for k in range(k_count):
        for c in range(2):
            for which, ref in enumerate((gate_ref, up_ref)):
                for z in range(z_count):
                    at = ((k * z_count + z) * 2 + c) * own
                    to = (which * z_count + z) * own
                    out_ref[k, c, :, to : to + own] = ref[:, at : at + own]


def join_kernel(k_count, z_count, in_ref, gate_ref, up_ref):
    own = in_ref.shape[3] // (2 * z_count)
    for k in range(k_count):
        for c in range(2):
            for which, ref in enumerate((gate_ref, up_ref)):
                for z in range(z_count):
                    to = ((k * z_count + z) * 2 + c) * own
                    at = (which * z_count + z) * own
                    ref[:, to : to + own] = in_ref[k, c, :, at : at + own].astype(ref.dtype)


def in_vmem(kernel, arrays, out_shape):
    vmem = pl.BlockSpec(memory_space=pltpu.VMEM)
    return pl.pallas_call(
        kernel,
        out_shape=out_shape,
        in_specs=[vmem] * len(arrays),
        out_specs=jax.tree.map(lambda _: vmem, out_shape),
        compiler_params=pltpu.CompilerParams(vmem_limit_bytes=48 * 2**20),
    )(*arrays)


class Place:
    def __init__(self):
        self.k_count = lax.axis_size("dp")
        self.s_count = lax.axis_size("seq")
        self.z_count = self.s_count // 2
        self.k = lax.axis_index("dp")
        self.s = lax.axis_index("seq")
        self.c = self.s % 2
        self.z = self.s // 2
        self.square = self.k_count == 4
        self.z_groups = [
            [k * self.s_count + 2 * z + c for z in range(self.z_count)]
            for k in range(self.k_count)
            for c in range(2)
        ]
        self.plane_groups = [
            [k * self.s_count + 2 * z + c for k in range(self.k_count) for c in range(2)]
            for z in range(self.z_count)
        ]

    def to_k(self, array, flip):
        return lax.ppermute(array, "dp", [(i, i ^ flip) for i in range(self.k_count)])

    def to_core(self, array):
        return lax.ppermute(array, "seq", [(i, i ^ 1) for i in range(self.s_count)])

    def to_z(self, array, by):
        pairs = [(i, i + 2 * by) for i in range(self.s_count) if 0 <= i + 2 * by < self.s_count]
        return lax.ppermute(array, "seq", pairs)

    def by_core(self, own, other):
        return jnp.where(self.c == 0, jnp.stack([own, other]), jnp.stack([other, own]))

    def gather_z(self, array):
        return lax.all_gather(array, AXES, axis_index_groups=self.z_groups, tiled=True)

    def z_pairs(self, pairs):
        return [(2 * a + c, 2 * b + c) for a, b in pairs for c in range(2)]

    def own_apart(self, split, axis):
        shape = [1] * split.ndim
        shape[axis] = self.z_count
        own = (jnp.arange(self.z_count) == self.z).reshape(shape)
        sent = jnp.moveaxis(jnp.where(own, 0.0, split).astype(low), axis, 0)
        kept = lax.dynamic_index_in_dim(split, self.z, axis, False)
        return sent.reshape((-1,) + sent.shape[-1:]), kept.reshape((-1,) + sent.shape[-1:])

    def scatter_z(self, parts):
        total = lax.psum_scatter(
            parts[0], AXES, scatter_dimension=0, axis_index_groups=self.z_groups, tiled=True
        )
        return total, parts[1]


    def sum_far(self, chunk):
        if self.z_count != 4:
            return ()
        pairs = self.z_pairs([(0, 1), (3, 2)])
        return (lax.ppermute(chunk(3 - self.z).astype(low), "seq", pairs),)

    def sum_near(self, chunk):
        if self.z_count != 4:
            return ()
        below = self.to_z(chunk(jnp.minimum(self.z + 1, 3)).astype(low), 1)
        above = self.to_z(chunk(jnp.maximum(self.z - 1, 0)).astype(low), -1)
        return below, above

    def sum_second(self, chunk, far):
        if self.z_count != 4:
            return ()
        second = (chunk(self.z ^ 2).astype(wide) + far[0].astype(wide)).astype(low)
        return (lax.ppermute(second, "seq", self.z_pairs([(0, 2), (1, 3), (2, 0), (3, 1)])),)

    def sum_all(self, sent, kept, near, second):
        total = kept.astype(wide)
        if self.z_count != 4:
            whole = lax.psum_scatter(
                sent.reshape(-1, sent.shape[-1]),
                AXES,
                scatter_dimension=0,
                axis_index_groups=self.z_groups,
                tiled=True,
            )
            return total + whole.astype(wide)
        for part in near + second:
            total = total + part.astype(wide)
        return total

    def sum_z(self, array):
        if self.z_count != 4:
            return lax.psum(array, AXES, axis_index_groups=self.z_groups)
        for flip in range(1, 3):
            array = array + lax.ppermute(array, "seq", self.z_pairs([(z, z ^ flip) for z in range(4)]))
        return array

    def gather_seq_small(self, array):
        if self.s_count != 8:
            return lax.all_gather(array, "seq")
        out = array[None]
        for bit in range(3):
            got = lax.ppermute(out, "seq", [(i, i ^ (1 << bit)) for i in range(8)])
            low_bit = (self.s >> bit) % 2 == 0
            out = jnp.where(low_bit, jnp.concatenate([out, got]), jnp.concatenate([got, out]))
        return out

    def gather_dp_small(self, array):
        if not self.square:
            return lax.all_gather(array, "dp")
        out = array[None]
        for bit in range(2):
            got = self.to_k(out, 1 << bit)
            low_bit = (self.k >> bit) % 2 == 0
            out = jnp.where(low_bit, jnp.concatenate([out, got]), jnp.concatenate([got, out]))
        return out

    def gather_plane(self, array):
        if not self.square:
            whole = lax.all_gather(array, AXES, axis_index_groups=self.plane_groups)
            whole = whole.reshape((self.k_count, 2) + array.shape)
            return jnp.swapaxes(whole, 0, 1).reshape((-1,) + array.shape[1:])
        return self.gather_end(self.gather_far(self.gather_near(array)))

    def gather_near(self, array):
        if not self.square:
            return (array,)
        return array, self.to_k(array, 1), self.to_k(array, 2)

    def gather_far(self, near):
        if not self.square:
            return near
        array, from_x, from_y = near
        half = array.shape[0] // 2
        return array, from_x, from_y, self.to_k(from_x[:half], 2), self.to_k(from_y[half:], 1)

    def gather_core(self, mine):
        if not self.square:
            return [self.gather_plane(mine[0])], None
        return list(mine), [self.to_core(part) for part in mine]

    def gather_end(self, mine):
        if not self.square:
            return self.gather_plane(mine[0])
        return lay_out(self.c, mine, [self.to_core(part) for part in mine])

    def gather_rows(self, array):
        if not self.square:
            return lax.all_gather(array, "dp", tiled=True)
        array = jnp.concatenate([array, self.to_k(array, 1)])
        return jnp.concatenate([array, self.to_k(array, 2)])

    def gather_plane_small(self, array):
        if not self.square:
            return self.gather_plane(array)
        near = jnp.stack([array, self.to_k(array, 1)])
        mine = jnp.concatenate([near, self.to_k(near, 2)])
        return self.by_core(mine, self.to_core(mine)).reshape((-1,) + array.shape[1:])

    def halves(self, array):
        count = array.shape[0] // 2
        own = lax.dynamic_slice_in_dim(array, self.c * count, count, 0)
        return own, lax.dynamic_slice_in_dim(array, (1 - self.c) * count, count, 0)

    def chip_product(self, left, right, dot, exact=False):
        own, other = self.halves(left)
        count = own.shape[0] // 2
        got = []
        for i in range(2):
            part = dot(other[i * count : (i + 1) * count], right)
            if exact:
                part = self.pack(part, self.power_of(part))
                got.append(self.unpack(self.to_core(part))[0])
            else:
                got.append(self.to_core(part.astype(low)).astype(wide))
        chip = []
        for i in range(2):
            part = dot(own[i * count : (i + 1) * count], right) + got[i]
            chip += list(part.reshape(self.k_count // 2, -1, part.shape[-1]))
        return chip

    def power_of(self, values):
        largest = jnp.max(jnp.abs(values), axis=-1, keepdims=True)
        return jnp.ceil(jnp.log2(jnp.clip(largest, 1e-30, 1e37)))

    def pack(self, parts, power):
        scaled = (parts * jnp.exp2(-power)).astype(jnp.float16)
        power = jnp.broadcast_to(power, power.shape[:-1] + (128,)).astype(jnp.float16)
        return jnp.concatenate([scaled, power], axis=-1)

    def unpack(self, got):
        got = got.astype(wide)
        width = got.shape[-1] - 128
        power = got[..., width : width + 1]
        return got[..., :width] * jnp.exp2(power), power

    def chip_send(self, left, right, side):
        if not self.square:
            return None, None
        other = other_call(self.c, left, right, left.shape[0] // 8, side)
        return other, self.to_core(other)

    def chip_own(self, left, right, got, side):
        if not self.square:
            return self.chip_product(left, right, dot_nt if side else dot_nn)
        return own_call(self.c, left, right, got, left.shape[0] // 8, side)

    def near_parts(self, parts):
        if not self.square:
            return self.near_plane(parts)
        chip, next_a, next_b, a, b = parts
        return (chip, next_a, next_b, *together(self.to_k(a, 1), self.to_k(b, 2)))

    def far_product(self, near):
        if not self.square:
            return self.far_plane(near)
        chip, next_a, next_b, got_a, got_b = near
        half = next_a.shape[1]
        got_a, got_b = got_a.astype(wide), got_b.astype(wide)
        own_a, own_b = chip[:, :half] + got_a[0], chip[:, half:] + got_b[0]
        return self.last_plane(next_a + got_a[1], next_b + got_b[1], None, None, own_a, own_b)

    def near_plane(self, chip, exact=False):
        if not self.square:
            return (lax.psum_scatter(jnp.stack(chip), "dp", scatter_dimension=0, tiled=False),)
        half = chip[0].shape[1] // 2
        power = [self.power_of(part) for part in chip] if exact else None

        def pick(a, i, j):
            return a if a is None else jnp.stack([a[i], a[j]])

        got_a = self.send_plane(jnp.stack([chip[1][:, :half], chip[3][:, :half]]), pick(power, 1, 3), 1)
        got_b = self.send_plane(jnp.stack([chip[2][:, half:], chip[3][:, half:]]), pick(power, 2, 3), 2)
        got_a, got_b = together(got_a, got_b)
        return chip, power, got_a, got_b

    def send_plane(self, parts, power, flip):
        if power is None:
            return self.to_k(parts.astype(low), flip), None
        return self.unpack(self.to_k(self.pack(parts, power), flip))

    def far_plane(self, near):
        if not self.square:
            return near[0]
        chip, power, (got_a, power_a), (got_b, power_b) = near
        half = chip[0].shape[1] // 2
        got_a, got_b = got_a.astype(wide), got_b.astype(wide)

        def above(a, i, b, j):
            return a if a is None else jnp.maximum(a[i], b[j]) + 1.0

        next_a, next_b = chip[2][:, :half] + got_a[1], chip[1][:, half:] + got_b[1]
        return self.last_plane(
            next_a,
            next_b,
            above(power_a, 1, power, 2),
            above(power_b, 1, power, 1),
            chip[0][:, :half] + got_a[0],
            chip[0][:, half:] + got_b[0],
        )

    def last_plane(self, next_a, next_b, power_a, power_b, own_a, own_b):
        if power_a is None:
            next_a, next_b = together(next_a.astype(low), next_b.astype(low))
            last_a, last_b = self.to_k(next_a, 2).astype(wide), self.to_k(next_b, 1).astype(wide)
        else:
            next_a, next_b = together(self.pack(next_a, power_a), self.pack(next_b, power_b))
            last_a, last_b = self.unpack(self.to_k(next_a, 2))[0], self.unpack(self.to_k(next_b, 1))[0]
        return jnp.concatenate([own_a + last_a, own_b + last_b], axis=1)

    def sum_plane(self, chip, exact=False):
        return self.far_plane(self.near_plane(chip, exact))

    def exchange_plane(self, array):
        return self.exchange_dp(self.exchange_core(array))

    def exchange_core(self, array):
        keep = lax.dynamic_index_in_dim(array, self.c, 1, False)
        got = self.to_core(lax.dynamic_index_in_dim(array, 1 - self.c, 1, False))
        return jnp.moveaxis(self.by_core(keep, got), 0, 1)

    def exchange_dp(self, pairs):
        if not self.square:
            return lax.all_to_all(pairs, "dp", 0, 0, tiled=True)
        parts = [lax.dynamic_index_in_dim(pairs, self.k, 0, False)]
        for flip in range(1, 4):
            parts.append(self.to_k(lax.dynamic_index_in_dim(pairs, self.k ^ flip, 0, False), flip))
        odd = self.k % 2 == 1
        parts = [jnp.where(odd, parts[i ^ 1], parts[i]) for i in range(4)]
        upper = self.k >= 2
        return jnp.stack([jnp.where(upper, parts[i ^ 2], parts[i]) for i in range(4)])


def gelu_pair(x):
    slope = 0.7978845608028654
    inner = jnp.tanh(slope * (x + 0.044715 * x * x * x))
    half = 0.5 * (1.0 + inner)
    return x * half, half + 0.5 * x * (1.0 - inner * inner) * slope * (1.0 + 0.134145 * x * x)


def rms_normed(values, gain):
    values = values.astype(wide)
    scale = lax.rsqrt(jnp.mean(values * values, axis=1, keepdims=True) + eps_value)
    return (values * scale * gain).astype(low)


def ordered(values, order):
    if order is None:
        return values
    size = values.shape[1] // len(order)
    return jnp.concatenate([values[:, i * size : (i + 1) * size] for i in order], axis=1)


def minus_expm1(x):
    near = 1.0
    for i in range(8, 1, -1):
        near = 1.0 + near * x * (1.0 / i)
    return jnp.where(x > -0.5, -x * near, 1.0 - jnp.exp(x))


def gates_of(conv_low, w_gates, params, not_start):
    width = conv_low.shape[1]
    pre = jnp.dot(conv_low, w_gates, preferred_element_type=wide)
    rate = jax.nn.sigmoid(pre[:, :width] + params[5:6])
    igate = jax.nn.sigmoid(pre[:, width:] + params[6:7])
    log_keep = params[7:8] * rate
    room = minus_expm1(2.0 * log_keep)
    mult = jnp.where(not_start > 0.5, jnp.sqrt(jnp.maximum(room, floor_value)), 1.0)
    return rate, igate, jnp.exp(log_keep), room, mult


def shifted(values, by, fill):
    count = values.shape[0]
    size = abs(by)
    if size % 8 == 0:
        free = jnp.full((size, values.shape[1]), fill, values.dtype)
        if by > 0:
            return jnp.concatenate([free, values[: count - size]])
        return jnp.concatenate([values[size:], free])
    place = lax.broadcasted_iota(jnp.int32, values.shape, 0)
    moved = pltpu.roll(values, by % count, 0)
    return jnp.where(place >= by if by > 0 else place < count - size, moved, fill)


def scan_rows(keep, drive, sign):
    by = 1
    while by < keep.shape[0]:
        drive = drive + keep * shifted(drive, sign * by, 0.0)
        keep = keep * shifted(keep, sign * by, 1.0)
        by *= 2
    return keep, drive


def conv_kernel(
    rows, span, order, x_ref, w_ref, halo_ref, gain_ref, params_ref, gates_ref,
    normed_ref, masks_ref, branch_ref, in_ref, low_ref, keep_ref, part_ref, run_ref, sums_ref, before_ref, tail, line, ends,
):
    step = pl.program_id(0)
    width = in_ref.shape[1]
    count = x_ref.shape[0]
    row_dev = count // span

    @pl.when(step == 0)
    def _():
        normed = rms_normed(halo_ref[...], gain_ref[...])
        before = jnp.dot(ordered(normed, order), w_ref[:, width:], preferred_element_type=wide)
        tail[...] = before.astype(low).astype(wide)
        before_ref[...] = tail[...]

    features = gain_ref.shape[1]
    normed = rms_normed(x_ref[:, :features], gain_ref[...])
    normed_ref[...] = normed
    masks_ref[...] = x_ref[:, features : features + 8].astype(wide)
    pre = jnp.dot(ordered(normed, order), w_ref[...], preferred_element_type=wide)
    branch_ref[...] = pre[:, :width]
    conv_in = pre[:, width:].astype(low)
    in_ref[...] = conv_in
    conv_in = conv_in.astype(wide)
    params = params_ref[...]
    for row in range(row_dev):
        at = slice(row * span, (row + 1) * span)
        own = conv_in[at]
        place = pl.ds(pl.multiple_of((lax.rem(step * row_dev + row, rows)) * 8, 8), 8)
        line[:8] = tail[place]
        line[8:] = own
        tail[place] = own[span - 8 :]
        masks = masks_ref[at]
        total = params[4:5] + params[0:1] * own
        for by in range(1, 4):
            total = total + params[by : by + 1] * line[8 - by : 8 - by + span] * masks[:, by - 1 : by]
        conv_low = total.astype(low)
        low_ref[at] = conv_low
        not_start = masks[:, 3:4]
        rate, igate, keep, room, mult = gates_of(conv_low, gates_ref[...], params, not_start)
        keep = keep * not_start
        keep_ref[at] = keep
        run, part = scan_rows(keep, mult * igate * conv_low.astype(wide), 1)

        @pl.when(step * row_dev < rows)
        def _(run=run, part=part, place=place, at=at):
            run_ref[at] = run
            part_ref[at] = part
            ends[0, place] = run[span - 8 :]
            ends[1, place] = part[span - 8 :]

        @pl.when(step * row_dev >= rows)
        def _(run=run, part=part, place=place, at=at):
            part = part + run * ends[1, place][7:8]
            run = run * ends[0, place][7:8]
            run_ref[at] = run
            part_ref[at] = part
            sums_ref[0, place] = run[span - 8 :]
            sums_ref[1, place] = part[span - 8 :]


def state_kernel(rows, span, part_ref, run_ref, start_ref, branch_ref, state_ref, mixed_ref):
    step = pl.program_id(0)
    row_dev = part_ref.shape[0] // span
    for row in range(row_dev):
        at = slice(row * span, (row + 1) * span)
        place = pl.ds(pl.multiple_of((lax.rem(step * row_dev + row, rows)) * 8, 8), 8)
        state = part_ref[at] + run_ref[at] * start_ref[place][7:8]
        state_ref[at] = state
        value, _ = gelu_pair(branch_ref[at])
        mixed_ref[at] = (value * state).astype(low)


def mlp_kernel(x_ref, cot_ref, w_ref, down_ref, hidden_ref, grad_ref):
    width = hidden_ref.shape[1]
    pre = jnp.dot(x_ref[...], w_ref[...], preferred_element_type=wide)
    grad = lax.dot_general(
        cot_ref[...], down_ref[...], (((1,), (1,)), ((), ())), preferred_element_type=wide
    )
    up = pre[:, width:]
    value, slope = gelu_pair(pre[:, :width])
    hidden_ref[...] = (value * up).astype(low)
    grad_ref[:, :width] = (grad * up * slope).astype(low)
    grad_ref[:, width:] = (grad * value).astype(low)


def other_kernel(side, core_ref, x_ref, w_ref, out_ref):
    product = lax.dot_general(
        x_ref[...], w_ref[...], (((1,), (side,)), ((), ())), preferred_element_type=wide
    )
    out_ref[...] = product.astype(low)


def own_kernel(side, core_ref, x_ref, w_ref, got_ref, chip_ref, next_a_ref, next_b_ref, a_ref, b_ref):
    step = pl.program_id(0)
    product = lax.dot_general(
        x_ref[...], w_ref[...], (((1,), (side,)), ((), ())), preferred_element_type=wide
    )
    product = product + got_ref[...].astype(wide)
    half = product.shape[1] // 2

    @pl.when(step == 0)
    def _():
        chip_ref[...] = product

    @pl.when(step == 1)
    def _():
        next_b_ref[...] = product[:, half:]

    @pl.when(step == 2)
    def _():
        next_a_ref[...] = product[:, :half]

    @pl.when((step == 1) | (step == 3))
    def _():
        a_ref[0] = product[:, :half].astype(low)

    @pl.when(step >= 2)
    def _():
        b_ref[0] = product[:, half:].astype(low)


def back_kernel(
    rows, span, x_ref, w_ref, branch_ref, state_ref, keep_ref, grad_branch_ref, part_ref, run_ref, sum_ref, ends
):
    step = pl.program_id(0)
    count = x_ref.shape[0]
    row_dev = count // span
    mixed = lax.dot_general(
        x_ref[...], w_ref[...], (((1,), (1,)), ((), ())), preferred_element_type=wide
    )
    late = step * row_dev < rows
    for row in range(row_dev):
        at = slice(row * span, (row + 1) * span)
        block = (pl.num_programs(0) - 1 - step) * row_dev + row
        place = pl.ds(pl.multiple_of(lax.rem(block, rows) * 8, 8), 8)
        value, slope = gelu_pair(branch_ref[at])
        grad_branch_ref[at] = (mixed[at] * state_ref[at] * slope).astype(low)
        grad = mixed[at] * value
        keep = keep_ref[at]
        run, part = scan_rows(keep, keep * grad, -1)

        @pl.when(late)
        def _(run=run, part=part, grad=grad, place=place, at=at):
            ends[0, place] = run[:8]
            ends[1, place] = part[:8]
            run_ref[at] = shifted(run, -1, 1.0)
            part_ref[at] = grad + shifted(part, -1, 0.0)

        @pl.when(jnp.logical_not(late))
        def _(run=run, part=part, grad=grad, place=place, at=at):
            next_run, next_part = ends[0, place][:1], ends[1, place][:1]
            part = part + run * next_part
            run = run * next_run
            last = lax.broadcasted_iota(jnp.int32, run.shape, 0) == span - 1
            run_ref[at] = jnp.where(last, next_run, shifted(run, -1, 1.0))
            part_ref[at] = grad + jnp.where(last, next_part, shifted(part, -1, 0.0))
            sum_ref[place] = part[:8]


def adjoint_kernel(
    rows, span, part_ref, run_ref, carry_ref, state_ref, start_ref, low_ref, gates_ref, params_ref,
    masks_ref, in_ref, before_ref, grad_conv_ref, small_ref, vectors_ref, gates_grad_ref, sums_ref, line, ends, tail,
):
    step = pl.program_id(0)
    width = low_ref.shape[1]
    row_dev = low_ref.shape[0] // span
    params = params_ref[...]

    @pl.when(step == 0)
    def _():
        gates_grad_ref[...] = jnp.zeros(gates_grad_ref.shape, wide)
        sums_ref[...] = jnp.zeros(sums_ref.shape, wide)
        ends[...] = start_ref[...]
        tail[...] = before_ref[...]

    for row in range(row_dev):
        at = slice(row * span, (row + 1) * span)
        place = pl.ds(pl.multiple_of((lax.rem(step * row_dev + row, rows)) * 8, 8), 8)
        conv_low = low_ref[at]
        conv_value = conv_low.astype(wide)
        masks = masks_ref[at]
        not_start = masks[:, 3:4]
        rate, igate, keep, room, mult = gates_of(conv_low, gates_ref[...], params, not_start)
        adj = part_ref[at] + run_ref[at] * carry_ref[place][:1]
        state = state_ref[at]
        line[:8] = ends[place]
        line[8:] = state
        ends[place] = state[span - 8 :]
        through = adj * line[7 : 7 + span]
        spread = jnp.where(room > floor_value, adj * igate * conv_value * keep * keep / mult, 0.0)
        grad_log = not_start * (through * keep - spread)
        grad_rate = (grad_log * params[7:8] * rate * (1.0 - rate)).astype(low)
        scaled = adj * mult
        grad_igate = (scaled * conv_value * igate * (1.0 - igate)).astype(low)
        both = jnp.concatenate([grad_rate, grad_igate], axis=1)
        grad_conv = scaled * igate + lax.dot_general(
            both, gates_ref[...], (((1,), (1,)), ((), ())), preferred_element_type=wide
        )
        grad_conv = grad_conv.astype(low)
        grad_conv_ref[at] = grad_conv
        gates_grad_ref[...] += lax.dot_general(
            conv_low, both, (((0,), (0,)), ((), ())), preferred_element_type=wide
        )
        grad_conv = grad_conv.astype(wide)
        conv_in = in_ref[at].astype(wide)
        line[:8] = tail[place]
        line[8:] = conv_in
        tail[place] = conv_in[span - 8 :]
        values = [grad_conv * conv_in]
        for by in range(1, 4):
            values.append(grad_conv * line[8 - by : 8 - by + span] * masks[:, by - 1 : by])
        values += [grad_conv, grad_rate.astype(wide), grad_igate.astype(wide), grad_log * rate * params[8:9]]
        for i, value in enumerate(values):
            sums_ref[i : i + 1] += jnp.sum(value, axis=0, keepdims=True)

    @pl.when(step == pl.num_programs(0) - 1)
    def _():
        block = small_ref.shape[1] // 2
        for head in range(width // block):
            at = slice(head * block, (head + 1) * block)
            small_ref[at, :block] = gates_grad_ref[at, at].astype(low)
            then = slice(width + head * block, width + (head + 1) * block)
            small_ref[at, block:] = gates_grad_ref[at, then].astype(low)
        vectors_ref[...] = sums_ref[...]


def conv_back_kernel(rows, span, grad_ref, halo_ref, masks_ref, halo_masks_ref, branch_ref, params_ref, one_ref, line):
    params = params_ref[...]

    def work(block, grad_next, masks_next):
        at = pl.ds(pl.multiple_of(block * span, 16), span)
        own = grad_ref[at].astype(wide)
        total = params[0:1] * own
        masks = masks_ref[at]
        for by in range(1, 4):
            line[:span] = own * masks[:, by - 1 : by]
            line[span:] = grad_next * masks_next[:, by - 1 : by]
            total = total + params[by : by + 1] * line[by : by + span]
        width = branch_ref.shape[1]
        one_ref[at, :width] = branch_ref[at]
        one_ref[at, width:] = total.astype(low)

    @pl.loop(0, rows)
    def _(block):
        then = pl.ds(pl.multiple_of((block + rows) * span, 16), 16)
        work(block, grad_ref[then].astype(wide)[:8], masks_ref[then][:8])

    @pl.loop(0, rows)
    def _(block):
        then = pl.ds(pl.multiple_of(block * 16, 16), 16)
        work(block + rows, halo_ref[then].astype(wide)[:8], halo_masks_ref[then][:8])


def whole_block(array):
    return pl.BlockSpec(array.shape, lambda *i, n=len(array.shape): (0,) * n)


def token_block(array, count, steps, backwards):
    def index(i):
        return (steps - 1 - i if backwards else i,) + (0,) * (len(array.shape) - 1)

    return pl.BlockSpec((count,) + array.shape[1:], index)


def half_of(core, x, count, width):
    return pl.BlockSpec((count, width), lambda k, core_ref: (core_ref[0] * (x.shape[0] // (2 * count)) + k, 0))


def half_call(kernel, core, x, w, count, extra, outputs):
    def spec(array, block, index):
        return pl.BlockSpec(block, lambda k, core_ref: index(k))

    return pl.pallas_call(
        kernel,
        out_shape=[array for array, _, _ in outputs],
        grid_spec=pltpu.PrefetchScalarGridSpec(
            num_scalar_prefetch=1,
            grid=(x.shape[0] // (2 * count),),
            in_specs=[
                half_of(core, x, count, x.shape[1]),
                pl.BlockSpec(w.shape, lambda k, core_ref: (0, 0)),
            ]
            + [spec(*one) for one in extra],
            out_specs=[spec(*one) for one in outputs],
        ),
        cost_estimate=pl.CostEstimate(flops=0, bytes_accessed=0, transcendentals=0),
        compiler_params=pltpu.CompilerParams(vmem_limit_bytes=60 * 2**20),
    )(core.reshape(1).astype(jnp.int32), x, w, *[array for array, _, _ in extra])


def other_call(core, x, w, count, side):
    width = w.shape[1 - side]
    out = jax.ShapeDtypeStruct((x.shape[0] // 2, width), low)
    kernel = functools.partial(other_kernel, side)
    return half_call(kernel, 1 - core, x, w, count, [], [(out, (count, width), lambda k: (k, 0))])[0]


def own_call(core, x, w, got, count, side):
    width = w.shape[1 - side]
    a = jax.ShapeDtypeStruct((2, count, width // 2), low)
    chip = jax.ShapeDtypeStruct((count, width), wide)
    after = jax.ShapeDtypeStruct((count, width // 2), wide)
    return half_call(
        functools.partial(own_kernel, side),
        core,
        x,
        w,
        count,
        [(got, (count, width), lambda k: (k, 0))],
        [
            (chip, chip.shape, lambda k: (0, 0)),
            (after, after.shape, lambda k: (0, 0)),
            (after, after.shape, lambda k: (0, 0)),
            (a, (1, count, width // 2), lambda k: (k // 2, 0, 0)),
            (a, (1, count, width // 2), lambda k: (k // 3, 0, 0)),
        ],
    )


def rows_kernel(core_ref, x_ref, grad_ref, sent_ref, kept_ref):
    count = kept_ref.shape[1]
    total = lax.dot_general(
        x_ref[...], grad_ref[...], (((0,), (0,)), ((), ())), preferred_element_type=wide
    )
    planes = sent_ref.shape[0]
    first = lax.rem(pl.program_id(0), core_ref[1]) * planes
    for i in range(planes):
        part = total[i * count : (i + 1) * count]
        mine = first + i == core_ref[0]
        sent_ref[i, 0] = jnp.where(mine, jnp.zeros_like(part), part).astype(low)

        @pl.when(mine)
        def _(part=part):
            kept_ref[0] = part


def rows_call(z, z_count, k_count, x, grad):
    tokens, features = x.shape
    count = features // (z_count * k_count)
    planes = max(2, 128 // count)
    width = grad.shape[1]
    per = z_count // planes
    sent = jax.ShapeDtypeStruct((z_count, k_count, count, width), low)
    kept = jax.ShapeDtypeStruct((k_count, count, width), wide)
    return pl.pallas_call(
        rows_kernel,
        out_shape=[sent, kept],
        grid_spec=pltpu.PrefetchScalarGridSpec(
            num_scalar_prefetch=1,
            grid=(k_count * per,),
            in_specs=[
                pl.BlockSpec((tokens, planes * count), lambda i, ref: (0, i)),
                pl.BlockSpec(grad.shape, lambda i, ref: (0, 0)),
            ],
            out_specs=[
                pl.BlockSpec((planes, 1, count, width), lambda i, ref: (i % per, i // per, 0, 0)),
                pl.BlockSpec((1, count, width), lambda i, ref: (i // per, 0, 0)),
            ],
        ),
        cost_estimate=pl.CostEstimate(flops=0, bytes_accessed=0, transcendentals=0),
        compiler_params=pltpu.CompilerParams(vmem_limit_bytes=60 * 2**20),
    )(jnp.stack([z, jnp.int32(per)]).astype(jnp.int32), x, grad)


def down_kernel(core_ref, hidden_ref, cot_ref, sent_ref, kept_ref):
    total = lax.dot_general(
        cot_ref[...], hidden_ref[...], (((0,), (0,)), ((), ())), preferred_element_type=wide
    )
    total = total.T
    count = kept_ref.shape[0]
    for i in range(sent_ref.shape[0]):
        part = total[i * count : (i + 1) * count]
        mine = core_ref[0] == i
        sent_ref[i] = jnp.where(mine, jnp.zeros_like(part), part).astype(low)

        @pl.when(mine)
        def _(part=part):
            kept_ref[...] = part


def down_call(z, z_count, hidden, cot):
    tokens, features = cot.shape
    count = hidden.shape[1] // z_count
    columns = 256
    sent = jax.ShapeDtypeStruct((z_count, count, features), low)
    kept = jax.ShapeDtypeStruct((count, features), wide)
    return pl.pallas_call(
        down_kernel,
        out_shape=[sent, kept],
        grid_spec=pltpu.PrefetchScalarGridSpec(
            num_scalar_prefetch=1,
            grid=(features // columns,),
            in_specs=[
                pl.BlockSpec(hidden.shape, lambda i, ref: (0, 0)),
                pl.BlockSpec((tokens, columns), lambda i, ref: (0, i)),
            ],
            out_specs=[
                pl.BlockSpec((z_count, count, columns), lambda i, ref: (0, 0, i)),
                pl.BlockSpec((count, columns), lambda i, ref: (0, i)),
            ],
        ),
        cost_estimate=pl.CostEstimate(flops=0, bytes_accessed=0, transcendentals=0),
        compiler_params=pltpu.CompilerParams(vmem_limit_bytes=60 * 2**20),
    )(z.reshape(1).astype(jnp.int32), hidden, cot)


def kernel_call(kernel, steps, inputs, outputs, scratch=(), backwards=False):
    def spec(array, count):
        return whole_block(array) if count is None else token_block(array, count, steps, backwards)

    return pl.pallas_call(
        kernel,
        out_shape=[array for array, _ in outputs],
        grid=(steps,),
        in_specs=[spec(array, count) for array, count in inputs],
        out_specs=[spec(array, count) for array, count in outputs],
        scratch_shapes=scratch,
        cost_estimate=pl.CostEstimate(flops=0, bytes_accessed=0, transcendentals=0),
        compiler_params=pltpu.CompilerParams(vmem_limit_bytes=60 * 2**20),
    )(*[array for array, _ in inputs])


def gathered_kernel(kernel, parts, steps, backwards, keep, given, core_ref, *refs):
    own, other = refs[:parts], refs[parts : 2 * parts]
    refs = refs[2 * parts :]
    inputs, refs = refs[:given], refs[given:]
    out_ref, refs = (refs[0], refs[1:]) if keep else (None, refs)
    buffer, sem, out_sem = refs[-3:]
    half = buffer.shape[0] // 2
    count = buffer.shape[0] // steps
    step = pl.program_id(0)
    block = steps - 1 - step if backwards else step

    @pl.when(step == 0)
    def _():
        for which, group in enumerate((own, other)):
            side = core_ref[0] if which == 0 else 1 - core_ref[0]
            start = 0
            for i, part in enumerate(group):
                to = pl.ds(pl.multiple_of(side * half + start, 16), part.shape[0])
                pltpu.make_async_copy(part, buffer.at[to], sem.at[side * parts + i]).start()
                start = start + part.shape[0]

    at = pl.ds(pl.multiple_of(block * count, 16), count)
    side = block // (steps // 2)
    place = lax.rem(block, steps // 2)
    whole = steps // 2 - 1

    @pl.when(place < whole)
    def _():
        pltpu.make_async_copy(buffer.at[at], buffer.at[at], sem.at[side * parts + place]).wait()

    @pl.when(place == whole)
    def _():
        for i in range(whole, parts):
            to = pl.ds(pl.multiple_of(block * count, 16), own[i].shape[0])
            pltpu.make_async_copy(buffer.at[to], buffer.at[to], sem.at[side * parts + i]).wait()

    if keep:
        pltpu.make_async_copy(buffer.at[at], out_ref.at[at], out_sem.at[block]).start()
    kernel(buffer.at[at], *inputs, *refs[:-3])
    if keep:

        @pl.when(step == steps - 1)
        def _():
            for i in range(steps):
                to = pl.ds(i * count, count)
                pltpu.make_async_copy(buffer.at[to], out_ref.at[to], out_sem.at[i]).wait()


def gathered_call(kernel, core, gathered, steps, inputs, outputs, scratch=(), backwards=False, keep=True, cost=0):
    own, other = gathered
    if other is None:
        count = own[0].shape[0] // steps
        results = kernel_call(kernel, steps, [(own[0], count)] + inputs, outputs, scratch, backwards)
        return ([own[0]] if keep else []) + list(results)

    def spec(array, count):
        return whole_block(array) if count is None else token_block(array, count, steps, backwards)

    anywhere = pl.BlockSpec(memory_space=pl.ANY)
    tokens = jax.ShapeDtypeStruct((2 * sum(p.shape[0] for p in own),) + own[0].shape[1:], own[0].dtype)
    return pl.pallas_call(
        functools.partial(gathered_kernel, kernel, len(own), steps, backwards, keep, len(inputs)),
        out_shape=([tokens] if keep else []) + [array for array, _ in outputs],
        grid=(steps,),
        in_specs=[pl.BlockSpec(memory_space=pltpu.SMEM)]
        + [anywhere] * (2 * len(own))
        + [spec(array, count) for array, count in inputs],
        out_specs=([anywhere] if keep else []) + [spec(array, count) for array, count in outputs],
        scratch_shapes=list(scratch)
        + [
            pltpu.VMEM(tokens.shape, tokens.dtype),
            pltpu.SemaphoreType.DMA((2 * len(own),)),
            pltpu.SemaphoreType.DMA((steps,)),
        ],
        cost_estimate=pl.CostEstimate(flops=0, bytes_accessed=cost << 20, transcendentals=0),
        compiler_params=pltpu.CompilerParams(vmem_limit_bytes=60 * 2**20),
    )(core.reshape(1).astype(jnp.int32), *own, *other, *[array for array, _ in inputs])


def per_device(
    tokens,
    segment_ids,
    cotangent,
    norm_one,
    branch_weight,
    input_proj,
    conv_weight,
    conv_bias,
    rate_weight,
    igate_weight,
    rate_bias,
    igate_bias,
    decay_param,
    out_proj,
    norm_two,
    mlp_gate,
    mlp_up,
    mlp_down,
):
    at = Place()
    k_count, z_count = at.k_count, at.z_count
    group = 2 * k_count
    row_dev, span, width_d = tokens.shape
    tok = row_dev * span
    rows = k_count * row_dev
    tok_all = 2 * rows * span
    d_own = norm_one.shape[0]
    w_own = conv_bias.shape[0]
    f_own = mlp_down.shape[0]
    width_r = branch_weight.shape[1]
    w_slot = width_r // group
    f_slot = f_own * z_count
    taps = conv_weight.shape[0]
    reach = taps - 1
    half_z = z_count // 2

    def by_feature(array):
        split = array.reshape(z_count, -1, 2 * d_own, array.shape[1])
        return jnp.swapaxes(split, 0, 1).reshape(array.shape)

    small = jnp.concatenate(
        [
            norm_one,
            norm_two,
            conv_weight.reshape(-1),
            conv_bias,
            rate_bias,
            igate_bias,
            decay_param,
        ]
    )
    rec_cols = jnp.concatenate(
        [
            branch_weight.reshape(d_own, k_count, 2, w_slot),
            input_proj.reshape(d_own, k_count, 2, w_slot),
        ],
        axis=3,
    )
    rec_pairs = at.exchange_core(jnp.moveaxis(rec_cols, 0, 2))

    seg_code = (segment_ids % 64).astype(low)
    pairs = [(i, i + 1) for i in range(at.s_count - 1)]
    before = lax.ppermute(seg_code[:, span - reach :], "seq", pairs)
    tokens = tokens.reshape(tok, width_d)
    tail = tokens.reshape(row_dev, span, width_d)[:, span - 8 :].reshape(row_dev * 8, width_d)
    tail = at.to_z(tail, 1)

    small = jnp.pad(small, (0, -small.shape[0] % 128)).reshape(-1, 128)
    small_rows = small.shape[0]
    small = jnp.pad(small, ((0, w_own - small_rows), (0, 0)))
    out_rows = jnp.concatenate([out_proj, rate_weight, igate_weight, small], axis=1)
    out_rows, before, tail = together(out_rows, before, tail)
    out_part = at.gather_z(out_rows)

    rec_cols = at.exchange_dp(rec_pairs)
    order = None
    if 2 * d_own % 128 == 0:
        order = [k * z_count + z for z in range(z_count) for k in range(k_count)]
    ext_code = jnp.concatenate([before, seg_code], axis=1)
    position = lax.broadcasted_iota(jnp.int32, (row_dev, span), 1)
    masks = [
        (ext_code[:, reach - by : reach - by + span] == seg_code) & ((at.s > 0) | (position >= by))
        for by in range(1, taps)
    ]
    masks = jnp.stack(masks + [masks[0]] * (9 - taps), axis=-1).astype(low).reshape(tok, 8)
    beside = jnp.concatenate([tokens, jnp.pad(masks, ((0, 0), (0, 120)))], axis=1)
    beside, rec_cols = together(beside, rec_cols)
    w1 = at.gather_z(rec_cols.reshape(group * d_own, 2 * w_slot))
    beside_near = at.gather_near(beside)
    tail = jnp.where(at.c == 1, tail, at.to_core(tail))
    inputs = tokens.astype(wide)
    s1 = lax.rsqrt(jnp.mean(inputs * inputs, axis=-1, keepdims=True) + eps_value)
    mlp_shape = jax.ShapeDtypeStruct((k_count, 2, d_own, 2 * f_slot), low)
    cut = functools.partial(cut_kernel, k_count, z_count)
    mlp_pairs = at.exchange_core(in_vmem(cut, (mlp_gate, mlp_up), mlp_shape))
    beside_near, tail, mlp_pairs, out_part = together(beside_near, tail, mlp_pairs, out_part)
    tail = at.gather_rows(tail)

    out_split = out_part.reshape(2, half_z, w_own, -1)

    def of_slot(columns):
        part = out_split[..., columns]
        keep = lax.dynamic_index_in_dim(part, at.c, 0, False)
        got = at.to_core(lax.dynamic_index_in_dim(part, 1 - at.c, 0, False))
        return jnp.swapaxes(at.by_core(keep, got), 0, 1).reshape(w_slot, -1)

    gate_rows = of_slot(slice(width_d, width_d + 2 * BS))
    small = out_part.reshape(z_count, w_own, -1)[:, :small_rows, width_d + 2 * BS :].reshape(z_count, -1)
    small = jnp.swapaxes(at.by_core(small, at.to_core(small)), 0, 1).reshape(at.s_count, -1)
    gains = at.gather_dp_small(small[:, : 2 * d_own]).reshape(k_count * at.s_count, -1)
    mine = lax.dynamic_slice_in_dim(small[:, 2 * d_own :], at.c * z_count, z_count, 0)
    mine = mine[:, : (taps + 4) * w_own].reshape(z_count, taps + 4, w_own).astype(wide)
    mine = jnp.swapaxes(mine, 0, 1).reshape(taps + 4, w_slot)
    w_conv = mine[:taps]
    b_conv, b_rate, b_igate, decay = (mine[taps + i][None, :] for i in range(4))
    log_slope = -rate_scale * jax.nn.softplus(-decay)
    decay_slope = rate_scale * jax.nn.sigmoid(-decay)
    params = jnp.concatenate([w_conv, b_conv, b_rate, b_igate, log_slope] + [decay_slope] * 8)
    beside_near, tail, gains, gate_rows = together(beside_near, tail, gains, gate_rows)
    heads = w_slot // BS

    def block_diagonal(columns):
        blocks = columns.reshape(heads, BS, 1, BS)
        same = jnp.eye(heads, dtype=low).reshape(heads, 1, heads, 1)
        return (blocks * same).reshape(w_slot, w_slot)

    w_gates = jnp.concatenate([block_diagonal(gate_rows[:, :BS]), block_diagonal(gate_rows[:, BS:])], axis=1)

    beside_far, mlp_pairs, w_gates, params = together(
        at.gather_far(beside_near), mlp_pairs, w_gates, params
    )
    gain_one = gains[:, :d_own].reshape(1, width_d).astype(wide)
    gain_two = gains[:, d_own:].reshape(1, width_d).astype(wide)
    mlp_cols = at.exchange_dp(mlp_pairs)
    cot = cotangent.reshape(tok, width_d)
    tokens_parts, mlp_cols, cot = together(at.gather_core(beside_far), mlp_cols, cot)
    shape = jax.ShapeDtypeStruct

    half_rows = group * d_own // 2
    w2_parts = [
        at.gather_z(part.reshape(half_rows, 2 * f_slot))
        for part in (mlp_cols[: k_count // 2], mlp_cols[k_count // 2 :])
    ]

    steps = tok_all // tok
    cot_near = at.gather_near(cot)
    flat32, flat16 = shape((tok_all, w_slot), wide), shape((tok_all, w_slot), low)
    ends = shape((rows * 8, w_slot), wide)

    def by_row(array):
        return jnp.repeat(array, 8, axis=0)

    n1_all, masks, branch_pre, conv_in, conv_low, keep_eff, part, run, summary, conv_before = gathered_call(
        functools.partial(conv_kernel, rows, span, order),
        at.c,
        tokens_parts,
        steps,
        [(w1 if order else by_feature(w1), None), (tail, None), (gain_one, None), (params, None), (w_gates, None)],
        [(shape((tok_all, width_d), low), tok), (shape((tok_all, 8), wide), tok), (flat32, tok), (flat16, tok), (flat16, tok)]
        + [(flat32, tok)] * 3
        + [(shape((2,) + ends.shape, wide), None), (ends, None)],
        [
            pltpu.VMEM(ends.shape, wide),
            pltpu.VMEM((span + 8, w_slot), wide),
            pltpu.VMEM((2,) + ends.shape, wide),
        ],
        keep=False,
    )
    summary = summary.reshape(2, rows, 8, w_slot)[:, :, 7]
    w_down = at.gather_z(mlp_down)
    summary, cot_near, out_split, w1 = together(summary, cot_near, out_split, w1)
    w1 = by_feature(w1)
    w_out = of_slot(slice(0, width_d))
    cot_far = at.gather_far(cot_near)
    before = [at.to_z(summary, by) for by in range(1, z_count)]
    state_in = jnp.zeros((rows, w_slot), wide)
    for one in reversed(before):
        state_in = one[1] + one[0] * state_in
    state_in = by_row(state_in)
    state, mixed = kernel_call(
        functools.partial(state_kernel, rows, span),
        steps,
        [(part, tok), (run, tok), (state_in, None), (branch_pre, tok)],
        [(flat32, tok), (flat16, tok)],
    )
    masks_after = at.to_z(masks.reshape(2, rows, span, 8)[0, :, :16], -1).reshape(rows * 16, 8)
    mixed, cot_far, w2_parts[0], masks_after, w1 = together(mixed, cot_far, w2_parts[0], masks_after, w1)

    chip_one = at.chip_product(mixed, w_out, dot_nn, exact=True)
    near_sum, cot_far = together(at.near_plane(chip_one, exact=True), cot_far)
    cot_all = at.gather_end(cot_far)
    resid = inputs + at.far_plane(near_sum)
    resid, w2_parts[1] = together(resid, w2_parts[1])
    w2 = jnp.concatenate([by_feature(part) for part in w2_parts])

    s2 = lax.rsqrt(jnp.mean(resid * resid, axis=-1, keepdims=True) + eps_value)
    normed_two = (resid * s2 * gain_two).astype(low)
    n2_near, w2, cot_all = together(at.gather_near(normed_two), w2, cot_all)
    n2_parts, w_down = together(at.gather_core(at.gather_far(n2_near)), w_down)
    n2_all, hidden, grad_two = gathered_call(
        mlp_kernel,
        at.c,
        n2_parts,
        steps,
        [(cot_all, tok), (w2, None), (w_down, None)],
        [(shape((tok_all, f_slot), low), tok), (shape((tok_all, 2 * f_slot), low), tok)],
    )
    def rows_apart(x, grad):
        sent, kept = rows_call(at.z, z_count, k_count, x, grad)
        return sent.reshape(-1, sent.shape[-1]), kept.reshape(-1, kept.shape[-1])

    _, got_two = at.chip_send(grad_two, w2, 1)
    near_two = at.near_parts(at.chip_own(grad_two, w2, got_two, 1))
    chip_two, grad_two = together(near_two[0], grad_two)
    w2_part = rows_apart(n2_all, grad_two)
    near_two, w2_part, hidden = together(near_two, w2_part, hidden)
    w2_sum = at.scatter_z(w2_part)
    grad_n2 = at.far_product(near_two)
    other_three, got_three = at.chip_send(hidden, w_down, 0)
    grad_n2, other_three, hidden = together(grad_n2, other_three, hidden)
    scaled_two = gain_two * grad_n2
    cot_f = cot.astype(wide)
    mean_two = jnp.mean(scaled_two * resid, axis=-1, keepdims=True)
    grad_resid = cot_f + s2 * scaled_two - resid * (s2 * s2 * s2) * mean_two
    grad_recur = grad_resid.astype(low)
    grad_recur, hidden = together(grad_recur, hidden)
    chip_three = at.chip_own(hidden, w_down, got_three, 0)
    down_sent, down_kept = down_call(at.z, z_count, hidden, cot_all)
    down_part = down_sent.reshape(-1, width_d), down_kept
    gr_near, chip_three, down_part = together(at.gather_near(grad_recur), chip_three, down_part)
    down_sum = at.scatter_z(down_part)
    gr_parts, chip_three = together(at.gather_core(at.gather_far(gr_near)), chip_three)

    def summed(pair):
        return pair[0].astype(wide) + pair[1].astype(wide)

    def to_owner(array, columns):
        return at.exchange_plane(array.reshape(k_count, 2, d_own, columns))


    gr_all, grad_branch, back_part, back_run, back = gathered_call(
        functools.partial(back_kernel, rows, span),
        at.c,
        gr_parts,
        steps,
        [(w_out, None), (branch_pre, tok), (state, tok), (keep_eff, tok)],
        [(flat16, tok), (flat32, tok), (flat32, tok), (ends, None)],
        [pltpu.VMEM((2,) + ends.shape, wide)],
        backwards=True,
        cost=70,
    )
    back = back.reshape(rows, 8, w_slot)[:, 0]
    back, mixed, near_three = together(back, mixed, at.near_parts(chip_three))

    def by_owner(array):
        split = array.reshape(half_z, 2, w_own, -1)
        keep = lax.dynamic_index_in_dim(split, at.c, 1, False)
        got = at.to_core(lax.dynamic_index_in_dim(split, 1 - at.c, 1, False))
        return at.by_core(keep, got).reshape(z_count, w_own, -1)

    own = jnp.stack([summary[0], back])
    after = [at.to_z(own, -by) for by in range(1, z_count)]
    grad_out = dot_tn(mixed, gr_all)
    after, grad_out, w2_sum = together(after, grad_out, w2_sum)
    carry_in = jnp.zeros((rows, w_slot), wide)
    for part in reversed(after):
        carry_in = part[1] + part[0] * carry_in
    mlp_pairs = at.exchange_core(summed(w2_sum).reshape(k_count, 2, d_own, 2 * f_slot))
    carry_in, mlp_pairs = together(carry_in, mlp_pairs)
    mlp_back = at.exchange_dp(mlp_pairs)
    grad_conv, rec_small, vectors = kernel_call(
        functools.partial(adjoint_kernel, rows, span),
        steps,
        [
            (back_part, tok),
            (back_run, tok),
            (by_row(carry_in), None),
            (state, tok),
            (state_in, None),
            (conv_low, tok),
            (w_gates, None),
            (params, None),
            (masks, tok),
            (conv_in, tok),
            (conv_before, None),
        ],
        [(flat16, tok), (shape((w_slot, 2 * BS), low), None), (shape((8, w_slot), wide), None)],
        [
            pltpu.VMEM((w_slot, 2 * w_slot), wide),
            pltpu.VMEM((8, w_slot), wide),
            pltpu.VMEM((span + 8, w_slot), wide),
            pltpu.VMEM(ends.shape, wide),
            pltpu.VMEM(ends.shape, wide),
        ],
    )
    grad_conv, near_three, mlp_back, rec_small, vectors = together(
        grad_conv, near_three, mlp_back, rec_small, vectors
    )
    block_out = (resid + at.far_product(near_three)).astype(low)
    head = at.to_z(grad_conv.reshape(2, rows, span, w_slot)[0, :, :16], -1).reshape(rows * 16, w_slot)
    rec_part = at.own_apart(by_owner(jnp.concatenate([grad_out.astype(low), rec_small], axis=1)), 0)
    head, rec_part = together(head, rec_part)
    rec_sum = at.scatter_z(rec_part)
    (grad_one,) = kernel_call(
        functools.partial(conv_back_kernel, rows, span),
        1,
        [(array, None) for array in (grad_conv, head, masks, masks_after, grad_branch, params)],
        [(shape((tok_all, 2 * w_slot), low), None)],
        [pltpu.VMEM((span + 8, w_slot), wide)],
    )

    grad_one, block_out = together(grad_one, block_out)
    other_one, got_one = at.chip_send(grad_one, w1, 1)
    other_one, then = together(other_one, grad_one)
    w1_part = rows_apart(n1_all, then)
    then, w1_part = together(then, w1_part)
    near_one = at.near_parts(at.chip_own(then, w1, got_one, 1))
    w1_sum = at.scatter_z(w1_part)
    mlp_whole = jax.ShapeDtypeStruct(mlp_gate.shape, wide)
    join = functools.partial(join_kernel, k_count, z_count)
    grad_gate_w, grad_up_w = in_vmem(join, (mlp_back,), (mlp_whole, mlp_whole))
    vectors = at.sum_z(vectors)
    vectors = at.by_core(vectors, at.to_core(vectors))
    near_one, grad_gate_w, grad_up_w, down_sum, vectors = together(
        near_one, grad_gate_w, grad_up_w, down_sum, vectors
    )
    vectors = lax.dynamic_index_in_dim(vectors, at.s // z_count, 0, False)
    grad_small = lax.dynamic_slice_in_dim(vectors, at.s % z_count * w_own, w_own, 1)
    grad_n1 = at.far_product(near_one)
    w1_sum, grad_n1, rec_sum = together(w1_sum, grad_n1, rec_sum)
    rec_pairs = at.exchange_core(summed(w1_sum).reshape(k_count, 2, d_own, 2 * w_slot))
    rec_pairs, grad_n1, rec_sum = together(rec_pairs, grad_n1, rec_sum)
    rec_back = at.exchange_dp(rec_pairs)
    scaled_one = gain_one * grad_n1
    mean_one = jnp.mean(scaled_one * inputs, axis=-1, keepdims=True)
    grad_tokens = grad_resid + s1 * scaled_one - inputs * (s1 * s1 * s1) * mean_one
    grad_tokens = grad_tokens.reshape(row_dev, span, width_d)
    block_out = block_out.reshape(row_dev, span, width_d)

    rec_rows = summed(rec_sum)
    grad_out_w = rec_rows[:, :width_d]
    grad_rate_w = rec_rows[:, width_d : width_d + BS]
    grad_igate_w = rec_rows[:, width_d + BS : width_d + 2 * BS]
    grad_down = summed(down_sum)
    rec_back = jnp.moveaxis(rec_back, 2, 0)
    grad_branch_w = rec_back[..., :w_slot].reshape(d_own, width_r)
    grad_input_w = rec_back[..., w_slot:].reshape(d_own, width_r)

    def gain_grad(pairs, gain):
        total = sum(jnp.sum(weight.astype(wide) * grad, axis=1) for weight, grad in pairs)
        return total / gain.astype(wide)

    grad_norm_one = gain_grad(((branch_weight, grad_branch_w), (input_proj, grad_input_w)), norm_one)
    grad_norm_two = gain_grad(((mlp_gate, grad_gate_w), (mlp_up, grad_up_w)), norm_two)
    return (
        block_out,
        grad_tokens,
        grad_norm_one,
        grad_branch_w,
        grad_input_w,
        grad_small[:taps],
        grad_small[taps],
        grad_rate_w,
        grad_igate_w,
        grad_small[taps + 1],
        grad_small[taps + 2],
        grad_small[taps + 3],
        grad_out_w,
        grad_norm_two,
        grad_gate_w,
        grad_up_w,
        grad_down,
    )


def solution(mesh):
    rows, matrix = P(AXES), P(AXES, None)
    tokens = P("dp", "seq", None)
    return jax.shard_map(
        per_device,
        mesh=mesh,
        in_specs=(
            tokens,
            P("dp", "seq"),
            tokens,
            rows,
            matrix,
            matrix,
            P(None, AXES),
            rows,
            matrix,
            matrix,
            rows,
            rows,
            rows,
            matrix,
            rows,
            matrix,
            matrix,
            matrix,
        ),
        out_specs=(
            tokens,
            tokens,
            rows,
            matrix,
            matrix,
            P(None, AXES),
            rows,
            matrix,
            matrix,
            rows,
            rows,
            rows,
            matrix,
            rows,
            matrix,
            matrix,
            matrix,
        ),
        check_vma=False,
    )
```

```python
import functools

import jax
import jax.numpy as jnp
from jax import lax
from jax.experimental import pallas as pl
from jax.experimental.pallas import tpu as pltpu
from jax.sharding import PartitionSpec as P

HEADS = 16
BS = 160
AXES = ("dp", "seq")

eps_value = 1e-06
rate_scale = 8.0
floor_value = 0.001
low = jnp.bfloat16
wide = jnp.float32


def gelu_tanh(value):
    return jax.nn.gelu(value, approximate=True)


def dot_nn(left, right):
    return lax.dot_general(left, right, (((1,), (0,)), ((), ())), preferred_element_type=wide)


def dot_nt(left, right):
    return lax.dot_general(left, right, (((1,), (1,)), ((), ())), preferred_element_type=wide)


def dot_tn(left, right):
    return lax.dot_general(left, right, (((0,), (0,)), ((), ())), preferred_element_type=wide)


def lay_out_kernel(count, c_ref, *refs):
    parts, (out_ref, buffer, sem, out_sem) = refs[: 2 * count], refs[2 * count :]
    core = c_ref[0]
    copies = []
    for which in range(2):
        start = (core if which == 0 else 1 - core) * (out_ref.shape[0] // 2)
        for i, part in enumerate(parts[which * count : (which + 1) * count]):
            at = pl.ds(pl.multiple_of(start, 16), part.shape[0])
            j = which * count + i
            into = pltpu.make_async_copy(part, buffer.at[at], sem.at[j])
            into.start()
            copies.append((into, pltpu.make_async_copy(buffer.at[at], out_ref.at[at], out_sem.at[j])))
            start = start + part.shape[0]
    for into, out in copies:
        into.wait()
        out.start()
    for into, out in copies:
        out.wait()


def lay_out(core, own, other):
    rows = 2 * sum(part.shape[0] for part in own)
    shape = (rows,) + own[0].shape[1:]
    anywhere = pl.BlockSpec(memory_space=pl.ANY)
    return pl.pallas_call(
        functools.partial(lay_out_kernel, len(own)),
        out_shape=jax.ShapeDtypeStruct(shape, own[0].dtype),
        in_specs=[pl.BlockSpec(memory_space=pltpu.SMEM)] + [anywhere] * (2 * len(own)),
        out_specs=anywhere,
        scratch_shapes=[
            pltpu.VMEM(shape, own[0].dtype),
            pltpu.SemaphoreType.DMA((2 * len(own),)),
            pltpu.SemaphoreType.DMA((2 * len(own),)),
        ],
        compiler_params=pltpu.CompilerParams(vmem_limit_bytes=32 * 2**20),
    )(core.reshape(1).astype(jnp.int32), *own, *other)


def together(*arrays):
    return lax.optimization_barrier(arrays)


def cut_kernel(k_count, z_count, gate_ref, up_ref, out_ref):
    own = out_ref.shape[3] // (2 * z_count)
    for k in range(k_count):
        for c in range(2):
            for which, ref in enumerate((gate_ref, up_ref)):
                for z in range(z_count):
                    at = ((k * z_count + z) * 2 + c) * own
                    to = (which * z_count + z) * own
                    out_ref[k, c, :, to : to + own] = ref[:, at : at + own]


def join_kernel(k_count, z_count, in_ref, gate_ref, up_ref):
    own = in_ref.shape[3] // (2 * z_count)
    for k in range(k_count):
        for c in range(2):
            for which, ref in enumerate((gate_ref, up_ref)):
                for z in range(z_count):
                    to = ((k * z_count + z) * 2 + c) * own
                    at = (which * z_count + z) * own
                    ref[:, to : to + own] = in_ref[k, c, :, at : at + own].astype(ref.dtype)


def in_vmem(kernel, arrays, out_shape):
    vmem = pl.BlockSpec(memory_space=pltpu.VMEM)
    return pl.pallas_call(
        kernel,
        out_shape=out_shape,
        in_specs=[vmem] * len(arrays),
        out_specs=jax.tree.map(lambda _: vmem, out_shape),
        compiler_params=pltpu.CompilerParams(vmem_limit_bytes=48 * 2**20),
    )(*arrays)


class Place:
    def __init__(self):
        self.k_count = lax.axis_size("dp")
        self.s_count = lax.axis_size("seq")
        self.z_count = self.s_count // 2
        self.k = lax.axis_index("dp")
        self.s = lax.axis_index("seq")
        self.c = self.s % 2
        self.z = self.s // 2
        self.square = self.k_count == 4
        self.z_groups = [
            [k * self.s_count + 2 * z + c for z in range(self.z_count)]
            for k in range(self.k_count)
            for c in range(2)
        ]
        self.plane_groups = [
            [k * self.s_count + 2 * z + c for k in range(self.k_count) for c in range(2)]
            for z in range(self.z_count)
        ]

    def to_k(self, array, flip):
        return lax.ppermute(array, "dp", [(i, i ^ flip) for i in range(self.k_count)])

    def to_core(self, array):
        return lax.ppermute(array, "seq", [(i, i ^ 1) for i in range(self.s_count)])

    def to_z(self, array, by):
        pairs = [(i, i + 2 * by) for i in range(self.s_count) if 0 <= i + 2 * by < self.s_count]
        return lax.ppermute(array, "seq", pairs)

    def by_core(self, own, other):
        return jnp.where(self.c == 0, jnp.stack([own, other]), jnp.stack([other, own]))

    def gather_z(self, array):
        return lax.all_gather(array, AXES, axis_index_groups=self.z_groups, tiled=True)

    def z_pairs(self, pairs):
        return [(2 * a + c, 2 * b + c) for a, b in pairs for c in range(2)]

    def own_apart(self, split, axis):
        shape = [1] * split.ndim
        shape[axis] = self.z_count
        own = (jnp.arange(self.z_count) == self.z).reshape(shape)
        sent = jnp.moveaxis(jnp.where(own, 0.0, split).astype(low), axis, 0)
        kept = lax.dynamic_index_in_dim(split, self.z, axis, False)
        return sent.reshape((-1,) + sent.shape[-1:]), kept.reshape((-1,) + sent.shape[-1:])

    def scatter_z(self, parts):
        total = lax.psum_scatter(
            parts[0], AXES, scatter_dimension=0, axis_index_groups=self.z_groups, tiled=True
        )
        return total, parts[1]


    def sum_far(self, chunk):
        if self.z_count != 4:
            return ()
        pairs = self.z_pairs([(0, 1), (3, 2)])
        return (lax.ppermute(chunk(3 - self.z).astype(low), "seq", pairs),)

    def sum_near(self, chunk):
        if self.z_count != 4:
            return ()
        below = self.to_z(chunk(jnp.minimum(self.z + 1, 3)).astype(low), 1)
        above = self.to_z(chunk(jnp.maximum(self.z - 1, 0)).astype(low), -1)
        return below, above

    def sum_second(self, chunk, far):
        if self.z_count != 4:
            return ()
        second = (chunk(self.z ^ 2).astype(wide) + far[0].astype(wide)).astype(low)
        return (lax.ppermute(second, "seq", self.z_pairs([(0, 2), (1, 3), (2, 0), (3, 1)])),)

    def sum_all(self, sent, kept, near, second):
        total = kept.astype(wide)
        if self.z_count != 4:
            whole = lax.psum_scatter(
                sent.reshape(-1, sent.shape[-1]),
                AXES,
                scatter_dimension=0,
                axis_index_groups=self.z_groups,
                tiled=True,
            )
            return total + whole.astype(wide)
        for part in near + second:
            total = total + part.astype(wide)
        return total

    def sum_z(self, array):
        if self.z_count != 4:
            return lax.psum(array, AXES, axis_index_groups=self.z_groups)
        for flip in range(1, 3):
            array = array + lax.ppermute(array, "seq", self.z_pairs([(z, z ^ flip) for z in range(4)]))
        return array

    def gather_seq_small(self, array):
        if self.s_count != 8:
            return lax.all_gather(array, "seq")
        out = array[None]
        for bit in range(3):
            got = lax.ppermute(out, "seq", [(i, i ^ (1 << bit)) for i in range(8)])
            low_bit = (self.s >> bit) % 2 == 0
            out = jnp.where(low_bit, jnp.concatenate([out, got]), jnp.concatenate([got, out]))
        return out

    def gather_dp_small(self, array):
        if not self.square:
            return lax.all_gather(array, "dp")
        out = array[None]
        for bit in range(2):
            got = self.to_k(out, 1 << bit)
            low_bit = (self.k >> bit) % 2 == 0
            out = jnp.where(low_bit, jnp.concatenate([out, got]), jnp.concatenate([got, out]))
        return out

    def gather_plane(self, array):
        if not self.square:
            whole = lax.all_gather(array, AXES, axis_index_groups=self.plane_groups)
            whole = whole.reshape((self.k_count, 2) + array.shape)
            return jnp.swapaxes(whole, 0, 1).reshape((-1,) + array.shape[1:])
        return self.gather_end(self.gather_far(self.gather_near(array)))

    def gather_near(self, array):
        if not self.square:
            return (array,)
        return array, self.to_k(array, 1), self.to_k(array, 2)

    def gather_far(self, near):
        if not self.square:
            return near
        array, from_x, from_y = near
        half = array.shape[0] // 2
        return array, from_x, from_y, self.to_k(from_x[:half], 2), self.to_k(from_y[half:], 1)

    def gather_core(self, mine):
        if not self.square:
            return [self.gather_plane(mine[0])], None
        return list(mine), [self.to_core(part) for part in mine]

    def gather_end(self, mine):
        if not self.square:
            return self.gather_plane(mine[0])
        return lay_out(self.c, mine, [self.to_core(part) for part in mine])

    def gather_rows(self, array):
        if not self.square:
            return lax.all_gather(array, "dp", tiled=True)
        array = jnp.concatenate([array, self.to_k(array, 1)])
        return jnp.concatenate([array, self.to_k(array, 2)])

    def gather_plane_small(self, array):
        if not self.square:
            return self.gather_plane(array)
        near = jnp.stack([array, self.to_k(array, 1)])
        mine = jnp.concatenate([near, self.to_k(near, 2)])
        return self.by_core(mine, self.to_core(mine)).reshape((-1,) + array.shape[1:])

    def halves(self, array):
        count = array.shape[0] // 2
        own = lax.dynamic_slice_in_dim(array, self.c * count, count, 0)
        return own, lax.dynamic_slice_in_dim(array, (1 - self.c) * count, count, 0)

    def chip_product(self, left, right, dot, exact=False):
        own, other = self.halves(left)
        count = own.shape[0] // 2
        got = []
        for i in range(2):
            part = dot(other[i * count : (i + 1) * count], right)
            if exact:
                part = self.pack(part, self.power_of(part))
                got.append(self.unpack(self.to_core(part))[0])
            else:
                got.append(self.to_core(part.astype(low)).astype(wide))
        chip = []
        for i in range(2):
            part = dot(own[i * count : (i + 1) * count], right) + got[i]
            chip += list(part.reshape(self.k_count // 2, -1, part.shape[-1]))
        return chip

    def power_of(self, values):
        largest = jnp.max(jnp.abs(values), axis=-1, keepdims=True)
        return jnp.ceil(jnp.log2(jnp.clip(largest, 1e-30, 1e37)))

    def pack(self, parts, power):
        scaled = (parts * jnp.exp2(-power)).astype(jnp.float16)
        power = jnp.broadcast_to(power, power.shape[:-1] + (128,)).astype(jnp.float16)
        return jnp.concatenate([scaled, power], axis=-1)

    def unpack(self, got):
        got = got.astype(wide)
        width = got.shape[-1] - 128
        power = got[..., width : width + 1]
        return got[..., :width] * jnp.exp2(power), power

    def chip_send(self, left, right, side):
        if not self.square:
            return None, None
        other = other_call(self.c, left, right, left.shape[0] // 8, side)
        return other, self.to_core(other)

    def chip_own(self, left, right, got, side):
        if not self.square:
            return self.chip_product(left, right, dot_nt if side else dot_nn)
        return own_call(self.c, left, right, got, left.shape[0] // 8, side)

    def near_parts(self, parts):
        if not self.square:
            return self.near_plane(parts)
        chip, next_a, next_b, a, b = parts
        return (chip, next_a, next_b, *together(self.to_k(a, 1), self.to_k(b, 2)))

    def far_product(self, near):
        if not self.square:
            return self.far_plane(near)
        chip, next_a, next_b, got_a, got_b = near
        half = next_a.shape[1]
        got_a, got_b = got_a.astype(wide), got_b.astype(wide)
        own_a, own_b = chip[:, :half] + got_a[0], chip[:, half:] + got_b[0]
        return self.last_plane(next_a + got_a[1], next_b + got_b[1], None, None, own_a, own_b)

    def near_plane(self, chip, exact=False):
        if not self.square:
            return (lax.psum_scatter(jnp.stack(chip), "dp", scatter_dimension=0, tiled=False),)
        half = chip[0].shape[1] // 2
        power = [self.power_of(part) for part in chip] if exact else None

        def pick(a, i, j):
            return a if a is None else jnp.stack([a[i], a[j]])

        got_a = self.send_plane(jnp.stack([chip[1][:, :half], chip[3][:, :half]]), pick(power, 1, 3), 1)
        got_b = self.send_plane(jnp.stack([chip[2][:, half:], chip[3][:, half:]]), pick(power, 2, 3), 2)
        got_a, got_b = together(got_a, got_b)
        return chip, power, got_a, got_b

    def send_plane(self, parts, power, flip):
        if power is None:
            return self.to_k(parts.astype(low), flip), None
        return self.unpack(self.to_k(self.pack(parts, power), flip))

    def far_plane(self, near):
        if not self.square:
            return near[0]
        chip, power, (got_a, power_a), (got_b, power_b) = near
        half = chip[0].shape[1] // 2
        got_a, got_b = got_a.astype(wide), got_b.astype(wide)

        def above(a, i, b, j):
            return a if a is None else jnp.maximum(a[i], b[j]) + 1.0

        next_a, next_b = chip[2][:, :half] + got_a[1], chip[1][:, half:] + got_b[1]
        return self.last_plane(
            next_a,
            next_b,
            above(power_a, 1, power, 2),
            above(power_b, 1, power, 1),
            chip[0][:, :half] + got_a[0],
            chip[0][:, half:] + got_b[0],
        )

    def last_plane(self, next_a, next_b, power_a, power_b, own_a, own_b):
        if power_a is None:
            next_a, next_b = together(next_a.astype(low), next_b.astype(low))
            last_a, last_b = self.to_k(next_a, 2).astype(wide), self.to_k(next_b, 1).astype(wide)
        else:
            next_a, next_b = together(self.pack(next_a, power_a), self.pack(next_b, power_b))
            last_a, last_b = self.unpack(self.to_k(next_a, 2))[0], self.unpack(self.to_k(next_b, 1))[0]
        return jnp.concatenate([own_a + last_a, own_b + last_b], axis=1)

    def sum_plane(self, chip, exact=False):
        return self.far_plane(self.near_plane(chip, exact))

    def exchange_plane(self, array):
        return self.exchange_dp(self.exchange_core(array))

    def exchange_core(self, array):
        keep = lax.dynamic_index_in_dim(array, self.c, 1, False)
        got = self.to_core(lax.dynamic_index_in_dim(array, 1 - self.c, 1, False))
        return jnp.moveaxis(self.by_core(keep, got), 0, 1)

    def exchange_dp(self, pairs):
        if not self.square:
            return lax.all_to_all(pairs, "dp", 0, 0, tiled=True)
        parts = [lax.dynamic_index_in_dim(pairs, self.k, 0, False)]
        for flip in range(1, 4):
            parts.append(self.to_k(lax.dynamic_index_in_dim(pairs, self.k ^ flip, 0, False), flip))
        odd = self.k % 2 == 1
        parts = [jnp.where(odd, parts[i ^ 1], parts[i]) for i in range(4)]
        upper = self.k >= 2
        return jnp.stack([jnp.where(upper, parts[i ^ 2], parts[i]) for i in range(4)])


def gelu_pair(x):
    slope = 0.7978845608028654
    inner = jnp.tanh(slope * (x + 0.044715 * x * x * x))
    half = 0.5 * (1.0 + inner)
    return x * half, half + 0.5 * x * (1.0 - inner * inner) * slope * (1.0 + 0.134145 * x * x)


def rms_normed(values, gain):
    values = values.astype(wide)
    scale = lax.rsqrt(jnp.mean(values * values, axis=1, keepdims=True) + eps_value)
    return (values * scale * gain).astype(low)


def ordered(values, order):
    if order is None:
        return values
    size = values.shape[1] // len(order)
    return jnp.concatenate([values[:, i * size : (i + 1) * size] for i in order], axis=1)


def minus_expm1(x):
    near = 1.0
    for i in range(8, 1, -1):
        near = 1.0 + near * x * (1.0 / i)
    return jnp.where(x > -0.5, -x * near, 1.0 - jnp.exp(x))


def gates_of(conv_low, w_gates, params, not_start):
    width = conv_low.shape[1]
    pre = jnp.dot(conv_low, w_gates, preferred_element_type=wide)
    rate = jax.nn.sigmoid(pre[:, :width] + params[5:6])
    igate = jax.nn.sigmoid(pre[:, width:] + params[6:7])
    log_keep = params[7:8] * rate
    room = minus_expm1(2.0 * log_keep)
    mult = jnp.where(not_start > 0.5, jnp.sqrt(jnp.maximum(room, floor_value)), 1.0)
    return rate, igate, jnp.exp(log_keep), room, mult


def shifted(values, by, fill):
    count = values.shape[0]
    size = abs(by)
    if size % 8 == 0:
        free = jnp.full((size, values.shape[1]), fill, values.dtype)
        if by > 0:
            return jnp.concatenate([free, values[: count - size]])
        return jnp.concatenate([values[size:], free])
    place = lax.broadcasted_iota(jnp.int32, values.shape, 0)
    moved = pltpu.roll(values, by % count, 0)
    return jnp.where(place >= by if by > 0 else place < count - size, moved, fill)


def scan_rows(keep, drive, sign):
    by = 1
    while by < keep.shape[0]:
        drive = drive + keep * shifted(drive, sign * by, 0.0)
        keep = keep * shifted(keep, sign * by, 1.0)
        by *= 2
    return keep, drive


def conv_kernel(
    rows, span, order, x_ref, w_ref, halo_ref, gain_ref, params_ref, gates_ref,
    normed_ref, masks_ref, branch_ref, in_ref, low_ref, keep_ref, part_ref, run_ref, sums_ref, before_ref, tail, line, ends,
):
    step = pl.program_id(0)
    width = in_ref.shape[1]
    count = x_ref.shape[0]
    row_dev = count // span

    @pl.when(step == 0)
    def _():
        normed = rms_normed(halo_ref[...], gain_ref[...])
        before = jnp.dot(ordered(normed, order), w_ref[:, width:], preferred_element_type=wide)
        tail[...] = before.astype(low).astype(wide)
        before_ref[...] = tail[...]

    features = gain_ref.shape[1]
    normed = rms_normed(x_ref[:, :features], gain_ref[...])
    normed_ref[...] = normed
    masks_ref[...] = x_ref[:, features : features + 8].astype(wide)
    pre = jnp.dot(ordered(normed, order), w_ref[...], preferred_element_type=wide)
    branch_ref[...] = pre[:, :width]
    conv_in = pre[:, width:].astype(low)
    in_ref[...] = conv_in
    conv_in = conv_in.astype(wide)
    params = params_ref[...]
    for row in range(row_dev):
        at = slice(row * span, (row + 1) * span)
        own = conv_in[at]
        place = pl.ds(pl.multiple_of((lax.rem(step * row_dev + row, rows)) * 8, 8), 8)
        line[:8] = tail[place]
        line[8:] = own
        tail[place] = own[span - 8 :]
        masks = masks_ref[at]
        total = params[4:5] + params[0:1] * own
        for by in range(1, 4):
            total = total + params[by : by + 1] * line[8 - by : 8 - by + span] * masks[:, by - 1 : by]
        conv_low = total.astype(low)
        low_ref[at] = conv_low
        not_start = masks[:, 3:4]
        rate, igate, keep, room, mult = gates_of(conv_low, gates_ref[...], params, not_start)
        keep = keep * not_start
        keep_ref[at] = keep
        run, part = scan_rows(keep, mult * igate * conv_low.astype(wide), 1)

        @pl.when(step * row_dev < rows)
        def _(run=run, part=part, place=place, at=at):
            run_ref[at] = run
            part_ref[at] = part
            ends[0, place] = run[span - 8 :]
            ends[1, place] = part[span - 8 :]

        @pl.when(step * row_dev >= rows)
        def _(run=run, part=part, place=place, at=at):
            part = part + run * ends[1, place][7:8]
            run = run * ends[0, place][7:8]
            run_ref[at] = run
            part_ref[at] = part
            sums_ref[0, place] = run[span - 8 :]
            sums_ref[1, place] = part[span - 8 :]


def state_kernel(rows, span, part_ref, run_ref, start_ref, branch_ref, state_ref, mixed_ref):
    step = pl.program_id(0)
    row_dev = part_ref.shape[0] // span
    for row in range(row_dev):
        at = slice(row * span, (row + 1) * span)
        place = pl.ds(pl.multiple_of((lax.rem(step * row_dev + row, rows)) * 8, 8), 8)
        state = part_ref[at] + run_ref[at] * start_ref[place][7:8]
        state_ref[at] = state
        value, _ = gelu_pair(branch_ref[at])
        mixed_ref[at] = (value * state).astype(low)


def mlp_kernel(x_ref, cot_ref, w_ref, down_ref, hidden_ref, grad_ref):
    width = hidden_ref.shape[1]
    pre = jnp.dot(x_ref[...], w_ref[...], preferred_element_type=wide)
    grad = lax.dot_general(
        cot_ref[...], down_ref[...], (((1,), (1,)), ((), ())), preferred_element_type=wide
    )
    up = pre[:, width:]
    value, slope = gelu_pair(pre[:, :width])
    hidden_ref[...] = (value * up).astype(low)
    grad_ref[:, :width] = (grad * up * slope).astype(low)
    grad_ref[:, width:] = (grad * value).astype(low)


def other_kernel(side, core_ref, x_ref, w_ref, out_ref):
    product = lax.dot_general(
        x_ref[...], w_ref[...], (((1,), (side,)), ((), ())), preferred_element_type=wide
    )
    out_ref[...] = product.astype(low)


def own_kernel(side, core_ref, x_ref, w_ref, got_ref, chip_ref, next_a_ref, next_b_ref, a_ref, b_ref):
    step = pl.program_id(0)
    product = lax.dot_general(
        x_ref[...], w_ref[...], (((1,), (side,)), ((), ())), preferred_element_type=wide
    )
    product = product + got_ref[...].astype(wide)
    half = product.shape[1] // 2

    @pl.when(step == 0)
    def _():
        chip_ref[...] = product

    @pl.when(step == 1)
    def _():
        next_b_ref[...] = product[:, half:]

    @pl.when(step == 2)
    def _():
        next_a_ref[...] = product[:, :half]

    @pl.when((step == 1) | (step == 3))
    def _():
        a_ref[0] = product[:, :half].astype(low)

    @pl.when(step >= 2)
    def _():
        b_ref[0] = product[:, half:].astype(low)


def back_kernel(
    rows, span, x_ref, w_ref, branch_ref, state_ref, keep_ref, grad_branch_ref, part_ref, run_ref, sum_ref, ends
):
    step = pl.program_id(0)
    count = x_ref.shape[0]
    row_dev = count // span
    mixed = lax.dot_general(
        x_ref[...], w_ref[...], (((1,), (1,)), ((), ())), preferred_element_type=wide
    )
    late = step * row_dev < rows
    for row in range(row_dev):
        at = slice(row * span, (row + 1) * span)
        block = (pl.num_programs(0) - 1 - step) * row_dev + row
        place = pl.ds(pl.multiple_of(lax.rem(block, rows) * 8, 8), 8)
        value, slope = gelu_pair(branch_ref[at])
        grad_branch_ref[at] = (mixed[at] * state_ref[at] * slope).astype(low)
        grad = mixed[at] * value
        keep = keep_ref[at]
        run, part = scan_rows(keep, keep * grad, -1)

        @pl.when(late)
        def _(run=run, part=part, grad=grad, place=place, at=at):
            ends[0, place] = run[:8]
            ends[1, place] = part[:8]
            run_ref[at] = shifted(run, -1, 1.0)
            part_ref[at] = grad + shifted(part, -1, 0.0)

        @pl.when(jnp.logical_not(late))
        def _(run=run, part=part, grad=grad, place=place, at=at):
            next_run, next_part = ends[0, place][:1], ends[1, place][:1]
            part = part + run * next_part
            run = run * next_run
            last = lax.broadcasted_iota(jnp.int32, run.shape, 0) == span - 1
            run_ref[at] = jnp.where(last, next_run, shifted(run, -1, 1.0))
            part_ref[at] = grad + jnp.where(last, next_part, shifted(part, -1, 0.0))
            sum_ref[place] = part[:8]


def adjoint_kernel(
    rows, span, part_ref, run_ref, carry_ref, state_ref, start_ref, low_ref, gates_ref, params_ref,
    masks_ref, in_ref, before_ref, grad_conv_ref, small_ref, vectors_ref, gates_grad_ref, sums_ref, line, ends, tail,
):
    step = pl.program_id(0)
    width = low_ref.shape[1]
    row_dev = low_ref.shape[0] // span
    params = params_ref[...]

    @pl.when(step == 0)
    def _():
        gates_grad_ref[...] = jnp.zeros(gates_grad_ref.shape, wide)
        sums_ref[...] = jnp.zeros(sums_ref.shape, wide)
        ends[...] = start_ref[...]
        tail[...] = before_ref[...]

    for row in range(row_dev):
        at = slice(row * span, (row + 1) * span)
        place = pl.ds(pl.multiple_of((lax.rem(step * row_dev + row, rows)) * 8, 8), 8)
        conv_low = low_ref[at]
        conv_value = conv_low.astype(wide)
        masks = masks_ref[at]
        not_start = masks[:, 3:4]
        rate, igate, keep, room, mult = gates_of(conv_low, gates_ref[...], params, not_start)
        adj = part_ref[at] + run_ref[at] * carry_ref[place][:1]
        state = state_ref[at]
        line[:8] = ends[place]
        line[8:] = state
        ends[place] = state[span - 8 :]
        through = adj * line[7 : 7 + span]
        spread = jnp.where(room > floor_value, adj * igate * conv_value * keep * keep / mult, 0.0)
        grad_log = not_start * (through * keep - spread)
        grad_rate = (grad_log * params[7:8] * rate * (1.0 - rate)).astype(low)
        scaled = adj * mult
        grad_igate = (scaled * conv_value * igate * (1.0 - igate)).astype(low)
        both = jnp.concatenate([grad_rate, grad_igate], axis=1)
        grad_conv = scaled * igate + lax.dot_general(
            both, gates_ref[...], (((1,), (1,)), ((), ())), preferred_element_type=wide
        )
        grad_conv = grad_conv.astype(low)
        grad_conv_ref[at] = grad_conv
        gates_grad_ref[...] += lax.dot_general(
            conv_low, both, (((0,), (0,)), ((), ())), preferred_element_type=wide
        )
        grad_conv = grad_conv.astype(wide)
        conv_in = in_ref[at].astype(wide)
        line[:8] = tail[place]
        line[8:] = conv_in
        tail[place] = conv_in[span - 8 :]
        values = [grad_conv * conv_in]
        for by in range(1, 4):
            values.append(grad_conv * line[8 - by : 8 - by + span] * masks[:, by - 1 : by])
        values += [grad_conv, grad_rate.astype(wide), grad_igate.astype(wide), grad_log * rate * params[8:9]]
        for i, value in enumerate(values):
            sums_ref[i : i + 1] += jnp.sum(value, axis=0, keepdims=True)

    @pl.when(step == pl.num_programs(0) - 1)
    def _():
        block = small_ref.shape[1] // 2
        for head in range(width // block):
            at = slice(head * block, (head + 1) * block)
            small_ref[at, :block] = gates_grad_ref[at, at].astype(low)
            then = slice(width + head * block, width + (head + 1) * block)
            small_ref[at, block:] = gates_grad_ref[at, then].astype(low)
        vectors_ref[...] = sums_ref[...]


def conv_back_kernel(rows, span, grad_ref, halo_ref, masks_ref, halo_masks_ref, branch_ref, params_ref, one_ref, line):
    params = params_ref[...]

    def work(block, grad_next, masks_next):
        at = pl.ds(pl.multiple_of(block * span, 16), span)
        own = grad_ref[at].astype(wide)
        total = params[0:1] * own
        masks = masks_ref[at]
        for by in range(1, 4):
            line[:span] = own * masks[:, by - 1 : by]
            line[span:] = grad_next * masks_next[:, by - 1 : by]
            total = total + params[by : by + 1] * line[by : by + span]
        width = branch_ref.shape[1]
        one_ref[at, :width] = branch_ref[at]
        one_ref[at, width:] = total.astype(low)

    @pl.loop(0, rows)
    def _(block):
        then = pl.ds(pl.multiple_of((block + rows) * span, 16), 16)
        work(block, grad_ref[then].astype(wide)[:8], masks_ref[then][:8])

    @pl.loop(0, rows)
    def _(block):
        then = pl.ds(pl.multiple_of(block * 16, 16), 16)
        work(block + rows, halo_ref[then].astype(wide)[:8], halo_masks_ref[then][:8])


def whole_block(array):
    return pl.BlockSpec(array.shape, lambda *i, n=len(array.shape): (0,) * n)


def token_block(array, count, steps, backwards):
    def index(i):
        return (steps - 1 - i if backwards else i,) + (0,) * (len(array.shape) - 1)

    return pl.BlockSpec((count,) + array.shape[1:], index)


def half_of(core, x, count, width):
    return pl.BlockSpec((count, width), lambda k, core_ref: (core_ref[0] * (x.shape[0] // (2 * count)) + k, 0))


def half_call(kernel, core, x, w, count, extra, outputs):
    def spec(array, block, index):
        return pl.BlockSpec(block, lambda k, core_ref: index(k))

    return pl.pallas_call(
        kernel,
        out_shape=[array for array, _, _ in outputs],
        grid_spec=pltpu.PrefetchScalarGridSpec(
            num_scalar_prefetch=1,
            grid=(x.shape[0] // (2 * count),),
            in_specs=[
                half_of(core, x, count, x.shape[1]),
                pl.BlockSpec(w.shape, lambda k, core_ref: (0, 0)),
            ]
            + [spec(*one) for one in extra],
            out_specs=[spec(*one) for one in outputs],
        ),
        cost_estimate=pl.CostEstimate(flops=0, bytes_accessed=0, transcendentals=0),
        compiler_params=pltpu.CompilerParams(vmem_limit_bytes=60 * 2**20),
    )(core.reshape(1).astype(jnp.int32), x, w, *[array for array, _, _ in extra])


def other_call(core, x, w, count, side):
    width = w.shape[1 - side]
    out = jax.ShapeDtypeStruct((x.shape[0] // 2, width), low)
    kernel = functools.partial(other_kernel, side)
    return half_call(kernel, 1 - core, x, w, count, [], [(out, (count, width), lambda k: (k, 0))])[0]


def own_call(core, x, w, got, count, side):
    width = w.shape[1 - side]
    a = jax.ShapeDtypeStruct((2, count, width // 2), low)
    chip = jax.ShapeDtypeStruct((count, width), wide)
    after = jax.ShapeDtypeStruct((count, width // 2), wide)
    return half_call(
        functools.partial(own_kernel, side),
        core,
        x,
        w,
        count,
        [(got, (count, width), lambda k: (k, 0))],
        [
            (chip, chip.shape, lambda k: (0, 0)),
            (after, after.shape, lambda k: (0, 0)),
            (after, after.shape, lambda k: (0, 0)),
            (a, (1, count, width // 2), lambda k: (k // 2, 0, 0)),
            (a, (1, count, width // 2), lambda k: (k // 3, 0, 0)),
        ],
    )


def rows_kernel(core_ref, x_ref, grad_ref, sent_ref, kept_ref):
    count = kept_ref.shape[1]
    total = lax.dot_general(
        x_ref[...], grad_ref[...], (((0,), (0,)), ((), ())), preferred_element_type=wide
    )
    planes = sent_ref.shape[0]
    first = lax.rem(pl.program_id(0), core_ref[1]) * planes
    for i in range(planes):
        part = total[i * count : (i + 1) * count]
        mine = first + i == core_ref[0]
        sent_ref[i, 0] = jnp.where(mine, jnp.zeros_like(part), part).astype(low)

        @pl.when(mine)
        def _(part=part):
            kept_ref[0] = part


def rows_call(z, z_count, k_count, x, grad):
    tokens, features = x.shape
    count = features // (z_count * k_count)
    planes = max(2, 128 // count)
    width = grad.shape[1]
    per = z_count // planes
    sent = jax.ShapeDtypeStruct((z_count, k_count, count, width), low)
    kept = jax.ShapeDtypeStruct((k_count, count, width), wide)
    return pl.pallas_call(
        rows_kernel,
        out_shape=[sent, kept],
        grid_spec=pltpu.PrefetchScalarGridSpec(
            num_scalar_prefetch=1,
            grid=(k_count * per,),
            in_specs=[
                pl.BlockSpec((tokens, planes * count), lambda i, ref: (0, i)),
                pl.BlockSpec(grad.shape, lambda i, ref: (0, 0)),
            ],
            out_specs=[
                pl.BlockSpec((planes, 1, count, width), lambda i, ref: (i % per, i // per, 0, 0)),
                pl.BlockSpec((1, count, width), lambda i, ref: (i // per, 0, 0)),
            ],
        ),
        cost_estimate=pl.CostEstimate(flops=0, bytes_accessed=0, transcendentals=0),
        compiler_params=pltpu.CompilerParams(vmem_limit_bytes=60 * 2**20),
    )(jnp.stack([z, jnp.int32(per)]).astype(jnp.int32), x, grad)


def down_kernel(core_ref, hidden_ref, cot_ref, sent_ref, kept_ref):
    total = lax.dot_general(
        cot_ref[...], hidden_ref[...], (((0,), (0,)), ((), ())), preferred_element_type=wide
    )
    total = total.T
    count = kept_ref.shape[0]
    for i in range(sent_ref.shape[0]):
        part = total[i * count : (i + 1) * count]
        mine = core_ref[0] == i
        sent_ref[i] = jnp.where(mine, jnp.zeros_like(part), part).astype(low)

        @pl.when(mine)
        def _(part=part):
            kept_ref[...] = part


def down_call(z, z_count, hidden, cot):
    tokens, features = cot.shape
    count = hidden.shape[1] // z_count
    columns = 256
    sent = jax.ShapeDtypeStruct((z_count, count, features), low)
    kept = jax.ShapeDtypeStruct((count, features), wide)
    return pl.pallas_call(
        down_kernel,
        out_shape=[sent, kept],
        grid_spec=pltpu.PrefetchScalarGridSpec(
            num_scalar_prefetch=1,
            grid=(features // columns,),
            in_specs=[
                pl.BlockSpec(hidden.shape, lambda i, ref: (0, 0)),
                pl.BlockSpec((tokens, columns), lambda i, ref: (0, i)),
            ],
            out_specs=[
                pl.BlockSpec((z_count, count, columns), lambda i, ref: (0, 0, i)),
                pl.BlockSpec((count, columns), lambda i, ref: (0, i)),
            ],
        ),
        cost_estimate=pl.CostEstimate(flops=0, bytes_accessed=0, transcendentals=0),
        compiler_params=pltpu.CompilerParams(vmem_limit_bytes=60 * 2**20),
    )(z.reshape(1).astype(jnp.int32), hidden, cot)


def kernel_call(kernel, steps, inputs, outputs, scratch=(), backwards=False):
    def spec(array, count):
        return whole_block(array) if count is None else token_block(array, count, steps, backwards)

    return pl.pallas_call(
        kernel,
        out_shape=[array for array, _ in outputs],
        grid=(steps,),
        in_specs=[spec(array, count) for array, count in inputs],
        out_specs=[spec(array, count) for array, count in outputs],
        scratch_shapes=scratch,
        cost_estimate=pl.CostEstimate(flops=0, bytes_accessed=0, transcendentals=0),
        compiler_params=pltpu.CompilerParams(vmem_limit_bytes=60 * 2**20),
    )(*[array for array, _ in inputs])


def gathered_kernel(kernel, parts, steps, backwards, keep, given, core_ref, *refs):
    own, other = refs[:parts], refs[parts : 2 * parts]
    refs = refs[2 * parts :]
    inputs, refs = refs[:given], refs[given:]
    out_ref, refs = (refs[0], refs[1:]) if keep else (None, refs)
    buffer, sem, out_sem = refs[-3:]
    half = buffer.shape[0] // 2
    count = buffer.shape[0] // steps
    step = pl.program_id(0)
    block = steps - 1 - step if backwards else step

    @pl.when(step == 0)
    def _():
        for which, group in enumerate((own, other)):
            side = core_ref[0] if which == 0 else 1 - core_ref[0]
            start = 0
            for i, part in enumerate(group):
                to = pl.ds(pl.multiple_of(side * half + start, 16), part.shape[0])
                pltpu.make_async_copy(part, buffer.at[to], sem.at[side * parts + i]).start()
                start = start + part.shape[0]

    at = pl.ds(pl.multiple_of(block * count, 16), count)
    side = block // (steps // 2)
    place = lax.rem(block, steps // 2)
    whole = steps // 2 - 1

    @pl.when(place < whole)
    def _():
        pltpu.make_async_copy(buffer.at[at], buffer.at[at], sem.at[side * parts + place]).wait()

    @pl.when(place == whole)
    def _():
        for i in range(whole, parts):
            to = pl.ds(pl.multiple_of(block * count, 16), own[i].shape[0])
            pltpu.make_async_copy(buffer.at[to], buffer.at[to], sem.at[side * parts + i]).wait()

    if keep:
        pltpu.make_async_copy(buffer.at[at], out_ref.at[at], out_sem.at[block]).start()
    kernel(buffer.at[at], *inputs, *refs[:-3])
    if keep:

        @pl.when(step == steps - 1)
        def _():
            for i in range(steps):
                to = pl.ds(i * count, count)
                pltpu.make_async_copy(buffer.at[to], out_ref.at[to], out_sem.at[i]).wait()


def gathered_call(kernel, core, gathered, steps, inputs, outputs, scratch=(), backwards=False, keep=True, cost=0):
    own, other = gathered
    if other is None:
        count = own[0].shape[0] // steps
        results = kernel_call(kernel, steps, [(own[0], count)] + inputs, outputs, scratch, backwards)
        return ([own[0]] if keep else []) + list(results)

    def spec(array, count):
        return whole_block(array) if count is None else token_block(array, count, steps, backwards)

    anywhere = pl.BlockSpec(memory_space=pl.ANY)
    tokens = jax.ShapeDtypeStruct((2 * sum(p.shape[0] for p in own),) + own[0].shape[1:], own[0].dtype)
    return pl.pallas_call(
        functools.partial(gathered_kernel, kernel, len(own), steps, backwards, keep, len(inputs)),
        out_shape=([tokens] if keep else []) + [array for array, _ in outputs],
        grid=(steps,),
        in_specs=[pl.BlockSpec(memory_space=pltpu.SMEM)]
        + [anywhere] * (2 * len(own))
        + [spec(array, count) for array, count in inputs],
        out_specs=([anywhere] if keep else []) + [spec(array, count) for array, count in outputs],
        scratch_shapes=list(scratch)
        + [
            pltpu.VMEM(tokens.shape, tokens.dtype),
            pltpu.SemaphoreType.DMA((2 * len(own),)),
            pltpu.SemaphoreType.DMA((steps,)),
        ],
        cost_estimate=pl.CostEstimate(flops=0, bytes_accessed=cost << 20, transcendentals=0),
        compiler_params=pltpu.CompilerParams(vmem_limit_bytes=60 * 2**20),
    )(core.reshape(1).astype(jnp.int32), *own, *other, *[array for array, _ in inputs])


def per_device(
    tokens,
    segment_ids,
    cotangent,
    norm_one,
    branch_weight,
    input_proj,
    conv_weight,
    conv_bias,
    rate_weight,
    igate_weight,
    rate_bias,
    igate_bias,
    decay_param,
    out_proj,
    norm_two,
    mlp_gate,
    mlp_up,
    mlp_down,
):
    at = Place()
    k_count, z_count = at.k_count, at.z_count
    group = 2 * k_count
    row_dev, span, width_d = tokens.shape
    tok = row_dev * span
    rows = k_count * row_dev
    tok_all = 2 * rows * span
    d_own = norm_one.shape[0]
    w_own = conv_bias.shape[0]
    f_own = mlp_down.shape[0]
    width_r = branch_weight.shape[1]
    w_slot = width_r // group
    f_slot = f_own * z_count
    taps = conv_weight.shape[0]
    reach = taps - 1
    half_z = z_count // 2

    def by_feature(array):
        split = array.reshape(z_count, -1, 2 * d_own, array.shape[1])
        return jnp.swapaxes(split, 0, 1).reshape(array.shape)

    small = jnp.concatenate(
        [
            norm_one,
            norm_two,
            conv_weight.reshape(-1),
            conv_bias,
            rate_bias,
            igate_bias,
            decay_param,
        ]
    )
    rec_cols = jnp.concatenate(
        [
            branch_weight.reshape(d_own, k_count, 2, w_slot),
            input_proj.reshape(d_own, k_count, 2, w_slot),
        ],
        axis=3,
    )
    rec_pairs = at.exchange_core(jnp.moveaxis(rec_cols, 0, 2))

    seg_code = (segment_ids % 64).astype(low)
    pairs = [(i, i + 1) for i in range(at.s_count - 1)]
    before = lax.ppermute(seg_code[:, span - reach :], "seq", pairs)
    tokens = tokens.reshape(tok, width_d)
    tail = tokens.reshape(row_dev, span, width_d)[:, span - 8 :].reshape(row_dev * 8, width_d)
    tail = at.to_z(tail, 1)

    small = jnp.pad(small, (0, -small.shape[0] % 128)).reshape(-1, 128)
    small_rows = small.shape[0]
    small = jnp.pad(small, ((0, w_own - small_rows), (0, 0)))
    out_rows = jnp.concatenate([out_proj, rate_weight, igate_weight, small], axis=1)
    out_rows, before, tail = together(out_rows, before, tail)
    out_part = at.gather_z(out_rows)

    rec_cols = at.exchange_dp(rec_pairs)
    order = None
    if 2 * d_own % 128 == 0:
        order = [k * z_count + z for z in range(z_count) for k in range(k_count)]
    ext_code = jnp.concatenate([before, seg_code], axis=1)
    position = lax.broadcasted_iota(jnp.int32, (row_dev, span), 1)
    masks = [
        (ext_code[:, reach - by : reach - by + span] == seg_code) & ((at.s > 0) | (position >= by))
        for by in range(1, taps)
    ]
    masks = jnp.stack(masks + [masks[0]] * (9 - taps), axis=-1).astype(low).reshape(tok, 8)
    beside = jnp.concatenate([tokens, jnp.pad(masks, ((0, 0), (0, 120)))], axis=1)
    beside, rec_cols = together(beside, rec_cols)
    w1 = at.gather_z(rec_cols.reshape(group * d_own, 2 * w_slot))
    beside_near = at.gather_near(beside)
    tail = jnp.where(at.c == 1, tail, at.to_core(tail))
    inputs = tokens.astype(wide)
    s1 = lax.rsqrt(jnp.mean(inputs * inputs, axis=-1, keepdims=True) + eps_value)
    mlp_shape = jax.ShapeDtypeStruct((k_count, 2, d_own, 2 * f_slot), low)
    cut = functools.partial(cut_kernel, k_count, z_count)
    mlp_pairs = at.exchange_core(in_vmem(cut, (mlp_gate, mlp_up), mlp_shape))
    beside_near, tail, mlp_pairs, out_part = together(beside_near, tail, mlp_pairs, out_part)
    tail = at.gather_rows(tail)

    out_split = out_part.reshape(2, half_z, w_own, -1)

    def of_slot(columns):
        part = out_split[..., columns]
        keep = lax.dynamic_index_in_dim(part, at.c, 0, False)
        got = at.to_core(lax.dynamic_index_in_dim(part, 1 - at.c, 0, False))
        return jnp.swapaxes(at.by_core(keep, got), 0, 1).reshape(w_slot, -1)

    gate_rows = of_slot(slice(width_d, width_d + 2 * BS))
    small = out_part.reshape(z_count, w_own, -1)[:, :small_rows, width_d + 2 * BS :].reshape(z_count, -1)
    small = jnp.swapaxes(at.by_core(small, at.to_core(small)), 0, 1).reshape(at.s_count, -1)
    gains = at.gather_dp_small(small[:, : 2 * d_own]).reshape(k_count * at.s_count, -1)
    mine = lax.dynamic_slice_in_dim(small[:, 2 * d_own :], at.c * z_count, z_count, 0)
    mine = mine[:, : (taps + 4) * w_own].reshape(z_count, taps + 4, w_own).astype(wide)
    mine = jnp.swapaxes(mine, 0, 1).reshape(taps + 4, w_slot)
    w_conv = mine[:taps]
    b_conv, b_rate, b_igate, decay = (mine[taps + i][None, :] for i in range(4))
    log_slope = -rate_scale * jax.nn.softplus(-decay)
    decay_slope = rate_scale * jax.nn.sigmoid(-decay)
    params = jnp.concatenate([w_conv, b_conv, b_rate, b_igate, log_slope] + [decay_slope] * 8)
    beside_near, tail, gains, gate_rows = together(beside_near, tail, gains, gate_rows)
    heads = w_slot // BS

    def block_diagonal(columns):
        blocks = columns.reshape(heads, BS, 1, BS)
        same = jnp.eye(heads, dtype=low).reshape(heads, 1, heads, 1)
        return (blocks * same).reshape(w_slot, w_slot)

    w_gates = jnp.concatenate([block_diagonal(gate_rows[:, :BS]), block_diagonal(gate_rows[:, BS:])], axis=1)

    beside_far, mlp_pairs, w_gates, params = together(
        at.gather_far(beside_near), mlp_pairs, w_gates, params
    )
    gain_one = gains[:, :d_own].reshape(1, width_d).astype(wide)
    gain_two = gains[:, d_own:].reshape(1, width_d).astype(wide)
    mlp_cols = at.exchange_dp(mlp_pairs)
    cot = cotangent.reshape(tok, width_d)
    tokens_parts, mlp_cols, cot = together(at.gather_core(beside_far), mlp_cols, cot)
    shape = jax.ShapeDtypeStruct

    half_rows = group * d_own // 2
    w2_parts = [
        at.gather_z(part.reshape(half_rows, 2 * f_slot))
        for part in (mlp_cols[: k_count // 2], mlp_cols[k_count // 2 :])
    ]

    steps = tok_all // tok
    cot_near = at.gather_near(cot)
    flat32, flat16 = shape((tok_all, w_slot), wide), shape((tok_all, w_slot), low)
    ends = shape((rows * 8, w_slot), wide)

    def by_row(array):
        return jnp.repeat(array, 8, axis=0)

    n1_all, masks, branch_pre, conv_in, conv_low, keep_eff, part, run, summary, conv_before = gathered_call(
        functools.partial(conv_kernel, rows, span, order),
        at.c,
        tokens_parts,
        steps,
        [(w1 if order else by_feature(w1), None), (tail, None), (gain_one, None), (params, None), (w_gates, None)],
        [(shape((tok_all, width_d), low), tok), (shape((tok_all, 8), wide), tok), (flat32, tok), (flat16, tok), (flat16, tok)]
        + [(flat32, tok)] * 3
        + [(shape((2,) + ends.shape, wide), None), (ends, None)],
        [
            pltpu.VMEM(ends.shape, wide),
            pltpu.VMEM((span + 8, w_slot), wide),
            pltpu.VMEM((2,) + ends.shape, wide),
        ],
        keep=False,
    )
    summary = summary.reshape(2, rows, 8, w_slot)[:, :, 7]
    w_down = at.gather_z(mlp_down)
    summary, cot_near, out_split, w1 = together(summary, cot_near, out_split, w1)
    w1 = by_feature(w1)
    w_out = of_slot(slice(0, width_d))
    cot_far = at.gather_far(cot_near)
    before = [at.to_z(summary, by) for by in range(1, z_count)]
    state_in = jnp.zeros((rows, w_slot), wide)
    for one in reversed(before):
        state_in = one[1] + one[0] * state_in
    state_in = by_row(state_in)
    state, mixed = kernel_call(
        functools.partial(state_kernel, rows, span),
        steps,
        [(part, tok), (run, tok), (state_in, None), (branch_pre, tok)],
        [(flat32, tok), (flat16, tok)],
    )
    masks_after = at.to_z(masks.reshape(2, rows, span, 8)[0, :, :16], -1).reshape(rows * 16, 8)
    mixed, cot_far, w2_parts[0], masks_after, w1 = together(mixed, cot_far, w2_parts[0], masks_after, w1)

    chip_one = at.chip_product(mixed, w_out, dot_nn, exact=True)
    near_sum, cot_far = together(at.near_plane(chip_one, exact=True), cot_far)
    cot_all = at.gather_end(cot_far)
    resid = inputs + at.far_plane(near_sum)
    resid, w2_parts[1] = together(resid, w2_parts[1])
    w2 = jnp.concatenate([by_feature(part) for part in w2_parts])

    s2 = lax.rsqrt(jnp.mean(resid * resid, axis=-1, keepdims=True) + eps_value)
    normed_two = (resid * s2 * gain_two).astype(low)
    n2_near, w2, cot_all = together(at.gather_near(normed_two), w2, cot_all)
    n2_parts, w_down = together(at.gather_core(at.gather_far(n2_near)), w_down)
    n2_all, hidden, grad_two = gathered_call(
        mlp_kernel,
        at.c,
        n2_parts,
        steps,
        [(cot_all, tok), (w2, None), (w_down, None)],
        [(shape((tok_all, f_slot), low), tok), (shape((tok_all, 2 * f_slot), low), tok)],
    )
    def rows_apart(x, grad):
        sent, kept = rows_call(at.z, z_count, k_count, x, grad)
        return sent.reshape(-1, sent.shape[-1]), kept.reshape(-1, kept.shape[-1])

    _, got_two = at.chip_send(grad_two, w2, 1)
    near_two = at.near_parts(at.chip_own(grad_two, w2, got_two, 1))
    chip_two, grad_two = together(near_two[0], grad_two)
    w2_part = rows_apart(n2_all, grad_two)
    near_two, w2_part, hidden = together(near_two, w2_part, hidden)
    w2_sum = at.scatter_z(w2_part)
    grad_n2 = at.far_product(near_two)
    other_three, got_three = at.chip_send(hidden, w_down, 0)
    grad_n2, other_three, hidden = together(grad_n2, other_three, hidden)
    scaled_two = gain_two * grad_n2
    cot_f = cot.astype(wide)
    mean_two = jnp.mean(scaled_two * resid, axis=-1, keepdims=True)
    grad_resid = cot_f + s2 * scaled_two - resid * (s2 * s2 * s2) * mean_two
    grad_recur = grad_resid.astype(low)
    grad_recur, hidden = together(grad_recur, hidden)
    chip_three = at.chip_own(hidden, w_down, got_three, 0)
    down_sent, down_kept = down_call(at.z, z_count, hidden, cot_all)
    down_part = down_sent.reshape(-1, width_d), down_kept
    gr_near, chip_three, down_part = together(at.gather_near(grad_recur), chip_three, down_part)
    down_sum = at.scatter_z(down_part)
    gr_parts, chip_three = together(at.gather_core(at.gather_far(gr_near)), chip_three)

    def summed(pair):
        return pair[0].astype(wide) + pair[1].astype(wide)

    def to_owner(array, columns):
        return at.exchange_plane(array.reshape(k_count, 2, d_own, columns))


    gr_all, grad_branch, back_part, back_run, back = gathered_call(
        functools.partial(back_kernel, rows, span),
        at.c,
        gr_parts,
        steps,
        [(w_out, None), (branch_pre, tok), (state, tok), (keep_eff, tok)],
        [(flat16, tok), (flat32, tok), (flat32, tok), (ends, None)],
        [pltpu.VMEM((2,) + ends.shape, wide)],
        backwards=True,
        cost=70,
    )
    back = back.reshape(rows, 8, w_slot)[:, 0]
    back, mixed, near_three = together(back, mixed, at.near_parts(chip_three))

    def by_owner(array):
        split = array.reshape(half_z, 2, w_own, -1)
        keep = lax.dynamic_index_in_dim(split, at.c, 1, False)
        got = at.to_core(lax.dynamic_index_in_dim(split, 1 - at.c, 1, False))
        return at.by_core(keep, got).reshape(z_count, w_own, -1)

    own = jnp.stack([summary[0], back])
    after = [at.to_z(own, -by) for by in range(1, z_count)]
    grad_out = dot_tn(mixed, gr_all)
    after, grad_out, w2_sum = together(after, grad_out, w2_sum)
    carry_in = jnp.zeros((rows, w_slot), wide)
    for part in reversed(after):
        carry_in = part[1] + part[0] * carry_in
    mlp_pairs = at.exchange_core(summed(w2_sum).reshape(k_count, 2, d_own, 2 * f_slot))
    carry_in, mlp_pairs = together(carry_in, mlp_pairs)
    mlp_back = at.exchange_dp(mlp_pairs)
    grad_conv, rec_small, vectors = kernel_call(
        functools.partial(adjoint_kernel, rows, span),
        steps,
        [
            (back_part, tok),
            (back_run, tok),
            (by_row(carry_in), None),
            (state, tok),
            (state_in, None),
            (conv_low, tok),
            (w_gates, None),
            (params, None),
            (masks, tok),
            (conv_in, tok),
            (conv_before, None),
        ],
        [(flat16, tok), (shape((w_slot, 2 * BS), low), None), (shape((8, w_slot), wide), None)],
        [
            pltpu.VMEM((w_slot, 2 * w_slot), wide),
            pltpu.VMEM((8, w_slot), wide),
            pltpu.VMEM((span + 8, w_slot), wide),
            pltpu.VMEM(ends.shape, wide),
            pltpu.VMEM(ends.shape, wide),
        ],
    )
    grad_conv, near_three, mlp_back, rec_small, vectors = together(
        grad_conv, near_three, mlp_back, rec_small, vectors
    )
    block_out = (resid + at.far_product(near_three)).astype(low)
    head = at.to_z(grad_conv.reshape(2, rows, span, w_slot)[0, :, :16], -1).reshape(rows * 16, w_slot)
    rec_part = at.own_apart(by_owner(jnp.concatenate([grad_out.astype(low), rec_small], axis=1)), 0)
    head, rec_part = together(head, rec_part)
    rec_sum = at.scatter_z(rec_part)
    (grad_one,) = kernel_call(
        functools.partial(conv_back_kernel, rows, span),
        1,
        [(array, None) for array in (grad_conv, head, masks, masks_after, grad_branch, params)],
        [(shape((tok_all, 2 * w_slot), low), None)],
        [pltpu.VMEM((span + 8, w_slot), wide)],
    )

    other_one, got_one = at.chip_send(grad_one, w1, 1)
    other_one, then, block_out = together(other_one, grad_one, block_out)
    w1_part = rows_apart(n1_all, then)
    then, w1_part = together(then, w1_part)
    near_one = at.near_parts(at.chip_own(then, w1, got_one, 1))
    w1_sum = at.scatter_z(w1_part)
    mlp_whole = jax.ShapeDtypeStruct(mlp_gate.shape, wide)
    join = functools.partial(join_kernel, k_count, z_count)
    grad_gate_w, grad_up_w = in_vmem(join, (mlp_back,), (mlp_whole, mlp_whole))
    vectors = at.sum_z(vectors)
    vectors = at.by_core(vectors, at.to_core(vectors))
    near_one, grad_gate_w, grad_up_w, down_sum, vectors = together(
        near_one, grad_gate_w, grad_up_w, down_sum, vectors
    )
    vectors = lax.dynamic_index_in_dim(vectors, at.s // z_count, 0, False)
    grad_small = lax.dynamic_slice_in_dim(vectors, at.s % z_count * w_own, w_own, 1)
    grad_n1 = at.far_product(near_one)
    w1_sum, grad_n1, rec_sum = together(w1_sum, grad_n1, rec_sum)
    rec_pairs = at.exchange_core(summed(w1_sum).reshape(k_count, 2, d_own, 2 * w_slot))
    rec_pairs, grad_n1, rec_sum = together(rec_pairs, grad_n1, rec_sum)
    rec_back = at.exchange_dp(rec_pairs)
    scaled_one = gain_one * grad_n1
    mean_one = jnp.mean(scaled_one * inputs, axis=-1, keepdims=True)
    grad_tokens = grad_resid + s1 * scaled_one - inputs * (s1 * s1 * s1) * mean_one
    grad_tokens = grad_tokens.reshape(row_dev, span, width_d)
    block_out = block_out.reshape(row_dev, span, width_d)

    rec_rows = summed(rec_sum)
    grad_out_w = rec_rows[:, :width_d]
    grad_rate_w = rec_rows[:, width_d : width_d + BS]
    grad_igate_w = rec_rows[:, width_d + BS : width_d + 2 * BS]
    grad_down = summed(down_sum)
    rec_back = jnp.moveaxis(rec_back, 2, 0)
    grad_branch_w = rec_back[..., :w_slot].reshape(d_own, width_r)
    grad_input_w = rec_back[..., w_slot:].reshape(d_own, width_r)

    def gain_grad(pairs, gain):
        total = sum(jnp.sum(weight.astype(wide) * grad, axis=1) for weight, grad in pairs)
        return total / gain.astype(wide)

    grad_norm_one = gain_grad(((branch_weight, grad_branch_w), (input_proj, grad_input_w)), norm_one)
    grad_norm_two = gain_grad(((mlp_gate, grad_gate_w), (mlp_up, grad_up_w)), norm_two)
    return (
        block_out,
        grad_tokens,
        grad_norm_one,
        grad_branch_w,
        grad_input_w,
        grad_small[:taps],
        grad_small[taps],
        grad_rate_w,
        grad_igate_w,
        grad_small[taps + 1],
        grad_small[taps + 2],
        grad_small[taps + 3],
        grad_out_w,
        grad_norm_two,
        grad_gate_w,
        grad_up_w,
        grad_down,
    )


def solution(mesh):
    rows, matrix = P(AXES), P(AXES, None)
    tokens = P("dp", "seq", None)
    return jax.shard_map(
        per_device,
        mesh=mesh,
        in_specs=(
            tokens,
            P("dp", "seq"),
            tokens,
            rows,
            matrix,
            matrix,
            P(None, AXES),
            rows,
            matrix,
            matrix,
            rows,
            rows,
            rows,
            matrix,
            rows,
            matrix,
            matrix,
            matrix,
        ),
        out_specs=(
            tokens,
            tokens,
            rows,
            matrix,
            matrix,
            P(None, AXES),
            rows,
            matrix,
            matrix,
            rows,
            rows,
            rows,
            matrix,
            rows,
            matrix,
            matrix,
            matrix,
        ),
        check_vma=False,
    )
```
